32 devices in a mesh: section: 4 (over z), dp: 8 (over y, x, core).
Axes of the slice: x: 2, y: 2, z: 4, core: 2. Of those that a mesh axis runs over, the one named last changes fastest.
Arguments:
- x0: bfloat16 [4, 256, 5120], P(None, 'dp'), may hold values from -6 to 6
- w_key: bfloat16 [4, 5120, 512], P('section'), may hold values from -0.078125 to 0.078125
- w_value: bfloat16 [4, 5120, 512], P('section'), may hold values from -0.078125 to 0.078125
- w_score: float32 [5120], replicated, may hold values from -0.078125 to 0.078125
- segments: int32 [4, 256], P(None, 'dp'), may hold values from 0 to 31, as said below
- lengths: int32 [4, 8], P(None, 'dp'), may hold values from 1 to 32, as said below
- grades: int32 [4, 256], P(None, 'dp'), may hold values from 0 to 3
Outputs:
- grad_key: float32 [4, 5120, 512], P('section', 'dp')
- grad_value: float32 [4, 5120, 512], P('section', 'dp')
The draws below stay inside these ranges and needn't reach their ends.
Inputs may be any that keep to these rules, and one draw needn't show every extreme that they name: `segments`: within each packed row of 32 slots the ids start at 0 and never fall; in every draw some packed row has a new id at every slot. `lengths`: every packed row has its live tokens at the front; in every draw some packed row is full.
All inputs are finite; a program needn't handle non-finite values.
Results may differ from the reference program's by a relative error of at most 0.035.
Values may be sent and summed in bfloat16 or wider, within the bound.
No kernel may reach another device: no remote copies, remote signals or barrier semaphores. Data moves between devices by JAX's collectives and lax.ppermute only.
A program may use at most 128 MiB of HBM per device.

```python
import jax
import jax.numpy as jnp
from jax import lax

D = 5120
HD = 128
KV_HEADS = 4
ROWS = 32
MICRO = 4
KW = 512
LAYERS = 4
TOKENS = 256
N_DP = 8


def draw_segments(key, part):
    key = jax.random.fold_in(key, 11)
    first_key, second_key = jax.random.split(key)
    count = MICRO * (TOKENS // ROWS)
    starts = jax.random.randint(first_key, (count, ROWS), 0, 12) == 0
    index = jnp.arange(ROWS, dtype=jnp.int32)
    chosen = jax.random.randint(second_key, (), 0, count)
    starts = starts | (index == 0)[None, :] | (jnp.arange(count, dtype=jnp.int32) == chosen)[:, None]
    ident = jnp.cumsum(starts.astype(jnp.int32), axis=-1) - 1
    return ident.reshape(MICRO, TOKENS).astype(jnp.int32)


def draw_lengths(key, part):
    key = jax.random.fold_in(key, 23)
    first_key, second_key = jax.random.split(key)
    count = MICRO * (TOKENS // ROWS)
    divisor = jax.random.randint(first_key, (count,), 1, 8)
    live = ROWS // divisor
    chosen = jax.random.randint(second_key, (), 0, count)
    live = jnp.where(jnp.arange(count, dtype=jnp.int32) == chosen, ROWS, live)
    return live.reshape(MICRO, TOKENS // ROWS).astype(jnp.int32)


def with_ends(values, stream_key, smallest, high):
    longest = values.shape.index(max(values.shape))
    spots = []
    for shift in (0, 1):
        where = [jax.random.randint(jax.random.fold_in(stream_key, axis), (), 0, length) for axis, length in enumerate(values.shape)]
        where[longest] = (where[longest] + shift) % values.shape[longest]
        spots.append(tuple(where))
    return values.at[spots[0]].set(smallest).at[spots[1]].set(high)


def level_of(rng, dims, cuts, least, largest):
    def one(position, parts):
        heights = jax.random.uniform(jax.random.fold_in(jax.random.fold_in(rng, 6), position), (parts,), jnp.float32, least / len(cuts), largest / len(cuts))
        return jnp.repeat(jnp.exp(heights), dims[position] // parts).reshape((-1,) + (1,) * (len(dims) - position - 1))

    factor_of = one(*cuts[0])
    for cut in cuts[1:]:
        factor_of = factor_of * one(*cut)
    return factor_of


def centred(own_key, extent, scale, reach, shards=(), kind=jnp.bfloat16):
    result = jax.random.normal(own_key, extent, jnp.float32) * scale
    if len(shards) > 0:
        result = level_of(own_key, extent, shards, -0.22, 0.18) * result
    return jnp.clip(result, min=-reach, max=reach).astype(kind)


def setup_inputs(seed: int = 0) -> dict:
    keys = jax.random.split(jax.random.key(seed), 8)
    return {
        "x0": centred(keys[0], (MICRO, TOKENS, D), 1.0, 6.0, ((1, 8),)),
        "w_key": centred(keys[1], (LAYERS, D, KW), D ** -0.5, 0.078125, ((0, 4),)),
        "w_value": centred(keys[2], (LAYERS, D, KW), D ** -0.5, 0.078125, ((0, 4),)),
        "w_score": centred(keys[3], (D,), D ** -0.5, 0.078125, (), jnp.float32),
        "segments": draw_segments(jax.random.fold_in(keys[7], 71), 0),
        "lengths": draw_lengths(jax.random.fold_in(keys[7], 71), 0),
        "grades": with_ends(jax.random.randint(keys[6], (MICRO, TOKENS), 0, 4), jax.random.fold_in(keys[6], 1), 0, 3).astype(jnp.int32),
    }


EPS = 1e-06
THETA = 1000000.0

def matmul(left, right):
    flat = left.reshape(-1, left.shape[-1])
    return jnp.dot(flat, right, preferred_element_type=jnp.float32).reshape(left.shape[:-1] + (right.shape[-1],))

def rope_tables(segments):
    width = segments.shape[-1]
    index = jnp.arange(width, dtype=jnp.int32)
    section_begin_offsets = jnp.concatenate([jnp.ones(segments.shape[:-1] + (1,), bool), segments[..., 1:] != segments[..., :-1]], axis=-1)
    leading_half = lax.cummax(jnp.where(section_begin_offsets, index, jnp.int32(0)), axis=segments.ndim - 1)
    offset = (index - leading_half).astype(jnp.float32)
    freqs = THETA ** (-(jnp.arange(HD // 2, dtype=jnp.float32) * 2.0) / HD)
    angles = offset[..., None] * freqs
    return (jnp.cos(angles), jnp.sin(angles))

def allowed_mask(segments, lengths):
    width = segments.shape[-1]
    index = jnp.arange(width, dtype=jnp.int32)
    same = segments[..., :, None] == segments[..., None, :]
    causal = index[None, :] <= index[:, None]
    live = index < lengths
    allowed = same & causal & live[..., :, None] & live[..., None, :]
    return allowed | jnp.eye(width, dtype=bool)

def rotate(vectors, cosine, sine_table):
    half = HD // 2
    cosine_value = cosine[..., :, None, :]
    sine_value = sine_table[..., :, None, :]
    leading_half, trailing_half = (vectors[..., :half], vectors[..., half:])
    return jnp.concatenate([leading_half * cosine_value - trailing_half * sine_value, trailing_half * cosine_value + leading_half * sine_value], axis=-1)

def rotate_back(grads, cosine, sine_table):
    half = HD // 2
    cosine_value = cosine[..., :, None, :]
    sine_value = sine_table[..., :, None, :]
    leading_half, trailing_half = (grads[..., :half], grads[..., half:])
    return jnp.concatenate([leading_half * cosine_value + trailing_half * sine_value, trailing_half * cosine_value - leading_half * sine_value], axis=-1)

def normalize(hidden):
    hfull = hidden.astype(jnp.float32)
    scale = lax.rsqrt(lax.optimization_barrier(jnp.mean(hfull * hfull, axis=-1, keepdims=True)) + EPS)
    return (hfull, scale)

def heads(array):
    return array.reshape(array.shape[:-1] + (KV_HEADS, HD))

def attend(keys_b, values_b, allowed):
    kf = keys_b.astype(jnp.float32)
    scores = jnp.einsum('...ihd,...jhd->...hij', kf, kf) / HD
    scores = jnp.where(allowed[..., None, :, :], scores, -1e+30)
    probs = jax.nn.softmax(scores, axis=-1)
    probs_b = probs.astype(jnp.bfloat16)
    mixed = jnp.einsum('...hij,...jhd->...ihd', probs_b.astype(jnp.float32), values_b.astype(jnp.float32))
    return (probs, probs_b, mixed)

def layer_forward(hidden, w_key, w_value, cosine, sine_table, allowed):
    hfull, scale = normalize(hidden)
    normed = (hfull * scale).astype(jnp.bfloat16)
    keys_b = rotate(heads(matmul(normed, w_key)), cosine, sine_table).astype(jnp.bfloat16)
    values_b = heads(matmul(normed, w_value).astype(jnp.bfloat16))
    probs, probs_b, mixed = attend(keys_b, values_b, allowed)
    mixed_b = mixed.astype(jnp.bfloat16).reshape(hidden.shape[:-1] + (KW,))
    output = hfull + matmul(mixed_b, w_value.T)
    return (output.astype(jnp.bfloat16), keys_b, values_b)

def layer_backward(hidden, keys_b, values_b, grad_out, w_key, w_value, cosine, sine_table, allowed):
    hfull, scale = normalize(hidden)
    probs, probs_b, mixed = attend(keys_b, values_b, allowed)
    mixed_b = mixed.astype(jnp.bfloat16).reshape(hidden.shape[:-1] + (KW,))
    grad_mixed = heads(matmul(grad_out, w_value).astype(jnp.bfloat16)).astype(jnp.float32)
    grad_probs = jnp.einsum('...ihd,...jhd->...hij', grad_mixed, values_b.astype(jnp.float32))
    grad_values = jnp.einsum('...hij,...ihd->...jhd', probs_b.astype(jnp.float32), grad_mixed)
    grad_values = grad_values.astype(jnp.bfloat16).reshape(hidden.shape[:-1] + (KW,))
    grad_scores = (probs * (grad_probs - lax.optimization_barrier(jnp.sum(probs * grad_probs, axis=-1, keepdims=True)))).astype(jnp.bfloat16)
    gsf = grad_scores.astype(jnp.float32)
    kf = keys_b.astype(jnp.float32)
    grad_keys = (jnp.einsum('...hij,...jhd->...ihd', gsf, kf) + jnp.einsum('...hij,...ihd->...jhd', gsf, kf)) / HD
    grad_keys = rotate_back(grad_keys, cosine, sine_table).astype(jnp.bfloat16).reshape(hidden.shape[:-1] + (KW,))
    grad_normed = matmul(grad_keys, w_key.T) + matmul(grad_values, w_value.T)
    incoming_gradient = grad_out.astype(jnp.float32) + scale * grad_normed - hfull * scale ** 3 * lax.optimization_barrier(jnp.mean(grad_normed * hfull, axis=-1, keepdims=True))
    normed = (hfull * scale).astype(jnp.bfloat16)
    return (incoming_gradient.astype(jnp.bfloat16), normed, grad_keys, grad_values, mixed_b)

def loss_gradient(hidden, segments, length, grades, w_score):
    hfull, scale = normalize(hidden)
    xfull = hfull * scale
    score = jnp.dot(xfull, w_score, precision=lax.Precision.HIGHEST)
    width = segments.shape[-1]
    index = jnp.arange(width, dtype=jnp.int32)
    following = jnp.concatenate([segments[..., 1:] != segments[..., :-1], jnp.ones(segments.shape[:-1] + (1,), bool)], axis=-1)
    ends = (index < length) & (following | (index == length - 1))
    target = jax.nn.softmax(jnp.where(ends, grades.astype(jnp.float32), -1e+30), axis=-1)
    model = jax.nn.softmax(jnp.where(ends, score, -1e+30), axis=-1)
    weight = jnp.where(ends, model - target, 0.0)
    grad_x = weight[..., None] * w_score
    grad_h = scale * grad_x - hfull * scale ** 3 * lax.optimization_barrier(jnp.mean(grad_x * hfull, axis=-1, keepdims=True))
    return grad_h.astype(jnp.bfloat16)

def reference(x0, w_key, w_value, w_score, segments, lengths, grades):
    row_segments = segments.reshape(MICRO, N_DP, ROWS)
    row_lengths = lengths[..., None]
    row_grades = grades.reshape(MICRO, N_DP, ROWS)
    cosine, sine_table = rope_tables(row_segments)
    allowed = allowed_mask(row_segments, row_lengths)
    hidden = x0.reshape(MICRO, N_DP, ROWS, D)
    saved = []
    for layer in range(LAYERS):
        produced, keys_b, values_b = layer_forward(hidden, w_key[layer], w_value[layer], cosine, sine_table, allowed)
        saved.append((hidden, keys_b, values_b))
        hidden = produced
    grad = loss_gradient(hidden, row_segments, row_lengths, row_grades, w_score)
    key_list = []
    value_list = []
    for layer in range(LAYERS - 1, -1, -1):
        h_in, keys_b, values_b = saved[layer]
        incoming_gradient, normed, grad_keys, grad_values, mixed_b = layer_backward(h_in, keys_b, values_b, grad, w_key[layer], w_value[layer], cosine, sine_table, allowed)
        normed2 = normed.reshape(-1, D)
        grad2 = grad.reshape(-1, D)
        key_list.append(jnp.dot(normed2.T, grad_keys.reshape(-1, KW), preferred_element_type=jnp.float32))
        value_list.append(jnp.dot(normed2.T, grad_values.reshape(-1, KW), preferred_element_type=jnp.float32) + jnp.dot(grad2.T, mixed_b.reshape(-1, KW), preferred_element_type=jnp.float32))
        grad = incoming_gradient
    grad_key = jnp.stack(key_list[::-1], axis=0)
    grad_value = jnp.stack(value_list[::-1], axis=0)
    return (grad_key, grad_value)
```

```python
import functools

import jax
import jax.numpy as jnp
from jax import lax
from jax.experimental import pallas as pl
from jax.experimental.pallas import tpu as pltpu
from jax.sharding import PartitionSpec as P

HD = 128
KV_HEADS = 4
EPS = 1e-06
THETA = 1000000.0
NEG = -1e30
CHUNK = 1280
BF16 = jnp.bfloat16
F32 = jnp.float32

VMEM = pl.BlockSpec(memory_space=pltpu.VMEM)
HBM = pl.BlockSpec(memory_space=pl.ANY)


def params():
    return pltpu.CompilerParams(vmem_limit_bytes=12 * 1024 * 1024)


def shifted(value, axis, steps):
    count = lax.axis_size(axis)
    first, last = (max(0, -steps), min(count, count - steps))
    return lax.ppermute(value, axis, [(source, source + steps) for source in range(first, last)])


def dot(left, right):
    return jnp.dot(left, right, preferred_element_type=F32)


def dot_tb(left, right):
    return lax.dot_general(left, right, (((1,), (1,)), ((), ())), preferred_element_type=F32)


def dot_ta(left, right):
    return lax.dot_general(left, right, (((0,), (0,)), ((), ())), preferred_element_type=F32)


def to_column(row, eye):
    return jnp.sum(jnp.where(eye, jnp.broadcast_to(row, eye.shape), 0.0), axis=1, keepdims=True)


def make_tables(
    micro, segments_ref, lengths_ref, grades_ref,
    cos_ref, sin_ref, mask_ref, ends_ref, target_ref,
):
    width = segments_ref.shape[1]
    square = (width, width)
    at_row = lax.broadcasted_iota(jnp.int32, square, 0)
    at_col = lax.broadcasted_iota(jnp.int32, square, 1)
    eye = at_row == at_col
    lane = lax.broadcasted_iota(jnp.int32, (width, HD), 1)
    half_lane = jnp.where(lane < HD // 2, lane, lane - HD // 2).astype(F32)
    freqs = jnp.exp(half_lane * F32(-2.0 / HD) * jnp.log(F32(THETA)))
    sign = jnp.where(lane < HD // 2, -1.0, 1.0)
    index = lax.broadcasted_iota(jnp.int32, (width, 1), 0)
    for slot in range(micro):
        seg_row = segments_ref[slot : slot + 1, :].astype(F32)
        seg_col = to_column(seg_row, eye)
        grade_col = to_column(grades_ref[slot : slot + 1, :].astype(F32), eye)
        length = lengths_ref[0, slot]
        same = seg_col == seg_row
        offset = jnp.sum(jnp.where(same & (at_col < at_row), 1.0, 0.0), axis=1, keepdims=True)
        angles = offset * freqs
        cos_ref[slot] = jnp.cos(angles)
        sin_ref[slot] = jnp.sin(angles) * sign
        allowed = same & (at_col <= at_row) & (at_row < length) & (at_col < length)
        mask = jnp.where(allowed | eye, 1.0, 0.0)
        for head in range(KV_HEADS):
            mask_ref[slot, head * width : (head + 1) * width, :] = mask
        changes = jnp.sum(
            jnp.where((at_col == at_row + 1) & jnp.logical_not(same), 1.0, 0.0),
            axis=1, keepdims=True,
        )
        following = (changes > 0.0) | (index == width - 1)
        ends = (index < length) & (following | (index == length - 1))
        logits = jnp.where(ends, grade_col, NEG)
        weight = jnp.exp(logits - jnp.max(logits, axis=0, keepdims=True))
        target = weight / jnp.sum(weight, axis=0, keepdims=True)
        ends_ref[slot] = jnp.broadcast_to(jnp.where(ends, 1.0, 0.0), (width, HD))
        target_ref[slot] = jnp.broadcast_to(target, (width, HD))


def first_kernel(
    sections, micro, peers,
    wk_hbm, wv_hbm, x0_hbm, score_hbm, segments_hbm, lengths_hbm, grades_hbm,
    w_score, wk, wv, cosine, sine, mask, ends, target,
    saved, keys, values, probs, scales, grads, sent, *rest,
):
    outgoing = rest[-13]
    segments_ref, lengths_ref, grades_ref, small, key_sems, value_sems = rest[-12:-6]
    scratch = rest[-6:]
    model = wk.shape[0]
    copies = [
        pltpu.make_async_copy(segments_hbm, segments_ref, small.at[0]),
        pltpu.make_async_copy(lengths_hbm, lengths_ref, small.at[1]),
        pltpu.make_async_copy(grades_hbm, grades_ref, small.at[2]),
        pltpu.make_async_copy(x0_hbm, saved, small.at[3]),
        pltpu.make_async_copy(score_hbm, w_score, small.at[4]),
    ]
    for copy in copies:
        copy.start()

    def chunk_copies(c):
        cols = pl.ds(c * CHUNK, CHUNK)
        return (
            pltpu.make_async_copy(wk_hbm.at[cols], wk.at[cols], key_sems.at[c]),
            pltpu.make_async_copy(wv_hbm.at[cols], wv.at[cols], value_sems.at[c]),
        )

    for c in range(model // CHUNK):
        for copy in chunk_copies(c):
            copy.start()
    for copy in copies[:3]:
        copy.wait()
    make_tables(
        micro, segments_ref, lengths_ref, grades_ref, cosine, sine, mask, ends, target
    )
    for copy in copies[3:]:
        copy.wait()
    section = lax.axis_index("section")

    @pl.when(section == 0)
    def _():
        def wait_chunk(c):
            for copy in chunk_copies(c):
                copy.wait()

        forward_body(
            0, section, sections, peers, wait_chunk,
            w_score, wk, wv, cosine, sine, mask, ends, target,
            saved, keys, values, probs, scales, grads, sent, outgoing, *scratch,
        )

    @pl.when(section != 0)
    def _():
        for c in range(model // CHUNK):
            for copy in chunk_copies(c):
                copy.wait()


def row_scale(ref_value_chunks, model):
    total = None
    for chunk in ref_value_chunks:
        part = chunk * chunk
        total = part if total is None else total + part
    return lax.rsqrt(jnp.sum(total, axis=1, keepdims=True) / model + EPS)


def head_cols(head):
    return slice(head * HD, (head + 1) * HD)


def forward_kernel(
    tick, sections, micro, peers,
    incoming, w_score, wk, wv, cosine, sine, mask, ends, target,
    *rest,
):
    section = lax.axis_index("section")
    offset = tick - 2 * section
    slot = jnp.clip(offset, 0, micro - 1)
    saved = rest[7]

    @pl.when((offset >= 0) & (offset < micro))
    def _():
        @pl.when(section != 0)
        def _():
            saved[slot] = incoming[...]

        forward_body(
            slot, section, sections, peers, None,
            w_score, wk, wv, cosine, sine, mask, ends, target, *rest[7:],
        )


def forward_body(
    slot, section, sections, peers, wait_chunk,
    w_score, wk, wv, cosine, sine, mask, ends, target,
    saved, keys, values, probs, scales, grads, sent, outgoing,
    acc_k, acc_v, normed, mixed, block, sem,
):
    width, model = outgoing.shape
    features = KV_HEADS * HD
    step = CHUNK // 2
    share = model // peers
    wide = block.shape[2] - features

    def chunk_of(ref, start):
        return ref[slot, :, start : start + step].astype(F32)

    scale = row_scale([chunk_of(saved, c) for c in range(0, model, step)], model)
    scales[slot] = jnp.broadcast_to(scale, (width, HD))
    for c in range(0, model, step):
        normed[:, c : c + step] = (chunk_of(saved, c) * scale).astype(BF16)
    acc_k[...] = jnp.zeros_like(acc_k)
    acc_v[...] = jnp.zeros_like(acc_v)

    @pl.loop(0, model // CHUNK)
    def _(c):
        if wait_chunk is not None:
            wait_chunk(c)
        cols = pl.ds(pl.multiple_of(c * CHUNK, CHUNK), CHUNK)
        piece = normed[:, cols]
        acc_k[...] += dot(piece, wk[cols, :])
        acc_v[...] += dot(piece, wv[cols, :])

    cos_value = cosine[slot]
    sin_value = sine[slot]
    scores = []
    for head in range(KV_HEADS):
        vec = acc_k[:, head_cols(head)]
        turned = vec * cos_value + pltpu.roll(vec, HD // 2, 1) * sin_value
        key = turned.astype(BF16)
        keys[slot, :, head_cols(head)] = key
        scores.append(dot_tb(key, key))
    values[slot] = acc_v[...].astype(BF16)
    score = jnp.concatenate(scores, axis=0) / HD
    score = jnp.where(mask[slot] > 0.0, score, NEG)
    weight = jnp.exp(score - jnp.max(score, axis=1, keepdims=True))
    prob = weight / jnp.sum(weight, axis=1, keepdims=True)
    probs[slot] = prob
    prob_b = prob.astype(BF16)
    for head in range(KV_HEADS):
        out = dot(prob_b[head * width : (head + 1) * width, :], values[slot, :, head_cols(head)])
        mixed[:, head_cols(head)] = out.astype(BF16)

    for peer in range(peers):
        block[peer, :, :share] = normed[:, peer * share : (peer + 1) * share]
        block[peer, :, wide:] = mixed[...]
    copy = pltpu.make_async_copy(block, sent.at[:, slot], sem)
    copy.start()

    @pl.loop(0, model // CHUNK)
    def _(c):
        cols = pl.ds(pl.multiple_of(c * CHUNK, CHUNK), CHUNK)
        out = saved[slot, :, cols].astype(F32) + dot_tb(mixed[...], wv[cols, :])
        outgoing[:, cols] = out.astype(BF16)

    @pl.when(section == sections - 1)
    def _():
        def last_of(start):
            return outgoing[:, start : start + step].astype(F32)

        last_scale = row_scale([last_of(c) for c in range(0, model, step)], model)
        along = None
        for c in range(0, model, step):
            part = last_of(c) * w_score[:, c : c + step]
            along = part if along is None else along + part
        along = jnp.sum(along, axis=1, keepdims=True)
        is_end = ends[slot][:, :1] > 0.0
        logits = jnp.where(is_end, last_scale * along, NEG)
        part = jnp.exp(logits - jnp.max(logits, axis=0, keepdims=True))
        chosen = part / jnp.sum(part, axis=0, keepdims=True)
        g = jnp.where(is_end, chosen - target[slot][:, :1], 0.0)
        first = last_scale * g
        second = last_scale * last_scale * last_scale * (g * along / model)
        for c in range(0, model, step):
            value = first * w_score[:, c : c + step] - last_of(c) * second
            grads[slot, :, c : c + step] = value.astype(BF16)

    copy.wait()


def backward_kernel(
    tick, sections, micro, peers, slots,
    incoming, wk, wv, cosine, sine, saved, keys, values, probs, scales, grads,
    *rest,
):
    sent = rest[len(slots) + 2 : 2 * len(slots) + 2]
    outgoing = rest[2 * len(slots) + 2]
    acc, full, current, flat, block, sem = rest[2 * len(slots) + 3 :]
    section = lax.axis_index("section")
    offset = tick - 2 * (sections - 1 - section)
    slot = jnp.clip(offset, 0, micro - 1)
    width, model = incoming.shape
    features = KV_HEADS * HD
    step = CHUNK // 2
    share = model // peers
    wide = block.shape[2] - 2 * features

    @pl.when((offset >= 0) & (offset < micro))
    def _():
        @pl.when(section == sections - 1)
        def _():
            current[...] = grads[slot]

        @pl.when(section != sections - 1)
        def _():
            current[...] = incoming[...]

        acc[...] = jnp.zeros_like(acc)

        @pl.loop(0, model // CHUNK)
        def _(c):
            cols = pl.ds(pl.multiple_of(c * CHUNK, CHUNK), CHUNK)
            acc[...] += dot(current[:, cols], wv[cols, :])

        cos_value = cosine[slot]
        sin_value = sine[slot]
        prob = probs[slot]
        prob_b = prob.astype(BF16)
        grad_probs = []
        for head in range(KV_HEADS):
            rows = slice(head * width, (head + 1) * width)
            mixed_grad = acc[:, head_cols(head)].astype(BF16)
            grad_probs.append(dot_tb(mixed_grad, values[slot, :, head_cols(head)]))
            flat[:, features + head * HD : features + (head + 1) * HD] = dot_ta(
                prob_b[rows, :], mixed_grad
            ).astype(BF16)
        grad_prob = jnp.concatenate(grad_probs, axis=0)
        grad_score = prob * (grad_prob - jnp.sum(prob * grad_prob, axis=1, keepdims=True))
        grad_score = grad_score.astype(BF16)
        for head in range(KV_HEADS):
            piece = grad_score[head * width : (head + 1) * width, :]
            key = keys[slot, :, head_cols(head)]
            vec = (dot(piece, key) + dot_ta(piece, key)) / HD
            turned = vec * cos_value - pltpu.roll(vec, HD // 2, 1) * sin_value
            flat[:, head_cols(head)] = turned.astype(BF16)

        for peer in range(peers):
            block[peer, :, :share] = current[:, peer * share : (peer + 1) * share]
            block[peer, :, wide:] = flat[...]
        for which, out in zip(slots, sent):
            @pl.when(slot == which)
            def _():
                pltpu.make_async_copy(block, out, sem).start()

        @pl.when(section != 0)
        def _():
            acc[...] = jnp.zeros_like(acc)

            @pl.loop(0, model // CHUNK)
            def _(c):
                cols = pl.ds(pl.multiple_of(c * CHUNK, CHUNK), CHUNK)
                out = dot_tb(flat[:, :features], wk[cols, :])
                out = out + dot_tb(flat[:, features:], wv[cols, :])
                full[:, cols] = out
                along = out * saved[slot, :, cols].astype(F32)
                total = along[:, :HD]
                for start in range(HD, CHUNK, HD):
                    total = total + along[:, start : start + HD]
                acc[:, :HD] += total

            scale = scales[slot][:, :1]
            mean = jnp.sum(acc[:, :HD], axis=1, keepdims=True) / model
            second = scale * scale * scale * mean
            for c in range(0, model, step):
                cols = slice(c, c + step)
                value = (
                    current[:, cols].astype(F32)
                    + scale * full[:, cols]
                    - saved[slot, :, cols].astype(F32) * second
                )
                outgoing[:, cols] = value.astype(BF16)

        for which, out in zip(slots, sent):
            @pl.when(slot == which)
            def _():
                pltpu.make_async_copy(block, out, sem).wait()


def gather_kernel(slots, share, wide, features, forward, *rest):
    backward, before, (key_out, value_out) = rest[: len(slots)], rest[len(slots) : -2], rest[-2:]
    tokens = forward.shape[0] * forward.shape[2]
    key_parts = [before[0][...]] if before else []
    value_parts = [before[1][...]] if before else []
    for slot, block in zip(slots, backward):
        def rows(ref, start, size):
            return ref[:, :, start : start + size].reshape(tokens, size)

        def forward_rows(start, size):
            return forward[:, slot, :, start : start + size].reshape(tokens, size)

        normed = forward_rows(0, share)
        key_parts.append(dot_ta(normed, rows(block, wide, features)))
        value_parts.append(dot_ta(normed, rows(block, wide + features, features)))
        value_parts.append(dot_ta(rows(block, 0, share), forward_rows(wide, features)))
    key_out[...] = sum(key_parts[1:], key_parts[0])
    value_out[...] = sum(value_parts[1:], value_parts[0])


def in_vmem(shape, dtype):
    return pltpu.VMEM(shape, dtype)


def shards(x0, w_key, w_value, w_score, segments, lengths, grades):
    sections = lax.axis_size("section")
    peers = lax.axis_size("dp")
    micro, width, model = x0.shape
    wk, wv = w_key[0], w_value[0]
    features = wk.shape[1]
    share = model // peers
    wide = -(-share // HD) * HD
    last = 2 * (sections - 1)
    ticks = micro + last
    rows = KV_HEADS * width

    tables = [
        in_vmem((1, model), F32),
        in_vmem(wk.shape, BF16),
        in_vmem(wv.shape, BF16),
        in_vmem((micro, width, HD), F32),
        in_vmem((micro, width, HD), F32),
        in_vmem((micro, rows, width), F32),
        in_vmem((micro, width, HD), F32),
        in_vmem((micro, width, HD), F32),
    ]
    state = [
        in_vmem((micro, width, model), BF16),
        in_vmem((micro, width, features), BF16),
        in_vmem((micro, width, features), BF16),
        in_vmem((micro, rows, width), F32),
        in_vmem((micro, width, HD), F32),
        in_vmem((micro, width, model), BF16),
    ]
    token = in_vmem((8, HD), F32)
    send_forward = jax.ShapeDtypeStruct((peers, micro, width, wide + features), BF16)
    send_backward = jax.ShapeDtypeStruct((peers, width, wide + 2 * features), BF16)
    row = jax.ShapeDtypeStruct((width, model), BF16)
    forward_scratch = [
        pltpu.VMEM((width, features), F32),
        pltpu.VMEM((width, features), F32),
        pltpu.VMEM((width, model), BF16),
        pltpu.VMEM((width, features), BF16),
        pltpu.VMEM((peers, width, wide + features), BF16),
        pltpu.SemaphoreType.DMA,
    ]
    inputs = [wk, wv, x0, w_score.reshape(1, model), segments, lengths.reshape(1, micro), grades]
    chunks = model // CHUNK
    made = pl.pallas_call(
        functools.partial(first_kernel, sections, micro, peers),
        out_shape=tables + state + [send_forward] + [send_backward] * micro + [token, row],
        in_specs=[HBM] * len(inputs),
        out_specs=[VMEM] * (len(tables) + len(state)) + [HBM] * (1 + micro) + [VMEM, VMEM],
        scratch_shapes=[
            pltpu.VMEM(segments.shape, jnp.int32),
            pltpu.SMEM((1, micro), jnp.int32),
            pltpu.VMEM(grades.shape, jnp.int32),
            pltpu.SemaphoreType.DMA((5,)),
            pltpu.SemaphoreType.DMA((chunks,)),
            pltpu.SemaphoreType.DMA((chunks,)),
        ]
        + forward_scratch,
        compiler_params=params(),
        name="first",
    )(*[pltpu.with_memory_space_constraint(value, pltpu.HBM) for value in inputs])
    w_score, wk, wv, cosine, sine, mask, ends, target = made[: len(tables)]
    held = list(made[len(tables) : len(tables) + len(state) + 1])
    blocks = list(made[len(tables) + len(state) + 1 : -2])
    token_value, produced = made[-2:]

    cost = pl.CostEstimate(flops=1000000, bytes_accessed=1000000, transcendentals=0)
    empty = jnp.zeros((width, model), BF16)
    incoming = [empty, empty, shifted(produced, "section", 1)]
    for tick in range(1, ticks):
        args = (incoming[tick], w_score, wk, wv, cosine, sine, mask, ends, target)
        count = len(held)
        *held, produced = pl.pallas_call(
            functools.partial(forward_kernel, tick, sections, micro, peers),
            out_shape=state + [send_forward, row],
            in_specs=[VMEM] * (len(args) + len(state)) + [HBM],
            out_specs=[VMEM] * len(state) + [HBM, VMEM],
            input_output_aliases={len(args) + n: n for n in range(count)},
            scratch_shapes=forward_scratch,
            compiler_params=params(),
            cost_estimate=cost,
            name="forward",
        )(*args, *held)
        if tick < ticks - 2:
            incoming.append(shifted(produced, "section", 1))

    saved, keys, values, probs, scales, grads, sent = held
    incoming = [empty] * 2
    received = []
    for tick in range(ticks):
        slots = [tick - 2 * hop for hop in range(sections)]
        slots = tuple(slot for slot in slots if 0 <= slot < micro)
        arrived = incoming[tick]
        if tick == 2:
            sent, token_value = lax.optimization_barrier((sent, token_value))
            got_forward = lax.all_to_all(sent, "dp", split_axis=0, concat_axis=0, tiled=True)
        if tick == last + 1:
            arrived, got_forward = lax.optimization_barrier((arrived, got_forward))
        if tick > last + 1:
            arrived, received[-2] = lax.optimization_barrier((arrived, received[-2]))
        args = (arrived, wk, wv, cosine, sine, saved, keys, values, probs, scales, grads)
        token_value, *outs = pl.pallas_call(
            functools.partial(backward_kernel, tick, sections, micro, peers, slots),
            out_shape=[token] + [send_backward] * len(slots) + [row],
            in_specs=[VMEM] * (len(args) + 1) + [HBM] * len(slots),
            out_specs=[VMEM] + [HBM] * len(slots) + [VMEM],
            input_output_aliases={len(args) + n: n for n in range(1 + len(slots))},
            scratch_shapes=[
                pltpu.VMEM((width, features), F32),
                pltpu.VMEM((width, model), F32),
                pltpu.VMEM((width, model), BF16),
                pltpu.VMEM((width, 2 * features), BF16),
                pltpu.VMEM((peers, width, wide + 2 * features), BF16),
                pltpu.SemaphoreType.DMA,
            ],
            compiler_params=params(),
            cost_estimate=cost,
            name="backward",
        )(*args, token_value, *[blocks[slot] for slot in slots])
        for slot, block in zip(slots, outs):
            blocks[slot] = block
        if tick < ticks - 2:
            incoming.append(shifted(outs[-1], "section", -1))
        if tick >= last:
            block = blocks[tick - last]
            received.append(
                lax.all_to_all(block, "dp", split_axis=0, concat_axis=0, tiled=True)
            )

    whole = jax.ShapeDtypeStruct((share, features), F32)
    total = ()
    for slots in (tuple(range(micro - 1)), (micro - 1,)):
        args = [got_forward, *[received[slot] for slot in slots], *total]
        total = pl.pallas_call(
            functools.partial(gather_kernel, slots, share, wide, features),
            out_shape=[whole, whole],
            in_specs=[VMEM] * len(args),
            out_specs=[VMEM] * 2,
            compiler_params=params(),
            cost_estimate=cost,
            name="gathered",
        )(*args)
    return (total[0][None], total[1][None])


def solution(mesh):
    placed = (
        P(None, "dp", None),
        P("section", None, None),
        P("section", None, None),
        P(),
        P(None, "dp"),
        P(None, "dp"),
        P(None, "dp"),
    )
    return jax.shard_map(
        shards,
        mesh=mesh,
        in_specs=placed,
        out_specs=(P("section", "dp", None), P("section", "dp", None)),
        check_vma=False,
    )
```

```python
import functools

import jax
import jax.numpy as jnp
from jax import lax
from jax.experimental import pallas as pl
from jax.experimental.pallas import tpu as pltpu
from jax.sharding import PartitionSpec as P

HD = 128
KV_HEADS = 4
EPS = 1e-06
THETA = 1000000.0
NEG = -1e30
CHUNK = 1280
BF16 = jnp.bfloat16
F32 = jnp.float32

VMEM = pl.BlockSpec(memory_space=pltpu.VMEM)
HBM = pl.BlockSpec(memory_space=pl.ANY)


def params(mib=12):
    return pltpu.CompilerParams(vmem_limit_bytes=mib * 1024 * 1024)


def shifted(value, steps, senders):
    return lax.ppermute(value, "section", [(source, source + steps) for source in senders])


def between_chips(value, mask, chips):
    pairs = [(2 * c + k, 2 * partner(c, mask, chips) + k) for c in range(chips) for k in range(2)]
    return lax.ppermute(value, "dp", pairs)


def between_cores(value, chips):
    return lax.ppermute(value, "dp", [(d, d ^ 1) for d in range(2 * chips)])


def partner(chip, mask, chips):
    return chip ^ mask if chips & (chips - 1) == 0 else (mask - chip) % chips


def dot(left, right):
    return jnp.dot(left, right, preferred_element_type=F32)


def dot_tb(left, right):
    return lax.dot_general(left, right, (((1,), (1,)), ((), ())), preferred_element_type=F32)


def dot_ta(left, right):
    return lax.dot_general(left, right, (((0,), (0,)), ((), ())), preferred_element_type=F32)


def to_column(row, eye):
    return jnp.sum(jnp.where(eye, jnp.broadcast_to(row, eye.shape), 0.0), axis=1, keepdims=True)


def make_tables(
    micro, segments_ref, lengths_ref, grades_ref,
    cos_ref, sin_ref, mask_ref, ends_ref, target_ref,
):
    width = segments_ref.shape[1]
    square = (width, width)
    at_row = lax.broadcasted_iota(jnp.int32, square, 0)
    at_col = lax.broadcasted_iota(jnp.int32, square, 1)
    eye = at_row == at_col
    lane = lax.broadcasted_iota(jnp.int32, (width, HD), 1)
    half_lane = jnp.where(lane < HD // 2, lane, lane - HD // 2).astype(F32)
    freqs = jnp.exp(half_lane * F32(-2.0 / HD) * jnp.log(F32(THETA)))
    sign = jnp.where(lane < HD // 2, -1.0, 1.0)
    index = lax.broadcasted_iota(jnp.int32, (width, 1), 0)
    for slot in range(micro):
        seg_row = segments_ref[slot : slot + 1, :].astype(F32)
        seg_col = to_column(seg_row, eye)
        grade_col = to_column(grades_ref[slot : slot + 1, :].astype(F32), eye)
        length = lengths_ref[0, slot]
        same = seg_col == seg_row
        offset = jnp.sum(jnp.where(same & (at_col < at_row), 1.0, 0.0), axis=1, keepdims=True)
        angles = offset * freqs
        cos_ref[slot] = jnp.cos(angles)
        sin_ref[slot] = jnp.sin(angles) * sign
        allowed = same & (at_col <= at_row) & (at_row < length) & (at_col < length)
        mask = jnp.where(allowed | eye, 1.0, 0.0)
        for head in range(KV_HEADS):
            mask_ref[slot, head * width : (head + 1) * width, :] = mask
        changes = jnp.sum(
            jnp.where((at_col == at_row + 1) & jnp.logical_not(same), 1.0, 0.0),
            axis=1, keepdims=True,
        )
        following = (changes > 0.0) | (index == width - 1)
        ends = (index < length) & (following | (index == length - 1))
        logits = jnp.where(ends, grade_col, NEG)
        weight = jnp.exp(logits - jnp.max(logits, axis=0, keepdims=True))
        target = weight / jnp.sum(weight, axis=0, keepdims=True)
        ends_ref[slot] = jnp.broadcast_to(jnp.where(ends, 1.0, 0.0), (width, HD))
        target_ref[slot] = jnp.broadcast_to(target, (width, HD))


def first_kernel(
    sections, micro, chips,
    wk_hbm, wv_hbm, x0_hbm, score_hbm, segments_hbm, lengths_hbm, grades_hbm,
    w_score, wk, wv, cosine, sine, mask, ends, target,
    saved, keys, values, probs, scales, grads, *rest,
):
    sent = rest[:chips]
    outgoing = rest[-13]
    segments_ref, lengths_ref, grades_ref, small, key_sems, value_sems = rest[-12:-6]
    scratch = rest[-6:]
    model = wk.shape[0]
    copies = [
        pltpu.make_async_copy(segments_hbm, segments_ref, small.at[0]),
        pltpu.make_async_copy(lengths_hbm, lengths_ref, small.at[1]),
        pltpu.make_async_copy(grades_hbm, grades_ref, small.at[2]),
        pltpu.make_async_copy(x0_hbm, saved, small.at[3]),
        pltpu.make_async_copy(score_hbm, w_score, small.at[4]),
    ]
    for copy in copies:
        copy.start()

    def chunk_copies(c):
        cols = pl.ds(c * CHUNK, CHUNK)
        return (
            pltpu.make_async_copy(wk_hbm.at[cols], wk.at[cols], key_sems.at[c]),
            pltpu.make_async_copy(wv_hbm.at[cols], wv.at[cols], value_sems.at[c]),
        )

    for c in range(model // CHUNK):
        for copy in chunk_copies(c):
            copy.start()
    for copy in copies[:3]:
        copy.wait()
    make_tables(
        micro, segments_ref, lengths_ref, grades_ref, cosine, sine, mask, ends, target
    )
    for copy in copies[3:]:
        copy.wait()
    section = lax.axis_index("section")

    @pl.when(section == 0)
    def _():
        def wait_chunk(c):
            for copy in chunk_copies(c):
                copy.wait()

        forward_body(
            0, section, sections, chips, wait_chunk,
            w_score, wk, wv, cosine, sine, mask, ends, target,
            saved, keys, values, probs, scales, grads, *sent, outgoing, *scratch,
        )

    @pl.when(section != 0)
    def _():
        for c in range(model // CHUNK):
            for copy in chunk_copies(c):
                copy.wait()


def row_scale(ref_value_chunks, model):
    total = None
    for chunk in ref_value_chunks:
        part = chunk * chunk
        total = part if total is None else total + part
    return lax.rsqrt(jnp.sum(total, axis=1, keepdims=True) / model + EPS)


def head_cols(head):
    return slice(head * HD, (head + 1) * HD)


def forward_kernel(
    tick, sections, micro, chips,
    incoming, w_score, wk, wv, cosine, sine, mask, ends, target,
    *rest,
):
    section = lax.axis_index("section")
    offset = tick - 2 * section
    slot = jnp.clip(offset, 0, micro - 1)
    rest = rest[6 + chips :]
    saved = rest[0]

    @pl.when((offset >= 0) & (offset < micro))
    def _():
        @pl.when(section != 0)
        def _():
            saved[slot] = incoming[...]

        forward_body(
            slot, section, sections, chips, None,
            w_score, wk, wv, cosine, sine, mask, ends, target, *rest,
        )


def fill_block(block, columns, factors):
    chips = block.shape[0]
    share = columns.shape[1] // (2 * chips)
    wide = (block.shape[2] - factors.shape[1]) // 2
    for device in range(2 * chips):
        start = (device % 2) * wide
        block[device // 2, :, start : start + share] = columns[:, device * share : (device + 1) * share]
    for chip in range(chips):
        block[chip, :, 2 * wide :] = factors[...]


def block_copies(block, targets, sems):
    chips = len(targets)
    chip = lax.axis_index("dp") // 2
    return [
        pltpu.make_async_copy(block.at[partner(chip, mask, chips)], target, sems.at[mask])
        for mask, target in enumerate(targets)
    ]


def forward_body(
    slot, section, sections, chips, wait_chunk,
    w_score, wk, wv, cosine, sine, mask, ends, target,
    saved, keys, values, probs, scales, grads, *rest,
):
    sent, outgoing = rest[:chips], rest[chips]
    acc_k, acc_v, normed, mixed, block, sems = rest[chips + 1 :]
    width, model = outgoing.shape
    features = KV_HEADS * HD
    step = CHUNK // 2

    def chunk_of(ref, start):
        return ref[slot, :, start : start + step].astype(F32)

    scale = row_scale([chunk_of(saved, c) for c in range(0, model, step)], model)
    scales[slot] = jnp.broadcast_to(scale, (width, HD))
    for c in range(0, model, step):
        normed[:, c : c + step] = (chunk_of(saved, c) * scale).astype(BF16)
    acc_k[...] = jnp.zeros_like(acc_k)
    acc_v[...] = jnp.zeros_like(acc_v)

    @pl.loop(0, model // CHUNK)
    def _(c):
        if wait_chunk is not None:
            wait_chunk(c)
        cols = pl.ds(pl.multiple_of(c * CHUNK, CHUNK), CHUNK)
        piece = normed[:, cols]
        acc_k[...] += dot(piece, wk[cols, :])
        acc_v[...] += dot(piece, wv[cols, :])

    cos_value = cosine[slot]
    sin_value = sine[slot]
    scores = []
    for head in range(KV_HEADS):
        vec = acc_k[:, head_cols(head)]
        turned = vec * cos_value + pltpu.roll(vec, HD // 2, 1) * sin_value
        key = turned.astype(BF16)
        keys[slot, :, head_cols(head)] = key
        scores.append(dot_tb(key, key))
    values[slot] = acc_v[...].astype(BF16)
    score = jnp.concatenate(scores, axis=0) / HD
    score = jnp.where(mask[slot] > 0.0, score, NEG)
    weight = jnp.exp(score - jnp.max(score, axis=1, keepdims=True))
    prob = weight / jnp.sum(weight, axis=1, keepdims=True)
    probs[slot] = prob
    prob_b = prob.astype(BF16)
    for head in range(KV_HEADS):
        out = dot(prob_b[head * width : (head + 1) * width, :], values[slot, :, head_cols(head)])
        mixed[:, head_cols(head)] = out.astype(BF16)

    fill_block(block, normed, mixed)
    copies = block_copies(block, [ref.at[slot] for ref in sent], sems)
    for copy in copies:
        copy.start()

    @pl.loop(0, model // CHUNK)
    def _(c):
        cols = pl.ds(pl.multiple_of(c * CHUNK, CHUNK), CHUNK)
        out = saved[slot, :, cols].astype(F32) + dot_tb(mixed[...], wv[cols, :])
        outgoing[:, cols] = out.astype(BF16)

    @pl.when(section == sections - 1)
    def _():
        def last_of(start):
            return outgoing[:, start : start + step].astype(F32)

        last_scale = row_scale([last_of(c) for c in range(0, model, step)], model)
        along = None
        for c in range(0, model, step):
            part = last_of(c) * w_score[:, c : c + step]
            along = part if along is None else along + part
        along = jnp.sum(along, axis=1, keepdims=True)
        is_end = ends[slot][:, :1] > 0.0
        logits = jnp.where(is_end, last_scale * along, NEG)
        part = jnp.exp(logits - jnp.max(logits, axis=0, keepdims=True))
        chosen = part / jnp.sum(part, axis=0, keepdims=True)
        g = jnp.where(is_end, chosen - target[slot][:, :1], 0.0)
        first = last_scale * g
        second = last_scale * last_scale * last_scale * (g * along / model)
        for c in range(0, model, step):
            value = first * w_score[:, c : c + step] - last_of(c) * second
            grads[slot, :, c : c + step] = value.astype(BF16)

    for copy in copies:
        copy.wait()


def backward_kernel(
    tick, sections, micro, chips, groups,
    incoming, wk, wv, cosine, sine, saved, keys, values, probs, scales, grads,
    *rest,
):
    count = len(groups) * chips
    sent = rest[count + 2 : 2 * count + 2]
    outgoing = rest[2 * count + 2]
    acc, full, current, flat, block, sems = rest[2 * count + 3 :]
    section = lax.axis_index("section")
    offset = tick - 2 * (sections - 1 - section)
    slot = jnp.clip(offset, 0, micro - 1)
    width, model = incoming.shape
    features = KV_HEADS * HD
    step = CHUNK // 2

    def for_group(act):
        for n, group in enumerate(groups):
            @pl.when((slot >= group[0]) & (slot <= group[-1]))
            def _():
                index = jnp.clip(slot - group[0], 0, len(group) - 1)
                targets = [ref.at[index] for ref in sent[n * chips : (n + 1) * chips]]
                for copy in block_copies(block, targets, sems):
                    act(copy)

    @pl.when((offset >= 0) & (offset < micro))
    def _():
        @pl.when(section == sections - 1)
        def _():
            current[...] = grads[slot]

        @pl.when(section != sections - 1)
        def _():
            current[...] = incoming[...]

        acc[...] = jnp.zeros_like(acc)

        @pl.loop(0, model // CHUNK)
        def _(c):
            cols = pl.ds(pl.multiple_of(c * CHUNK, CHUNK), CHUNK)
            acc[...] += dot(current[:, cols], wv[cols, :])

        cos_value = cosine[slot]
        sin_value = sine[slot]
        prob = probs[slot]
        prob_b = prob.astype(BF16)
        grad_probs = []
        for head in range(KV_HEADS):
            rows = slice(head * width, (head + 1) * width)
            mixed_grad = acc[:, head_cols(head)].astype(BF16)
            grad_probs.append(dot_tb(mixed_grad, values[slot, :, head_cols(head)]))
            flat[:, features + head * HD : features + (head + 1) * HD] = dot_ta(
                prob_b[rows, :], mixed_grad
            ).astype(BF16)
        grad_prob = jnp.concatenate(grad_probs, axis=0)
        grad_score = prob * (grad_prob - jnp.sum(prob * grad_prob, axis=1, keepdims=True))
        grad_score = grad_score.astype(BF16)
        for head in range(KV_HEADS):
            piece = grad_score[head * width : (head + 1) * width, :]
            key = keys[slot, :, head_cols(head)]
            vec = (dot(piece, key) + dot_ta(piece, key)) / HD
            turned = vec * cos_value - pltpu.roll(vec, HD // 2, 1) * sin_value
            flat[:, head_cols(head)] = turned.astype(BF16)

        fill_block(block, current, flat)
        for_group(lambda copy: copy.start())

        @pl.when(section != 0)
        def _():
            acc[...] = jnp.zeros_like(acc)

            @pl.loop(0, model // CHUNK)
            def _(c):
                cols = pl.ds(pl.multiple_of(c * CHUNK, CHUNK), CHUNK)
                out = dot_tb(flat[:, :features], wk[cols, :])
                out = out + dot_tb(flat[:, features:], wv[cols, :])
                full[:, cols] = out
                along = out * saved[slot, :, cols].astype(F32)
                total = along[:, :HD]
                for start in range(HD, CHUNK, HD):
                    total = total + along[:, start : start + HD]
                acc[:, :HD] += total

            scale = scales[slot][:, :1]
            mean = jnp.sum(acc[:, :HD], axis=1, keepdims=True) / model
            second = scale * scale * scale * mean
            for c in range(0, model, step):
                cols = slice(c, c + step)
                value = (
                    current[:, cols].astype(F32)
                    + scale * full[:, cols]
                    - saved[slot, :, cols].astype(F32) * second
                )
                outgoing[:, cols] = value.astype(BF16)

        for_group(lambda copy: copy.wait())


def gather_kernel(groups, share, wide, features, final, *rest):
    count = 2 + 2 * len(groups)
    forward, backward = rest[:2], rest[2:count]
    before = rest[count : count + 2] if final else ()
    key_out, value_out = rest[count + len(before) : count + len(before) + 2]
    normed, mixed, grads, flat, totals, sems, out_sems = rest[count + len(before) + 2 :]
    mine = pl.multiple_of(lax.axis_index("dp") % 2 * wide, HD)
    first = groups[0][0]
    slots = normed.shape[2]
    pairs = []
    for half, ref in enumerate(forward):
        at = ref.at[:, pl.ds(first, slots)]
        pairs.append((at.at[:, :, :, pl.ds(mine, wide)], normed.at[half]))
        pairs.append((at.at[:, :, :, pl.ds(2 * wide, features)], mixed.at[half]))
    for n, ref in enumerate(backward):
        group = groups[n // 2]
        inside = pl.ds(group[0] - first, len(group))
        pairs.append((ref.at[:, :, :, pl.ds(mine, wide)], grads.at[n % 2, :, inside]))
        pairs.append((ref.at[:, :, :, pl.ds(2 * wide, 2 * features)], flat.at[n % 2, :, inside]))
    copies = [pltpu.make_async_copy(*pair, sems.at[n]) for n, pair in enumerate(pairs)]
    for copy in copies:
        copy.start()
    for copy in copies:
        copy.wait()
    tokens = normed.shape[0] * normed.shape[1] * normed.shape[3]

    def rows(ref, slot, start, size):
        return ref[:, :, slot, :, start : start + size].reshape(tokens, size)

    size = HD if share % HD == 0 else share
    outs = []
    for start in range(0, share, size):
        at = pl.ds(start, size)
        key_part, value_part = [ref[at, :] for ref in before] if final else (0.0, 0.0)
        for slot in range(slots):
            left = rows(normed, slot, start, size)
            key_part += dot_ta(left, rows(flat, slot, 0, features))
            value_part += dot_ta(left, rows(flat, slot, features, features))
            value_part += dot_ta(rows(grads, slot, start, size), rows(mixed, slot, 0, features))
        if final:
            totals[0, at, :] = key_part
            totals[1, at, :] = value_part
            for n, out in enumerate((key_out, value_out)):
                outs.append(
                    pltpu.make_async_copy(totals.at[n, at], out.at[at], out_sems.at[len(outs)])
                )
                outs[-1].start()
        else:
            key_out[at, :] = key_part
            value_out[at, :] = value_part
    for copy in outs:
        copy.wait()


def in_vmem(shape, dtype):
    return pltpu.VMEM(shape, dtype)


def shards(x0, w_key, w_value, w_score, segments, lengths, grades):
    sections = lax.axis_size("section")
    peers = lax.axis_size("dp")
    chips = peers // 2
    micro, width, model = x0.shape
    wk, wv = w_key[0], w_value[0]
    features = wk.shape[1]
    share = model // peers
    wide = -(-share // HD) * HD
    last = 2 * (sections - 1)
    ticks = micro + last
    rows = KV_HEADS * width

    tables = [
        in_vmem((1, model), F32),
        in_vmem(wk.shape, BF16),
        in_vmem(wv.shape, BF16),
        in_vmem((micro, width, HD), F32),
        in_vmem((micro, width, HD), F32),
        in_vmem((micro, rows, width), F32),
        in_vmem((micro, width, HD), F32),
        in_vmem((micro, width, HD), F32),
    ]
    state = [
        in_vmem((micro, width, model), BF16),
        in_vmem((micro, width, features), BF16),
        in_vmem((micro, width, features), BF16),
        in_vmem((micro, rows, width), F32),
        in_vmem((micro, width, HD), F32),
        in_vmem((micro, width, model), BF16),
    ]
    token = in_vmem((8, HD), F32)
    send_forward = pltpu.HBM((micro, width, 2 * wide + features), BF16)
    groups = [tuple(range(micro - 2)), (micro - 2,), (micro - 1,)]
    send_backward = [
        pltpu.HBM((len(group), width, 2 * wide + 2 * features), BF16) for group in groups
    ]
    row = jax.ShapeDtypeStruct((width, model), BF16)
    forward_scratch = [
        pltpu.VMEM((width, features), F32),
        pltpu.VMEM((width, features), F32),
        pltpu.VMEM((width, model), BF16),
        pltpu.VMEM((width, features), BF16),
        pltpu.VMEM((chips, width, 2 * wide + features), BF16),
        pltpu.SemaphoreType.DMA((chips,)),
    ]
    inputs = [wk, wv, x0, w_score.reshape(1, model), segments, lengths.reshape(1, micro), grades]
    chunks = model // CHUNK
    sends = [send_forward] * chips + [shape for shape in send_backward for _ in range(chips)]
    made = pl.pallas_call(
        functools.partial(first_kernel, sections, micro, chips),
        out_shape=tables + state + sends + [token, row],
        in_specs=[HBM] * len(inputs),
        out_specs=[VMEM] * (len(tables) + len(state)) + [HBM] * len(sends) + [VMEM, VMEM],
        scratch_shapes=[
            pltpu.VMEM(segments.shape, jnp.int32),
            pltpu.SMEM((1, micro), jnp.int32),
            pltpu.VMEM(grades.shape, jnp.int32),
            pltpu.SemaphoreType.DMA((5,)),
            pltpu.SemaphoreType.DMA((chunks,)),
            pltpu.SemaphoreType.DMA((chunks,)),
        ]
        + forward_scratch,
        compiler_params=params(),
        name="first",
    )(*[pltpu.with_memory_space_constraint(value, pltpu.HBM) for value in inputs])
    w_score, wk, wv, cosine, sine, mask, ends, target = made[: len(tables)]
    held = list(made[len(tables) : len(tables) + len(state) + chips])
    blocks = list(made[len(tables) + len(state) + chips : -2])
    blocks = [blocks[n : n + chips] for n in range(0, len(blocks), chips)]
    token_value, produced = made[-2:]

    def senders(tick, rank):
        return [s for s in range(sections) if rank(s) < sections - 1 and 0 <= tick - 2 * rank(s) < micro]

    def up(section):
        return section

    def down(section):
        return sections - 1 - section

    cost = pl.CostEstimate(flops=1000000, bytes_accessed=1000000, transcendentals=0)
    empty = jnp.zeros((width, model), BF16)
    incoming = [empty, empty, shifted(produced, 1, senders(0, up))]
    for tick in range(1, ticks):
        args = (incoming[tick], w_score, wk, wv, cosine, sine, mask, ends, target)
        count = len(held)
        *held, produced = pl.pallas_call(
            functools.partial(forward_kernel, tick, sections, micro, chips),
            out_shape=state + [send_forward] * chips + [row],
            in_specs=[VMEM] * (len(args) + len(state)) + [HBM] * chips,
            out_specs=[VMEM] * len(state) + [HBM] * chips + [VMEM],
            input_output_aliases={len(args) + n: n for n in range(count)},
            scratch_shapes=forward_scratch,
            compiler_params=params(),
            cost_estimate=cost,
            name="forward",
        )(*args, *held)
        if tick < ticks - 2:
            incoming.append(shifted(produced, 1, senders(tick, up)))

    saved, keys, values, probs, scales, grads, *sent = held
    incoming = [empty] * 2
    masks = sorted(range(1, chips), key=lambda m: (-bin(m).count("1"), m))
    per_tick = -(-len(masks) // 3)
    gathered = [None] * len(groups)
    for tick in range(ticks):
        for m in masks[(tick - 1) * per_tick : tick * per_tick] if tick else ():
            sent[m], token_value = lax.optimization_barrier((sent[m], token_value))
            sent[m] = between_chips(sent[m], m, chips)
        possible = [tick - 2 * hop for hop in range(sections)]
        filled = [n for n, group in enumerate(groups) if set(group) & set(possible)]
        args = (
            incoming[tick], wk, wv, cosine, sine, saved, keys, values, probs, scales, grads,
            token_value,
        )
        targets = [block for n in filled for block in blocks[n]]
        shapes = [send_backward[n] for n in filled for _ in range(chips)]
        token_value, *outs = pl.pallas_call(
            functools.partial(
                backward_kernel, tick, sections, micro, chips, [groups[n] for n in filled]
            ),
            out_shape=[token] + shapes + [row],
            in_specs=[VMEM] * len(args) + [HBM] * len(targets),
            out_specs=[VMEM] + [HBM] * len(targets) + [VMEM],
            input_output_aliases={len(args) - 1 + n: n for n in range(1 + len(targets))},
            scratch_shapes=[
                pltpu.VMEM((width, features), F32),
                pltpu.VMEM((width, model), F32),
                pltpu.VMEM((width, model), BF16),
                pltpu.VMEM((width, 2 * features), BF16),
                pltpu.VMEM((chips, width, 2 * wide + 2 * features), BF16),
                pltpu.SemaphoreType.DMA((chips,)),
            ],
            compiler_params=params(),
            cost_estimate=cost,
            name="backward",
        )(*args, *targets)
        for position, n in enumerate(filled):
            blocks[n] = outs[position * chips : (position + 1) * chips]
        if tick < ticks - 2:
            incoming.append(shifted(outs[-1], -1, senders(tick, down)))

        def both_cores(parts, token_value):
            parts, token_value = lax.optimization_barrier((parts, token_value))
            stacked = jnp.stack(parts)
            return [stacked, between_cores(stacked, chips)], token_value

        for n, group in enumerate(groups):
            if tick == last + group[-1]:
                for m in masks:
                    blocks[n][m] = between_chips(blocks[n][m], m, chips)
        if tick == last + groups[0][-1]:
            forward_blocks, token_value = both_cores(sent, token_value)
        for n, group in enumerate(groups[:-1]):
            if tick == last + group[-1] + 1:
                gathered[n], token_value = both_cores(blocks[n], token_value)
    gathered[-1], token_value = both_cores(blocks[-1], token_value)

    whole = jax.ShapeDtypeStruct((share, features), F32)
    total = ()
    for final, chosen in ((False, groups[:-1]), (True, groups[-1:])):
        args = [*forward_blocks, *[value for group in chosen for value in gathered[groups.index(group)]]]
        slots = sum(len(group) for group in chosen)
        at = (2, chips, slots, width)
        rows_out = share // HD if share % HD == 0 else 1
        total = pl.pallas_call(
            functools.partial(gather_kernel, chosen, share, wide, features, final),
            out_shape=[whole, whole],
            in_specs=[HBM] * len(args) + [VMEM] * len(total),
            out_specs=[HBM if final else VMEM] * 2,
            scratch_shapes=[
                pltpu.VMEM(at + (wide,), BF16),
                pltpu.VMEM(at + (features,), BF16),
                pltpu.VMEM(at + (wide,), BF16),
                pltpu.VMEM(at + (2 * features,), BF16),
                pltpu.VMEM((2, share if final else 8, features), F32),
                pltpu.SemaphoreType.DMA((2 * len(args),)),
                pltpu.SemaphoreType.DMA((2 * rows_out,)),
            ],
            compiler_params=params(24),
            cost_estimate=cost,
            name="gathered",
        )(*args, *total)
    return (total[0][None], total[1][None])


def solution(mesh):
    placed = (
        P(None, "dp", None),
        P("section", None, None),
        P("section", None, None),
        P(),
        P(None, "dp"),
        P(None, "dp"),
        P(None, "dp"),
    )
    return jax.shard_map(
        shards,
        mesh=mesh,
        in_specs=placed,
        out_specs=(P("section", "dp", None), P("section", "dp", None)),
        check_vma=False,
    )
```

```python
import functools

import jax
import jax.numpy as jnp
from jax import lax
from jax.experimental import pallas as pl
from jax.experimental.pallas import tpu as pltpu
from jax.sharding import PartitionSpec as P

HD = 128
KV_HEADS = 4
EPS = 1e-06
THETA = 1000000.0
NEG = -1e30
CHUNK = 1280
BF16 = jnp.bfloat16
F32 = jnp.float32

VMEM = pl.BlockSpec(memory_space=pltpu.VMEM)
HBM = pl.BlockSpec(memory_space=pl.ANY)


def params(mib=12):
    return pltpu.CompilerParams(vmem_limit_bytes=mib * 1024 * 1024)


def shifted(value, steps, senders):
    return lax.ppermute(value, "section", [(source, source + steps) for source in senders])


def between_chips(value, mask, chips):
    pairs = [(2 * c + k, 2 * partner(c, mask, chips) + k) for c in range(chips) for k in range(2)]
    return lax.ppermute(value, "dp", pairs)


def between_cores(value, chips):
    return lax.ppermute(value, "dp", [(d, d ^ 1) for d in range(2 * chips)])


def partner(chip, mask, chips):
    return chip ^ mask if chips & (chips - 1) == 0 else (mask - chip) % chips


def dot(left, right):
    return jnp.dot(left, right, preferred_element_type=F32)


def dot_tb(left, right):
    return lax.dot_general(left, right, (((1,), (1,)), ((), ())), preferred_element_type=F32)


def dot_ta(left, right):
    return lax.dot_general(left, right, (((0,), (0,)), ((), ())), preferred_element_type=F32)


def to_column(row, eye):
    return jnp.sum(jnp.where(eye, jnp.broadcast_to(row, eye.shape), 0.0), axis=1, keepdims=True)


def make_tables(
    micro, segments_ref, lengths_ref, grades_ref,
    cos_ref, sin_ref, mask_ref, ends_ref, target_ref,
):
    width = segments_ref.shape[1]
    square = (width, width)
    at_row = lax.broadcasted_iota(jnp.int32, square, 0)
    at_col = lax.broadcasted_iota(jnp.int32, square, 1)
    eye = at_row == at_col
    lane = lax.broadcasted_iota(jnp.int32, (width, HD), 1)
    half_lane = jnp.where(lane < HD // 2, lane, lane - HD // 2).astype(F32)
    freqs = jnp.exp(half_lane * F32(-2.0 / HD) * jnp.log(F32(THETA)))
    sign = jnp.where(lane < HD // 2, -1.0, 1.0)
    index = lax.broadcasted_iota(jnp.int32, (width, 1), 0)
    angles = lax.broadcasted_iota(jnp.int32, (width, HD), 0).astype(F32) * freqs
    cos_table = jnp.cos(angles)
    sin_table = jnp.sin(angles) * sign

    def picked(chosen, table):
        return jnp.dot(
            chosen, table, precision=lax.Precision.HIGHEST, preferred_element_type=F32
        )

    for slot in range(micro):
        seg_row = segments_ref[slot : slot + 1, :].astype(F32)
        seg_col = to_column(seg_row, eye)
        grade_col = to_column(grades_ref[slot : slot + 1, :].astype(F32), eye)
        length = lengths_ref[0, slot]
        same = seg_col == seg_row
        offset = jnp.sum(jnp.where(same & (at_col < at_row), 1.0, 0.0), axis=1, keepdims=True)
        chosen = jnp.where(offset == at_col.astype(F32), 1.0, 0.0)
        cos_ref[slot] = picked(chosen, cos_table)
        sin_ref[slot] = picked(chosen, sin_table)
        allowed = same & (at_col <= at_row) & (at_row < length) & (at_col < length)
        mask = jnp.where(allowed | eye, 1.0, 0.0)
        for head in range(KV_HEADS):
            mask_ref[slot, head * width : (head + 1) * width, :] = mask
        changes = jnp.sum(
            jnp.where((at_col == at_row + 1) & jnp.logical_not(same), 1.0, 0.0),
            axis=1, keepdims=True,
        )
        following = (changes > 0.0) | (index == width - 1)
        ends = (index < length) & (following | (index == length - 1))
        logits = jnp.where(ends, grade_col, NEG)
        weight = jnp.exp(logits - jnp.max(logits, axis=0, keepdims=True))
        target = weight / jnp.sum(weight, axis=0, keepdims=True)
        ends_ref[slot] = jnp.broadcast_to(jnp.where(ends, 1.0, 0.0), (width, HD))
        target_ref[slot] = jnp.broadcast_to(target, (width, HD))


def first_kernel(
    sections, micro, chips,
    wk_hbm, wv_hbm, x0_hbm, score_hbm, segments_hbm, lengths_hbm, grades_hbm,
    w_score, wk, wv, cosine, sine, mask, ends, target,
    saved, keys, values, probs, scales, grads, *rest,
):
    sent = rest[:chips]
    outgoing = rest[-12]
    segments_ref, lengths_ref, grades_ref, small, key_sems, value_sems = rest[-11:-5]
    scratch = rest[-5:]
    model = wk.shape[0]
    copies = [
        pltpu.make_async_copy(segments_hbm, segments_ref, small.at[0]),
        pltpu.make_async_copy(lengths_hbm, lengths_ref, small.at[1]),
        pltpu.make_async_copy(grades_hbm, grades_ref, small.at[2]),
        pltpu.make_async_copy(x0_hbm, saved, small.at[3]),
        pltpu.make_async_copy(score_hbm, w_score, small.at[4]),
    ]
    for copy in copies:
        copy.start()

    def key_copy(c):
        cols = pl.ds(c * CHUNK, CHUNK)
        return pltpu.make_async_copy(wk_hbm.at[cols], wk.at[cols], key_sems.at[c])

    def value_copy(c):
        cols = pl.ds(c * CHUNK, CHUNK)
        return pltpu.make_async_copy(wv_hbm.at[cols], wv.at[cols], value_sems.at[c])

    for c in range(model // CHUNK):
        key_copy(c).start()
    for copy in copies[:3]:
        copy.wait()
    make_tables(
        micro, segments_ref, lengths_ref, grades_ref, cosine, sine, mask, ends, target
    )
    for copy in copies[3:]:
        copy.wait()
    for c in range(model // CHUNK):
        value_copy(c).start()
    section = lax.axis_index("section")

    @pl.when(section == 0)
    def _():
        def wait_values():
            for c in range(model // CHUNK):
                value_copy(c).wait()

        forward_body(
            0, section, sections, chips, (lambda c: key_copy(c).wait(), wait_values),
            w_score, wk, wv, cosine, sine, mask, ends, target,
            saved, keys, values, probs, scales, grads, *sent, outgoing, *scratch,
        )

    @pl.when(section != 0)
    def _():
        for c in range(model // CHUNK):
            key_copy(c).wait()
            value_copy(c).wait()


def row_scale(ref_value_chunks, model):
    total = None
    for chunk in ref_value_chunks:
        part = chunk * chunk
        total = part if total is None else total + part
    return lax.rsqrt(jnp.sum(total, axis=1, keepdims=True) / model + EPS)


def head_cols(head):
    return slice(head * HD, (head + 1) * HD)


def forward_kernel(
    tick, sections, micro, chips,
    incoming, w_score, wk, wv, cosine, sine, mask, ends, target,
    *rest,
):
    section = lax.axis_index("section")
    offset = tick - 2 * section
    slot = jnp.clip(offset, 0, micro - 1)
    rest = rest[6 + chips :]
    saved = rest[0]

    @pl.when((offset >= 0) & (offset < micro))
    def _():
        @pl.when(section != 0)
        def _():
            saved[slot] = incoming[...]

        forward_body(
            slot, section, sections, chips, None,
            w_score, wk, wv, cosine, sine, mask, ends, target, *rest,
        )


def fill_block(block, columns, factors):
    chips = block.shape[0]
    share = columns.shape[1] // (2 * chips)
    wide = (block.shape[2] - factors.shape[1]) // 2
    for device in range(2 * chips):
        start = (device % 2) * wide
        block[device // 2, :, start : start + share] = columns[:, device * share : (device + 1) * share]
    for chip in range(chips):
        block[chip, :, 2 * wide :] = factors[...]


def block_copies(block, targets, sems):
    chips = len(targets)
    chip = lax.axis_index("dp") // 2
    return [
        pltpu.make_async_copy(block.at[partner(chip, mask, chips)], target, sems.at[mask])
        for mask, target in enumerate(targets)
    ]


def forward_body(
    slot, section, sections, chips, waits,
    w_score, wk, wv, cosine, sine, mask, ends, target,
    saved, keys, values, probs, scales, grads, *rest,
):
    sent, outgoing = rest[:chips], rest[chips]
    acc_k, normed, mixed, block, sems = rest[chips + 1 :]
    width, model = outgoing.shape
    features = KV_HEADS * HD
    step = CHUNK // 2

    def chunk_of(ref, start):
        return ref[slot, :, start : start + step].astype(F32)

    scale = row_scale([chunk_of(saved, c) for c in range(0, model, step)], model)
    scales[slot] = jnp.broadcast_to(scale, (width, HD))
    for c in range(0, model, step):
        normed[:, c : c + step] = (chunk_of(saved, c) * scale).astype(BF16)
    acc_k[...] = jnp.zeros_like(acc_k)

    @pl.loop(0, model // CHUNK)
    def _(c):
        if waits is not None:
            waits[0](c)
        cols = pl.ds(pl.multiple_of(c * CHUNK, CHUNK), CHUNK)
        acc_k[...] += dot(normed[:, cols], wk[cols, :])

    if waits is not None:
        waits[1]()
    value = None
    for c in range(0, model, CHUNK):
        part = dot(normed[:, c : c + CHUNK], wv[c : c + CHUNK, :])
        value = part if value is None else value + part
    values[slot] = value.astype(BF16)
    cos_value = cosine[slot]
    sin_value = sine[slot]
    scores = []
    for head in range(KV_HEADS):
        vec = acc_k[:, head_cols(head)]
        turned = vec * cos_value + pltpu.roll(vec, HD // 2, 1) * sin_value
        key = turned.astype(BF16)
        keys[slot, :, head_cols(head)] = key
        scores.append(dot_tb(key, key))
    score = jnp.concatenate(scores, axis=0) / HD
    score = jnp.where(mask[slot] > 0.0, score, NEG)
    weight = jnp.exp(score - jnp.max(score, axis=1, keepdims=True))
    prob = weight / jnp.sum(weight, axis=1, keepdims=True)
    probs[slot] = prob
    prob_b = prob.astype(BF16)
    for head in range(KV_HEADS):
        out = dot(prob_b[head * width : (head + 1) * width, :], values[slot, :, head_cols(head)])
        mixed[:, head_cols(head)] = out.astype(BF16)

    fill_block(block, normed, mixed)
    copies = block_copies(block, [ref.at[slot] for ref in sent], sems)
    for copy in copies:
        copy.start()

    @pl.loop(0, model // CHUNK)
    def _(c):
        cols = pl.ds(pl.multiple_of(c * CHUNK, CHUNK), CHUNK)
        out = saved[slot, :, cols].astype(F32) + dot_tb(mixed[...], wv[cols, :])
        outgoing[:, cols] = out.astype(BF16)

    @pl.when(section == sections - 1)
    def _():
        def last_of(start):
            return outgoing[:, start : start + step].astype(F32)

        last_scale = row_scale([last_of(c) for c in range(0, model, step)], model)
        along = None
        for c in range(0, model, step):
            part = last_of(c) * w_score[:, c : c + step]
            along = part if along is None else along + part
        along = jnp.sum(along, axis=1, keepdims=True)
        is_end = ends[slot][:, :1] > 0.0
        logits = jnp.where(is_end, last_scale * along, NEG)
        part = jnp.exp(logits - jnp.max(logits, axis=0, keepdims=True))
        chosen = part / jnp.sum(part, axis=0, keepdims=True)
        g = jnp.where(is_end, chosen - target[slot][:, :1], 0.0)
        first = last_scale * g
        second = last_scale * last_scale * last_scale * (g * along / model)
        for c in range(0, model, step):
            value = first * w_score[:, c : c + step] - last_of(c) * second
            grads[slot, :, c : c + step] = value.astype(BF16)

    for copy in copies:
        copy.wait()


def backward_kernel(
    tick, sections, micro, chips, groups, through,
    incoming, wk, wv, cosine, sine, saved, keys, values, probs, scales, grads,
    *rest,
):
    count = len(groups) * chips
    total = count + through
    sent = rest[total + 2 : total + 2 + count]
    outgoing = rest[2 * total + 2]
    acc, full, current, flat, block, sems = rest[2 * total + 3 :]
    section = lax.axis_index("section")
    offset = tick - 2 * (sections - 1 - section)
    slot = jnp.clip(offset, 0, micro - 1)
    width, model = incoming.shape
    features = KV_HEADS * HD
    step = CHUNK // 2

    def for_group(act):
        for n, group in enumerate(groups):
            @pl.when((slot >= group[0]) & (slot <= group[-1]))
            def _():
                index = jnp.clip(slot - group[0], 0, len(group) - 1)
                targets = [ref.at[index] for ref in sent[n * chips : (n + 1) * chips]]
                for copy in block_copies(block, targets, sems):
                    act(copy)

    @pl.when((offset >= 0) & (offset < micro))
    def _():
        @pl.when(section == sections - 1)
        def _():
            current[...] = grads[slot]

        @pl.when(section != sections - 1)
        def _():
            current[...] = incoming[...]

        acc[...] = jnp.zeros_like(acc)

        @pl.loop(0, model // CHUNK)
        def _(c):
            cols = pl.ds(pl.multiple_of(c * CHUNK, CHUNK), CHUNK)
            acc[...] += dot(current[:, cols], wv[cols, :])

        def factors(value_pass):
            cos_value = cosine[slot]
            sin_value = sine[slot]
            prob = probs[slot]
            prob_b = prob.astype(BF16)
            grad_probs = []
            for head in range(KV_HEADS):
                rows = slice(head * width, (head + 1) * width)
                mixed_grad = acc[:, head_cols(head)].astype(BF16)
                grad_probs.append(dot_tb(mixed_grad, values[slot, :, head_cols(head)]))
                flat[:, features + head * HD : features + (head + 1) * HD] = dot_ta(
                    prob_b[rows, :], mixed_grad
                ).astype(BF16)
            if value_pass:
                for c in range(0, model, CHUNK):
                    full[:, c : c + CHUNK] = dot_tb(flat[:, features:], wv[c : c + CHUNK, :])
            grad_prob = jnp.concatenate(grad_probs, axis=0)
            grad_score = prob * (grad_prob - jnp.sum(prob * grad_prob, axis=1, keepdims=True))
            grad_score = grad_score.astype(BF16)
            for head in range(KV_HEADS):
                piece = grad_score[head * width : (head + 1) * width, :]
                key = keys[slot, :, head_cols(head)]
                vec = (dot(piece, key) + dot_ta(piece, key)) / HD
                turned = vec * cos_value - pltpu.roll(vec, HD // 2, 1) * sin_value
                flat[:, head_cols(head)] = turned.astype(BF16)
            fill_block(block, current, flat)

        @pl.when(section == 0)
        def _():
            factors(False)
            for_group(lambda copy: copy.start())

        @pl.when(section != 0)
        def _():
            factors(True)
            for_group(lambda copy: copy.start())
            acc[...] = jnp.zeros_like(acc)

            @pl.loop(0, model // CHUNK)
            def _(c):
                cols = pl.ds(pl.multiple_of(c * CHUNK, CHUNK), CHUNK)
                out = full[:, cols] + dot_tb(flat[:, :features], wk[cols, :])
                full[:, cols] = out
                along = out * saved[slot, :, cols].astype(F32)
                total = along[:, :HD]
                for start in range(HD, CHUNK, HD):
                    total = total + along[:, start : start + HD]
                acc[:, :HD] += total

            scale = scales[slot][:, :1]
            mean = jnp.sum(acc[:, :HD], axis=1, keepdims=True) / model
            second = scale * scale * scale * mean
            for c in range(0, model, step):
                cols = slice(c, c + step)
                value = (
                    current[:, cols].astype(F32)
                    + scale * full[:, cols]
                    - saved[slot, :, cols].astype(F32) * second
                )
                outgoing[:, cols] = value.astype(BF16)

        for_group(lambda copy: copy.wait())


def gate_kernel(*refs):
    del refs


def gather_kernel(group, pieces, share, wide, features, final, *rest):
    count = sum(pieces)
    sources = iter(rest[:count])
    before = rest[count : count + 2] if final else ()
    key_out, value_out = rest[count + len(before) : count + len(before) + 2]
    normed, mixed, grads, flat, totals, sems, out_sems = rest[count + len(before) + 2 :]
    mine = pl.multiple_of(lax.axis_index("dp") % 2 * wide, HD)
    slots = len(group)
    pairs = []
    for half, number in enumerate(pieces):
        chips = 0
        for ref in [next(sources) for _ in range(number)]:
            inside = pl.ds(chips, ref.shape[0])
            chips += ref.shape[0]
            if half < 2:
                ref, size, targets = ref.at[:, pl.ds(group[0], slots)], features, (normed, mixed)
            else:
                size, targets = 2 * features, (grads, flat)
            pairs.append((ref.at[:, :, :, pl.ds(mine, wide)], targets[0].at[half % 2, inside]))
            pairs.append((ref.at[:, :, :, pl.ds(2 * wide, size)], targets[1].at[half % 2, inside]))
    copies = [pltpu.make_async_copy(*pair, sems.at[n]) for n, pair in enumerate(pairs)]
    for copy in copies:
        copy.start()
    for copy in copies:
        copy.wait()
    tokens = normed.shape[0] * normed.shape[1] * normed.shape[3]

    def rows(ref, slot, start, size):
        return ref[:, :, slot, :, start : start + size].reshape(tokens, size)

    size = HD if share % HD == 0 else share
    outs = []
    for start in range(0, share, size):
        at = pl.ds(start, size)
        key_part, value_part = [ref[at, :] for ref in before] if final else (0.0, 0.0)
        for slot in range(slots):
            left = rows(normed, slot, start, size)
            key_part += dot_ta(left, rows(flat, slot, 0, features))
            value_part += dot_ta(left, rows(flat, slot, features, features))
            value_part += dot_ta(rows(grads, slot, start, size), rows(mixed, slot, 0, features))
        if final:
            totals[0, at, :] = key_part
            totals[1, at, :] = value_part
            for n, out in enumerate((key_out, value_out)):
                outs.append(
                    pltpu.make_async_copy(totals.at[n, at], out.at[at], out_sems.at[len(outs)])
                )
                outs[-1].start()
        else:
            key_out[at, :] = key_part
            value_out[at, :] = value_part
    for copy in outs:
        copy.wait()


def in_vmem(shape, dtype):
    return pltpu.VMEM(shape, dtype)


def shards(x0, w_key, w_value, w_score, segments, lengths, grades):
    sections = lax.axis_size("section")
    peers = lax.axis_size("dp")
    chips = peers // 2
    micro, width, model = x0.shape
    wk, wv = w_key[0], w_value[0]
    features = wk.shape[1]
    share = model // peers
    wide = -(-share // HD) * HD
    last = 2 * (sections - 1)
    ticks = micro + last
    rows = KV_HEADS * width

    tables = [
        in_vmem((1, model), F32),
        in_vmem(wk.shape, BF16),
        in_vmem(wv.shape, BF16),
        in_vmem((micro, width, HD), F32),
        in_vmem((micro, width, HD), F32),
        in_vmem((micro, rows, width), F32),
        in_vmem((micro, width, HD), F32),
        in_vmem((micro, width, HD), F32),
    ]
    state = [
        in_vmem((micro, width, model), BF16),
        in_vmem((micro, width, features), BF16),
        in_vmem((micro, width, features), BF16),
        in_vmem((micro, rows, width), F32),
        in_vmem((micro, width, HD), F32),
        in_vmem((micro, width, model), BF16),
    ]
    token = in_vmem((8, HD), F32)
    send_forward = pltpu.HBM((micro, width, 2 * wide + features), BF16)
    groups = [tuple(range(micro - 2)), (micro - 2, micro - 1)]
    send_backward = [
        pltpu.HBM((len(group), width, 2 * wide + 2 * features), BF16) for group in groups
    ]
    row = jax.ShapeDtypeStruct((width, model), BF16)
    forward_scratch = [
        pltpu.VMEM((width, features), F32),
        pltpu.VMEM((width, model), BF16),
        pltpu.VMEM((width, features), BF16),
        pltpu.VMEM((chips, width, 2 * wide + features), BF16),
        pltpu.SemaphoreType.DMA((chips,)),
    ]
    inputs = [wk, wv, x0, w_score.reshape(1, model), segments, lengths.reshape(1, micro), grades]
    chunks = model // CHUNK
    sends = [send_forward] * chips + [shape for shape in send_backward for _ in range(chips)]
    made = pl.pallas_call(
        functools.partial(first_kernel, sections, micro, chips),
        out_shape=tables + state + sends + [token, row],
        in_specs=[HBM] * len(inputs),
        out_specs=[VMEM] * (len(tables) + len(state)) + [HBM] * len(sends) + [VMEM, VMEM],
        scratch_shapes=[
            pltpu.VMEM(segments.shape, jnp.int32),
            pltpu.SMEM((1, micro), jnp.int32),
            pltpu.VMEM(grades.shape, jnp.int32),
            pltpu.SemaphoreType.DMA((5,)),
            pltpu.SemaphoreType.DMA((chunks,)),
            pltpu.SemaphoreType.DMA((chunks,)),
        ]
        + forward_scratch,
        compiler_params=params(),
        name="first",
    )(*[pltpu.with_memory_space_constraint(value, pltpu.HBM) for value in inputs])
    w_score, wk, wv, cosine, sine, mask, ends, target = made[: len(tables)]
    held = list(made[len(tables) : len(tables) + len(state) + chips])
    blocks = list(made[len(tables) + len(state) + chips : -2])
    blocks = [blocks[n : n + chips] for n in range(0, len(blocks), chips)]
    token_value, produced = made[-2:]

    def senders(tick, rank):
        return [s for s in range(sections) if rank(s) < sections - 1 and 0 <= tick - 2 * rank(s) < micro]

    def up(section):
        return section

    def down(section):
        return sections - 1 - section

    cost = pl.CostEstimate(flops=1000, bytes_accessed=1000, transcendentals=0)
    empty = jnp.zeros((width, model), BF16)
    incoming = [empty, empty, shifted(produced, 1, senders(0, up))]
    for tick in range(1, ticks):
        args = (incoming[tick], w_score, wk, wv, cosine, sine, mask, ends, target)
        count = len(held)
        *held, produced = pl.pallas_call(
            functools.partial(forward_kernel, tick, sections, micro, chips),
            out_shape=state + [send_forward] * chips + [row],
            in_specs=[VMEM] * (len(args) + len(state)) + [HBM] * chips,
            out_specs=[VMEM] * len(state) + [HBM] * chips + [VMEM],
            input_output_aliases={len(args) + n: n for n in range(count)},
            scratch_shapes=forward_scratch,
            compiler_params=params(),
            cost_estimate=cost,
            name="forward",
        )(*args, *held)
        if tick < ticks - 2:
            incoming.append(shifted(produced, 1, senders(tick, up)))

    saved, keys, values, probs, scales, grads, *sent = held
    incoming = [empty] * 2
    masks = sorted(range(1, chips), key=lambda m: (-bin(m).count("1"), m))
    per_tick = -(-len(masks) // 3)
    for tick in range(ticks):
        for m in masks[(tick - 1) * per_tick : tick * per_tick] if tick else ():
            sent[m] = between_chips(sent[m], m, chips)
        possible = [tick - 2 * hop for hop in range(sections)]
        filled = [n for n, group in enumerate(groups) if set(group) & set(possible)]
        args = (
            incoming[tick], wk, wv, cosine, sine, saved, keys, values, probs, scales, grads,
            token_value,
        )
        targets = [block for n in filled for block in blocks[n]]
        shapes = [send_backward[n] for n in filled for _ in range(chips)]
        through = tick in (last - 2, last + micro - 2)
        if through:
            targets += sent
            shapes += [send_forward] * chips
        token_value, *outs = pl.pallas_call(
            functools.partial(
                backward_kernel, tick, sections, micro, chips, [groups[n] for n in filled],
                chips if through else 0,
            ),
            out_shape=[token] + shapes + [row],
            in_specs=[VMEM] * len(args) + [HBM] * len(targets),
            out_specs=[VMEM] + [HBM] * len(targets) + [VMEM],
            input_output_aliases={len(args) - 1 + n: n for n in range(1 + len(targets))},
            scratch_shapes=[
                pltpu.VMEM((width, features), F32),
                pltpu.VMEM((width, model), F32),
                pltpu.VMEM((width, model), BF16),
                pltpu.VMEM((width, 2 * features), BF16),
                pltpu.VMEM((chips, width, 2 * wide + 2 * features), BF16),
                pltpu.SemaphoreType.DMA((chips,)),
            ],
            compiler_params=params(),
            cost_estimate=cost,
            name="backward",
        )(*args, *targets)
        for position, n in enumerate(filled):
            blocks[n] = outs[position * chips : (position + 1) * chips]
        if through:
            sent = list(outs[-1 - chips : -1])
        if tick < ticks - 2:
            incoming.append(shifted(outs[-1], -1, senders(tick, down)))

        for n, group in enumerate(groups):
            if tick == last + group[-1]:
                for m in masks:
                    blocks[n][m] = between_chips(blocks[n][m], m, chips)

    stacked = jnp.stack(sent)
    forward_blocks = [stacked], [between_cores(stacked, chips)]
    passed = blocks[0]
    token_value, *passed = pl.pallas_call(
        gate_kernel,
        out_shape=[token] + [pltpu.HBM(value.shape, value.dtype) for value in passed],
        in_specs=[VMEM] + [HBM] * len(passed),
        out_specs=[VMEM] + [HBM] * len(passed),
        input_output_aliases={n: n for n in range(1 + len(passed))},
        cost_estimate=cost,
        name="gate",
    )(token_value, *passed)

    stacked = jnp.stack(passed)
    gathered = [([stacked], [between_cores(stacked, chips)])]
    ours = [value[None] for value in blocks[1]]
    gathered.append((ours, [between_cores(value, chips) for value in ours]))

    whole = jax.ShapeDtypeStruct((share, features), F32)
    total = ()
    for final, chosen in ((False, 0), (True, 1)):
        args = [value for half in (*forward_blocks, *gathered[chosen]) for value in half]
        pieces = [len(half) for half in (*forward_blocks, *gathered[chosen])]
        chosen = groups[chosen]
        at = (2, chips, len(chosen), width)
        rows_out = share // HD if share % HD == 0 else 1
        total = pl.pallas_call(
            functools.partial(gather_kernel, chosen, pieces, share, wide, features, final),
            out_shape=[whole, whole],
            in_specs=[HBM] * len(args) + [VMEM] * len(total),
            out_specs=[HBM if final else VMEM] * 2,
            scratch_shapes=[
                pltpu.VMEM(at + (wide,), BF16),
                pltpu.VMEM(at + (features,), BF16),
                pltpu.VMEM(at + (wide,), BF16),
                pltpu.VMEM(at + (2 * features,), BF16),
                pltpu.VMEM((2, share if final else 8, features), F32),
                pltpu.SemaphoreType.DMA((2 * len(args),)),
                pltpu.SemaphoreType.DMA((2 * rows_out,)),
            ],
            compiler_params=params(24),
            cost_estimate=cost,
            name="gathered",
        )(*args, *total)
    return (total[0][None], total[1][None])


def solution(mesh):
    placed = (
        P(None, "dp", None),
        P("section", None, None),
        P("section", None, None),
        P(),
        P(None, "dp"),
        P(None, "dp"),
        P(None, "dp"),
    )
    return jax.shard_map(
        shards,
        mesh=mesh,
        in_specs=placed,
        out_specs=(P("section", "dp", None), P("section", "dp", None)),
        check_vma=False,
    )
```

```python
import functools

import jax
import jax.numpy as jnp
from jax import lax
from jax.experimental import pallas as pl
from jax.experimental.pallas import tpu as pltpu
from jax.sharding import PartitionSpec as P

HD = 128
KV_HEADS = 4
EPS = 1e-06
THETA = 1000000.0
NEG = -1e30
CHUNK = 1280
BF16 = jnp.bfloat16
F32 = jnp.float32

VMEM = pl.BlockSpec(memory_space=pltpu.VMEM)
HBM = pl.BlockSpec(memory_space=pl.ANY)


def params(mib=12):
    return pltpu.CompilerParams(vmem_limit_bytes=mib * 1024 * 1024)


def shifted(value, steps, senders):
    return lax.ppermute(value, "section", [(source, source + steps) for source in senders])


def between_chips(value, mask, chips):
    pairs = [(2 * c + k, 2 * partner(c, mask, chips) + k) for c in range(chips) for k in range(2)]
    return lax.ppermute(value, "dp", pairs)


def between_cores(value, chips):
    return lax.ppermute(value, "dp", [(d, d ^ 1) for d in range(2 * chips)])


def partner(chip, mask, chips):
    return chip ^ mask if chips & (chips - 1) == 0 else (mask - chip) % chips


def dot(left, right):
    return jnp.dot(left, right, preferred_element_type=F32)


def dot_tb(left, right):
    return lax.dot_general(left, right, (((1,), (1,)), ((), ())), preferred_element_type=F32)


def dot_ta(left, right):
    return lax.dot_general(left, right, (((0,), (0,)), ((), ())), preferred_element_type=F32)


def to_column(row, eye):
    return jnp.sum(jnp.where(eye, jnp.broadcast_to(row, eye.shape), 0.0), axis=1, keepdims=True)


def make_tables(
    micro, segments_ref, lengths_ref, grades_ref,
    cos_ref, sin_ref, mask_ref, ends_ref, target_ref,
):
    width = segments_ref.shape[1]
    square = (width, width)
    at_row = lax.broadcasted_iota(jnp.int32, square, 0)
    at_col = lax.broadcasted_iota(jnp.int32, square, 1)
    eye = at_row == at_col
    lane = lax.broadcasted_iota(jnp.int32, (width, HD), 1)
    half_lane = jnp.where(lane < HD // 2, lane, lane - HD // 2).astype(F32)
    freqs = jnp.exp(half_lane * F32(-2.0 / HD) * jnp.log(F32(THETA)))
    sign = jnp.where(lane < HD // 2, -1.0, 1.0)
    index = lax.broadcasted_iota(jnp.int32, (width, 1), 0)
    for slot in range(micro):
        seg_row = segments_ref[slot : slot + 1, :].astype(F32)
        seg_col = to_column(seg_row, eye)
        grade_col = to_column(grades_ref[slot : slot + 1, :].astype(F32), eye)
        length = lengths_ref[0, slot]
        same = seg_col == seg_row
        offset = jnp.sum(jnp.where(same & (at_col < at_row), 1.0, 0.0), axis=1, keepdims=True)
        angles = offset * freqs
        cos_ref[slot] = jnp.cos(angles)
        sin_ref[slot] = jnp.sin(angles) * sign
        allowed = same & (at_col <= at_row) & (at_row < length) & (at_col < length)
        mask = jnp.where(allowed | eye, 1.0, 0.0)
        for head in range(KV_HEADS):
            mask_ref[slot, head * width : (head + 1) * width, :] = mask
        changes = jnp.sum(
            jnp.where((at_col == at_row + 1) & jnp.logical_not(same), 1.0, 0.0),
            axis=1, keepdims=True,
        )
        following = (changes > 0.0) | (index == width - 1)
        ends = (index < length) & (following | (index == length - 1))
        logits = jnp.where(ends, grade_col, NEG)
        weight = jnp.exp(logits - jnp.max(logits, axis=0, keepdims=True))
        target = weight / jnp.sum(weight, axis=0, keepdims=True)
        ends_ref[slot] = jnp.broadcast_to(jnp.where(ends, 1.0, 0.0), (width, HD))
        target_ref[slot] = jnp.broadcast_to(target, (width, HD))


def first_kernel(
    sections, micro, chips,
    wk_hbm, wv_hbm, x0_hbm, score_hbm, segments_hbm, lengths_hbm, grades_hbm,
    w_score, wk, wv, cosine, sine, mask, ends, target,
    saved, keys, values, probs, scales, grads, *rest,
):
    sent = rest[:chips]
    outgoing = rest[-13]
    segments_ref, lengths_ref, grades_ref, small, key_sems, value_sems = rest[-12:-6]
    scratch = rest[-6:]
    model = wk.shape[0]
    copies = [
        pltpu.make_async_copy(segments_hbm, segments_ref, small.at[0]),
        pltpu.make_async_copy(lengths_hbm, lengths_ref, small.at[1]),
        pltpu.make_async_copy(grades_hbm, grades_ref, small.at[2]),
        pltpu.make_async_copy(x0_hbm.at[0], saved.at[0], small.at[3]),
    ]
    later = [
        pltpu.make_async_copy(x0_hbm.at[pl.ds(1, micro - 1)], saved.at[pl.ds(1, micro - 1)], small.at[4]),
        pltpu.make_async_copy(score_hbm, w_score, small.at[5]),
    ]
    chunks = model // CHUNK

    def chunk_copies(c):
        cols = pl.ds(c * CHUNK, CHUNK)
        return (
            pltpu.make_async_copy(wk_hbm.at[cols], wk.at[cols], key_sems.at[c]),
            pltpu.make_async_copy(wv_hbm.at[cols], wv.at[cols], value_sems.at[c]),
        )

    def wait_chunk(c):
        for copy in chunk_copies(c):
            copy.wait()

        @pl.when(c + 2 < chunks)
        def _():
            for copy in chunk_copies(jnp.minimum(c + 2, chunks - 1)):
                copy.start()

    for copy in copies:
        copy.start()
    for c in range(2):
        for copy in chunk_copies(c):
            copy.start()
    section = lax.axis_index("section")
    second = lax.axis_index("dp") % 2 == 1
    ahead = (section == 0) & jnp.logical_not(second)
    behind = (section == 0) & second
    for copy in copies:
        copy.wait()

    @pl.when(jnp.logical_not(ahead))
    def _():
        @pl.loop(0, chunks)
        def _(c):
            wait_chunk(c)

        for copy in later:
            copy.start()

    make_tables(
        micro, segments_ref, lengths_ref, grades_ref, cosine, sine, mask, ends, target
    )

    @pl.when(section == 0)
    def _():
        def wait_ahead(c):
            @pl.when(ahead)
            def _():
                wait_chunk(c)

        forward_body(
            0, section, sections, chips, wait_ahead,
            w_score, wk, wv, cosine, sine, mask, ends, target,
            saved, keys, values, probs, scales, grads, *sent, outgoing, *scratch,
        )

    @pl.when(ahead)
    def _():
        for copy in later:
            copy.start()

    for copy in later:
        copy.wait()


def row_scale(ref_value_chunks, model):
    total = None
    for chunk in ref_value_chunks:
        part = chunk * chunk
        total = part if total is None else total + part
    return lax.rsqrt(jnp.sum(total, axis=1, keepdims=True) / model + EPS)


def head_cols(head):
    return slice(head * HD, (head + 1) * HD)


def forward_kernel(
    tick, sections, micro, chips,
    incoming, w_score, wk, wv, cosine, sine, mask, ends, target,
    *rest,
):
    section = lax.axis_index("section")
    offset = tick - 2 * section
    slot = jnp.clip(offset, 0, micro - 1)
    rest = rest[6 + chips :]
    saved = rest[0]

    @pl.when((offset >= 0) & (offset < micro))
    def _():
        @pl.when(section != 0)
        def _():
            saved[slot] = incoming[...]

        forward_body(
            slot, section, sections, chips, None,
            w_score, wk, wv, cosine, sine, mask, ends, target, *rest,
        )


def fill_block(block, columns, factors):
    chips = block.shape[0]
    share = columns.shape[1] // (2 * chips)
    wide = (block.shape[2] - factors.shape[1]) // 2
    for device in range(2 * chips):
        start = (device % 2) * wide
        block[device // 2, :, start : start + share] = columns[:, device * share : (device + 1) * share]
    for chip in range(chips):
        block[chip, :, 2 * wide :] = factors[...]


def block_copies(block, targets, sems):
    chips = len(targets)
    chip = lax.axis_index("dp") // 2
    return [
        pltpu.make_async_copy(block.at[partner(chip, mask, chips)], target, sems.at[mask])
        for mask, target in enumerate(targets)
    ]


def forward_body(
    slot, section, sections, chips, wait_chunk,
    w_score, wk, wv, cosine, sine, mask, ends, target,
    saved, keys, values, probs, scales, grads, *rest,
):
    sent, outgoing = rest[:chips], rest[chips]
    acc_k, acc_v, normed, mixed, block, sems = rest[chips + 1 :]
    width, model = outgoing.shape
    features = KV_HEADS * HD
    step = CHUNK // 2

    def chunk_of(ref, start):
        return ref[slot, :, start : start + step].astype(F32)

    scale = row_scale([chunk_of(saved, c) for c in range(0, model, step)], model)
    scales[slot] = jnp.broadcast_to(scale, (width, HD))
    for c in range(0, model, step):
        normed[:, c : c + step] = (chunk_of(saved, c) * scale).astype(BF16)
    acc_k[...] = jnp.zeros_like(acc_k)
    acc_v[...] = jnp.zeros_like(acc_v)

    @pl.loop(0, model // CHUNK)
    def _(c):
        if wait_chunk is not None:
            wait_chunk(c)
        cols = pl.ds(pl.multiple_of(c * CHUNK, CHUNK), CHUNK)
        piece = normed[:, cols]
        acc_k[...] += dot(piece, wk[cols, :])
        acc_v[...] += dot(piece, wv[cols, :])

    cos_value = cosine[slot]
    sin_value = sine[slot]
    scores = []
    for head in range(KV_HEADS):
        vec = acc_k[:, head_cols(head)]
        turned = vec * cos_value + pltpu.roll(vec, HD // 2, 1) * sin_value
        key = turned.astype(BF16)
        keys[slot, :, head_cols(head)] = key
        scores.append(dot_tb(key, key))
    values[slot] = acc_v[...].astype(BF16)
    score = jnp.concatenate(scores, axis=0) / HD
    score = jnp.where(mask[slot] > 0.0, score, NEG)
    weight = jnp.exp(score - jnp.max(score, axis=1, keepdims=True))
    prob = weight / jnp.sum(weight, axis=1, keepdims=True)
    probs[slot] = prob
    prob_b = prob.astype(BF16)
    for head in range(KV_HEADS):
        out = dot(prob_b[head * width : (head + 1) * width, :], values[slot, :, head_cols(head)])
        mixed[:, head_cols(head)] = out.astype(BF16)

    fill_block(block, normed, mixed)
    copies = block_copies(block, [ref.at[slot] for ref in sent], sems)
    for copy in copies:
        copy.start()

    @pl.loop(0, model // CHUNK)
    def _(c):
        cols = pl.ds(pl.multiple_of(c * CHUNK, CHUNK), CHUNK)
        out = saved[slot, :, cols].astype(F32) + dot_tb(mixed[...], wv[cols, :])
        outgoing[:, cols] = out.astype(BF16)

    @pl.when(section == sections - 1)
    def _():
        def last_of(start):
            return outgoing[:, start : start + step].astype(F32)

        last_scale = row_scale([last_of(c) for c in range(0, model, step)], model)
        along = None
        for c in range(0, model, step):
            part = last_of(c) * w_score[:, c : c + step]
            along = part if along is None else along + part
        along = jnp.sum(along, axis=1, keepdims=True)
        is_end = ends[slot][:, :1] > 0.0
        logits = jnp.where(is_end, last_scale * along, NEG)
        part = jnp.exp(logits - jnp.max(logits, axis=0, keepdims=True))
        chosen = part / jnp.sum(part, axis=0, keepdims=True)
        g = jnp.where(is_end, chosen - target[slot][:, :1], 0.0)
        first = last_scale * g
        second = last_scale * last_scale * last_scale * (g * along / model)
        for c in range(0, model, step):
            value = first * w_score[:, c : c + step] - last_of(c) * second
            grads[slot, :, c : c + step] = value.astype(BF16)

    for copy in copies:
        copy.wait()


def backward_kernel(
    tick, sections, micro, chips, groups,
    incoming, wk, wv, cosine, sine, saved, keys, values, probs, scales, grads,
    *rest,
):
    count = len(groups) * chips
    sent = rest[count + 2 : 2 * count + 2]
    outgoing = rest[2 * count + 2]
    acc, full, current, flat, block, sems = rest[2 * count + 3 :]
    section = lax.axis_index("section")
    offset = tick - 2 * (sections - 1 - section)
    slot = jnp.clip(offset, 0, micro - 1)
    width, model = incoming.shape
    features = KV_HEADS * HD
    step = CHUNK // 2

    def for_group(act):
        for n, group in enumerate(groups):
            @pl.when((slot >= group[0]) & (slot <= group[-1]))
            def _():
                index = jnp.clip(slot - group[0], 0, len(group) - 1)
                targets = [ref.at[index] for ref in sent[n * chips : (n + 1) * chips]]
                for copy in block_copies(block, targets, sems):
                    act(copy)

    @pl.when((offset >= 0) & (offset < micro))
    def _():
        @pl.when(section == sections - 1)
        def _():
            current[...] = grads[slot]

        @pl.when(section != sections - 1)
        def _():
            current[...] = incoming[...]

        acc[...] = jnp.zeros_like(acc)

        @pl.loop(0, model // CHUNK)
        def _(c):
            cols = pl.ds(pl.multiple_of(c * CHUNK, CHUNK), CHUNK)
            acc[...] += dot(current[:, cols], wv[cols, :])

        cos_value = cosine[slot]
        sin_value = sine[slot]
        prob = probs[slot]
        prob_b = prob.astype(BF16)
        grad_probs = []
        for head in range(KV_HEADS):
            rows = slice(head * width, (head + 1) * width)
            mixed_grad = acc[:, head_cols(head)].astype(BF16)
            grad_probs.append(dot_tb(mixed_grad, values[slot, :, head_cols(head)]))
            flat[:, features + head * HD : features + (head + 1) * HD] = dot_ta(
                prob_b[rows, :], mixed_grad
            ).astype(BF16)
        grad_prob = jnp.concatenate(grad_probs, axis=0)
        grad_score = prob * (grad_prob - jnp.sum(prob * grad_prob, axis=1, keepdims=True))
        grad_score = grad_score.astype(BF16)
        for head in range(KV_HEADS):
            piece = grad_score[head * width : (head + 1) * width, :]
            key = keys[slot, :, head_cols(head)]
            vec = (dot(piece, key) + dot_ta(piece, key)) / HD
            turned = vec * cos_value - pltpu.roll(vec, HD // 2, 1) * sin_value
            flat[:, head_cols(head)] = turned.astype(BF16)

        fill_block(block, current, flat)
        for_group(lambda copy: copy.start())

        @pl.when(section != 0)
        def _():
            acc[...] = jnp.zeros_like(acc)

            @pl.loop(0, model // CHUNK)
            def _(c):
                cols = pl.ds(pl.multiple_of(c * CHUNK, CHUNK), CHUNK)
                out = dot_tb(flat[:, :features], wk[cols, :])
                out = out + dot_tb(flat[:, features:], wv[cols, :])
                full[:, cols] = out
                along = out * saved[slot, :, cols].astype(F32)
                total = along[:, :HD]
                for start in range(HD, CHUNK, HD):
                    total = total + along[:, start : start + HD]
                acc[:, :HD] += total

            scale = scales[slot][:, :1]
            mean = jnp.sum(acc[:, :HD], axis=1, keepdims=True) / model
            second = scale * scale * scale * mean
            for c in range(0, model, step):
                cols = slice(c, c + step)
                value = (
                    current[:, cols].astype(F32)
                    + scale * full[:, cols]
                    - saved[slot, :, cols].astype(F32) * second
                )
                outgoing[:, cols] = value.astype(BF16)

        for_group(lambda copy: copy.wait())


def gather_kernel(groups, share, wide, features, final, *rest):
    count = 2 + 2 * len(groups)
    forward, backward = rest[:2], rest[2:count]
    before = rest[count : count + 2] if final else ()
    key_out, value_out = rest[count + len(before) : count + len(before) + 2]
    normed, mixed, grads, flat, totals, sems, out_sems = rest[count + len(before) + 2 :]
    mine = pl.multiple_of(lax.axis_index("dp") % 2 * wide, HD)
    first = groups[0][0]
    slots = normed.shape[2]
    pairs = []
    for half, ref in enumerate(forward):
        at = ref.at[:, pl.ds(first, slots)]
        pairs.append((at.at[:, :, :, pl.ds(mine, wide)], normed.at[half]))
        pairs.append((at.at[:, :, :, pl.ds(2 * wide, features)], mixed.at[half]))
    for n, ref in enumerate(backward):
        group = groups[n // 2]
        inside = pl.ds(group[0] - first, len(group))
        pairs.append((ref.at[:, :, :, pl.ds(mine, wide)], grads.at[n % 2, :, inside]))
        pairs.append((ref.at[:, :, :, pl.ds(2 * wide, 2 * features)], flat.at[n % 2, :, inside]))
    copies = [pltpu.make_async_copy(*pair, sems.at[n]) for n, pair in enumerate(pairs)]
    for copy in copies:
        copy.start()
    for copy in copies:
        copy.wait()
    tokens = normed.shape[0] * normed.shape[1] * normed.shape[3]

    def rows(ref, slot, start, size):
        return ref[:, :, slot, :, start : start + size].reshape(tokens, size)

    size = HD if share % HD == 0 else share
    outs = []
    for start in range(0, share, size):
        at = pl.ds(start, size)
        key_part, value_part = [ref[at, :] for ref in before] if final else (0.0, 0.0)
        for slot in range(slots):
            left = rows(normed, slot, start, size)
            key_part += dot_ta(left, rows(flat, slot, 0, features))
            value_part += dot_ta(left, rows(flat, slot, features, features))
            value_part += dot_ta(rows(grads, slot, start, size), rows(mixed, slot, 0, features))
        if final:
            totals[0, at, :] = key_part
            totals[1, at, :] = value_part
            for n, out in enumerate((key_out, value_out)):
                outs.append(
                    pltpu.make_async_copy(totals.at[n, at], out.at[at], out_sems.at[len(outs)])
                )
                outs[-1].start()
        else:
            key_out[at, :] = key_part
            value_out[at, :] = value_part
    for copy in outs:
        copy.wait()


def in_vmem(shape, dtype):
    return pltpu.VMEM(shape, dtype)


def shards(x0, w_key, w_value, w_score, segments, lengths, grades):
    sections = lax.axis_size("section")
    peers = lax.axis_size("dp")
    chips = peers // 2
    micro, width, model = x0.shape
    wk, wv = w_key[0], w_value[0]
    features = wk.shape[1]
    share = model // peers
    wide = -(-share // HD) * HD
    last = 2 * (sections - 1)
    ticks = micro + last
    rows = KV_HEADS * width

    tables = [
        in_vmem((1, model), F32),
        in_vmem(wk.shape, BF16),
        in_vmem(wv.shape, BF16),
        in_vmem((micro, width, HD), F32),
        in_vmem((micro, width, HD), F32),
        in_vmem((micro, rows, width), F32),
        in_vmem((micro, width, HD), F32),
        in_vmem((micro, width, HD), F32),
    ]
    state = [
        in_vmem((micro, width, model), BF16),
        in_vmem((micro, width, features), BF16),
        in_vmem((micro, width, features), BF16),
        in_vmem((micro, rows, width), F32),
        in_vmem((micro, width, HD), F32),
        in_vmem((micro, width, model), BF16),
    ]
    token = in_vmem((8, HD), F32)
    send_forward = pltpu.HBM((micro, width, 2 * wide + features), BF16)
    groups = [tuple(range(micro - 2)), (micro - 2,), (micro - 1,)]
    send_backward = [
        pltpu.HBM((len(group), width, 2 * wide + 2 * features), BF16) for group in groups
    ]
    row = jax.ShapeDtypeStruct((width, model), BF16)
    forward_scratch = [
        pltpu.VMEM((width, features), F32),
        pltpu.VMEM((width, features), F32),
        pltpu.VMEM((width, model), BF16),
        pltpu.VMEM((width, features), BF16),
        pltpu.VMEM((chips, width, 2 * wide + features), BF16),
        pltpu.SemaphoreType.DMA((chips,)),
    ]
    inputs = [wk, wv, x0, w_score.reshape(1, model), segments, lengths.reshape(1, micro), grades]
    chunks = model // CHUNK
    sends = [send_forward] * chips + [shape for shape in send_backward for _ in range(chips)]
    made = pl.pallas_call(
        functools.partial(first_kernel, sections, micro, chips),
        out_shape=tables + state + sends + [token, row],
        in_specs=[HBM] * len(inputs),
        out_specs=[VMEM] * (len(tables) + len(state)) + [HBM] * len(sends) + [VMEM, VMEM],
        scratch_shapes=[
            pltpu.VMEM(segments.shape, jnp.int32),
            pltpu.SMEM((1, micro), jnp.int32),
            pltpu.VMEM(grades.shape, jnp.int32),
            pltpu.SemaphoreType.DMA((6,)),
            pltpu.SemaphoreType.DMA((chunks,)),
            pltpu.SemaphoreType.DMA((chunks,)),
        ]
        + forward_scratch,
        compiler_params=params(),
        name="first",
    )(*[pltpu.with_memory_space_constraint(value, pltpu.HBM) for value in inputs])
    w_score, wk, wv, cosine, sine, mask, ends, target = made[: len(tables)]
    held = list(made[len(tables) : len(tables) + len(state) + chips])
    blocks = list(made[len(tables) + len(state) + chips : -2])
    blocks = [blocks[n : n + chips] for n in range(0, len(blocks), chips)]
    token_value, produced = made[-2:]

    def senders(tick, rank):
        return [s for s in range(sections) if rank(s) < sections - 1 and 0 <= tick - 2 * rank(s) < micro]

    def up(section):
        return section

    def down(section):
        return sections - 1 - section

    cost = pl.CostEstimate(flops=1000000, bytes_accessed=1000000, transcendentals=0)
    empty = jnp.zeros((width, model), BF16)
    incoming = [empty, empty, shifted(produced, 1, senders(0, up))]
    for tick in range(1, ticks):
        args = (incoming[tick], w_score, wk, wv, cosine, sine, mask, ends, target)
        count = len(held)
        *held, produced = pl.pallas_call(
            functools.partial(forward_kernel, tick, sections, micro, chips),
            out_shape=state + [send_forward] * chips + [row],
            in_specs=[VMEM] * (len(args) + len(state)) + [HBM] * chips,
            out_specs=[VMEM] * len(state) + [HBM] * chips + [VMEM],
            input_output_aliases={len(args) + n: n for n in range(count)},
            scratch_shapes=forward_scratch,
            compiler_params=params(),
            cost_estimate=cost,
            name="forward",
        )(*args, *held)
        if tick < ticks - 2:
            incoming.append(shifted(produced, 1, senders(tick, up)))

    saved, keys, values, probs, scales, grads, *sent = held
    incoming = [empty] * 2
    masks = sorted(range(1, chips), key=lambda m: (-bin(m).count("1"), m))
    per_tick = -(-len(masks) // 3)
    gathered = [None] * len(groups)
    for tick in range(ticks):
        for m in masks[(tick - 1) * per_tick : tick * per_tick] if tick else ():
            sent[m], token_value = lax.optimization_barrier((sent[m], token_value))
            sent[m] = between_chips(sent[m], m, chips)
        possible = [tick - 2 * hop for hop in range(sections)]
        filled = [n for n, group in enumerate(groups) if set(group) & set(possible)]
        args = (
            incoming[tick], wk, wv, cosine, sine, saved, keys, values, probs, scales, grads,
            token_value,
        )
        targets = [block for n in filled for block in blocks[n]]
        shapes = [send_backward[n] for n in filled for _ in range(chips)]
        token_value, *outs = pl.pallas_call(
            functools.partial(
                backward_kernel, tick, sections, micro, chips, [groups[n] for n in filled]
            ),
            out_shape=[token] + shapes + [row],
            in_specs=[VMEM] * len(args) + [HBM] * len(targets),
            out_specs=[VMEM] + [HBM] * len(targets) + [VMEM],
            input_output_aliases={len(args) - 1 + n: n for n in range(1 + len(targets))},
            scratch_shapes=[
                pltpu.VMEM((width, features), F32),
                pltpu.VMEM((width, model), F32),
                pltpu.VMEM((width, model), BF16),
                pltpu.VMEM((width, 2 * features), BF16),
                pltpu.VMEM((chips, width, 2 * wide + 2 * features), BF16),
                pltpu.SemaphoreType.DMA((chips,)),
            ],
            compiler_params=params(),
            cost_estimate=cost,
            name="backward",
        )(*args, *targets)
        for position, n in enumerate(filled):
            blocks[n] = outs[position * chips : (position + 1) * chips]
        if tick < ticks - 2:
            incoming.append(shifted(outs[-1], -1, senders(tick, down)))

        def both_cores(parts, token_value):
            parts, token_value = lax.optimization_barrier((parts, token_value))
            stacked = jnp.stack(parts)
            return [stacked, between_cores(stacked, chips)], token_value

        for n, group in enumerate(groups):
            if tick == last + group[-1]:
                for m in masks:
                    blocks[n][m] = between_chips(blocks[n][m], m, chips)
        if tick == last + groups[0][-1]:
            forward_blocks, token_value = both_cores(sent, token_value)
        for n, group in enumerate(groups[:-1]):
            if tick == last + group[-1] + 1:
                gathered[n], token_value = both_cores(blocks[n], token_value)
    gathered[-1], token_value = both_cores(blocks[-1], token_value)

    whole = jax.ShapeDtypeStruct((share, features), F32)
    total = ()
    for final, chosen in ((False, groups[:-1]), (True, groups[-1:])):
        args = [*forward_blocks, *[value for group in chosen for value in gathered[groups.index(group)]]]
        slots = sum(len(group) for group in chosen)
        at = (2, chips, slots, width)
        rows_out = share // HD if share % HD == 0 else 1
        total = pl.pallas_call(
            functools.partial(gather_kernel, chosen, share, wide, features, final),
            out_shape=[whole, whole],
            in_specs=[HBM] * len(args) + [VMEM] * len(total),
            out_specs=[HBM if final else VMEM] * 2,
            scratch_shapes=[
                pltpu.VMEM(at + (wide,), BF16),
                pltpu.VMEM(at + (features,), BF16),
                pltpu.VMEM(at + (wide,), BF16),
                pltpu.VMEM(at + (2 * features,), BF16),
                pltpu.VMEM((2, share if final else 8, features), F32),
                pltpu.SemaphoreType.DMA((2 * len(args),)),
                pltpu.SemaphoreType.DMA((2 * rows_out,)),
            ],
            compiler_params=params(24),
            cost_estimate=cost,
            name="gathered",
        )(*args, *total)
    return (total[0][None], total[1][None])


def solution(mesh):
    placed = (
        P(None, "dp", None),
        P("section", None, None),
        P("section", None, None),
        P(),
        P(None, "dp"),
        P(None, "dp"),
        P(None, "dp"),
    )
    return jax.shard_map(
        shards,
        mesh=mesh,
        in_specs=placed,
        out_specs=(P("section", "dp", None), P("section", "dp", None)),
        check_vma=False,
    )
```

```python
import functools

import jax
import jax.numpy as jnp
from jax import lax
from jax.experimental import pallas as pl
from jax.experimental.pallas import tpu as pltpu
from jax.sharding import PartitionSpec as P

HD = 128
KV_HEADS = 4
EPS = 1e-06
THETA = 1000000.0
NEG = -1e30
CHUNK = 1280
PIECES = 4
BF16 = jnp.bfloat16
F32 = jnp.float32

VMEM = pl.BlockSpec(memory_space=pltpu.VMEM)
HBM = pl.BlockSpec(memory_space=pl.ANY)


def params(mib=12):
    return pltpu.CompilerParams(vmem_limit_bytes=mib * 1024 * 1024)


def shifted(value, steps, senders):
    return lax.ppermute(value, "section", [(source, source + steps) for source in senders])


def between_chips(value, mask, chips):
    pairs = [(2 * c + k, 2 * partner(c, mask, chips) + k) for c in range(chips) for k in range(2)]
    return lax.ppermute(value, "dp", pairs)


def between_cores(value, chips):
    return lax.ppermute(value, "dp", [(d, d ^ 1) for d in range(2 * chips)])


def partner(chip, mask, chips):
    return chip ^ mask if chips & (chips - 1) == 0 else (mask - chip) % chips


def dot(left, right):
    return jnp.dot(left, right, preferred_element_type=F32)


def dot_tb(left, right):
    return lax.dot_general(left, right, (((1,), (1,)), ((), ())), preferred_element_type=F32)


def dot_ta(left, right):
    return lax.dot_general(left, right, (((0,), (0,)), ((), ())), preferred_element_type=F32)


def to_column(row, eye):
    return jnp.sum(jnp.where(eye, jnp.broadcast_to(row, eye.shape), 0.0), axis=1, keepdims=True)


def make_tables(
    micro, segments_ref, lengths_ref, grades_ref,
    cos_ref, sin_ref, mask_ref, ends_ref, target_ref,
):
    width = segments_ref.shape[1]
    square = (width, width)
    at_row = lax.broadcasted_iota(jnp.int32, square, 0)
    at_col = lax.broadcasted_iota(jnp.int32, square, 1)
    eye = at_row == at_col
    lane = lax.broadcasted_iota(jnp.int32, (width, HD), 1)
    half_lane = jnp.where(lane < HD // 2, lane, lane - HD // 2).astype(F32)
    freqs = jnp.exp(half_lane * F32(-2.0 / HD) * jnp.log(F32(THETA)))
    sign = jnp.where(lane < HD // 2, -1.0, 1.0)
    index = lax.broadcasted_iota(jnp.int32, (width, 1), 0)
    for slot in range(micro):
        seg_row = segments_ref[slot : slot + 1, :].astype(F32)
        seg_col = to_column(seg_row, eye)
        grade_col = to_column(grades_ref[slot : slot + 1, :].astype(F32), eye)
        length = lengths_ref[0, slot]
        same = seg_col == seg_row
        offset = jnp.sum(jnp.where(same & (at_col < at_row), 1.0, 0.0), axis=1, keepdims=True)
        angles = offset * freqs
        cos_ref[slot] = jnp.cos(angles)
        sin_ref[slot] = jnp.sin(angles) * sign
        allowed = same & (at_col <= at_row) & (at_row < length) & (at_col < length)
        mask = jnp.where(allowed | eye, 1.0, 0.0)
        for head in range(KV_HEADS):
            mask_ref[slot, head * width : (head + 1) * width, :] = mask
        changes = jnp.sum(
            jnp.where((at_col == at_row + 1) & jnp.logical_not(same), 1.0, 0.0),
            axis=1, keepdims=True,
        )
        following = (changes > 0.0) | (index == width - 1)
        ends = (index < length) & (following | (index == length - 1))
        logits = jnp.where(ends, grade_col, NEG)
        weight = jnp.exp(logits - jnp.max(logits, axis=0, keepdims=True))
        target = weight / jnp.sum(weight, axis=0, keepdims=True)
        ends_ref[slot] = jnp.broadcast_to(jnp.where(ends, 1.0, 0.0), (width, HD))
        target_ref[slot] = jnp.broadcast_to(target, (width, HD))


def first_kernel(
    sections, micro, chips,
    wk_hbm, wv_hbm, x0_hbm, score_hbm, segments_hbm, lengths_hbm, grades_hbm,
    w_score, wk, wv, cosine, sine, mask, ends, target,
    saved, keys, values, probs, scales, grads, *rest,
):
    sent = rest[:chips]
    outgoing = rest[-13]
    segments_ref, lengths_ref, grades_ref, small, key_sems, value_sems = rest[-12:-6]
    scratch = rest[-6:]
    model = wk.shape[0]
    copies = [
        pltpu.make_async_copy(segments_hbm, segments_ref, small.at[0]),
        pltpu.make_async_copy(lengths_hbm, lengths_ref, small.at[1]),
        pltpu.make_async_copy(grades_hbm, grades_ref, small.at[2]),
        pltpu.make_async_copy(x0_hbm.at[0], saved.at[0], small.at[3]),
    ]
    later = [
        pltpu.make_async_copy(x0_hbm.at[pl.ds(1, micro - 1)], saved.at[pl.ds(1, micro - 1)], small.at[4]),
        pltpu.make_async_copy(score_hbm, w_score, small.at[5]),
    ]
    chunks = model // CHUNK

    size = CHUNK // PIECES

    def chunk_copies(c):
        copies = []
        for piece in range(PIECES):
            rows = pl.ds(pl.multiple_of(c * CHUNK + piece * size, 64), size)
            at = c * PIECES + piece
            copies.append(pltpu.make_async_copy(wk_hbm.at[rows], wk.at[rows], key_sems.at[at]))
            copies.append(pltpu.make_async_copy(wv_hbm.at[rows], wv.at[rows], value_sems.at[at]))
        return copies

    def wait_chunk(c):
        for copy in chunk_copies(c):
            copy.wait()

        @pl.when(c + 2 < chunks)
        def _():
            for copy in chunk_copies(jnp.minimum(c + 2, chunks - 1)):
                copy.start()

    for copy in copies:
        copy.start()
    for c in range(2):
        for copy in chunk_copies(c):
            copy.start()
    section = lax.axis_index("section")
    second = lax.axis_index("dp") % 2 == 1
    ahead = (section == 0) & jnp.logical_not(second)
    behind = (section == 0) & second
    for copy in copies:
        copy.wait()

    @pl.when(jnp.logical_not(ahead))
    def _():
        @pl.loop(0, chunks)
        def _(c):
            wait_chunk(c)

        for copy in later:
            copy.start()

    make_tables(
        micro, segments_ref, lengths_ref, grades_ref, cosine, sine, mask, ends, target
    )

    @pl.when(section == 0)
    def _():
        def wait_ahead(c):
            @pl.when(ahead)
            def _():
                wait_chunk(c)

        forward_body(
            0, 0, section, sections, chips, wait_ahead,
            w_score, wk, wv, cosine, sine, mask, ends, target,
            saved, keys, values, probs, scales, grads, *sent, outgoing, *scratch,
        )

    @pl.when(ahead)
    def _():
        for copy in later:
            copy.start()

    for copy in later:
        copy.wait()


def row_scale(ref_value_chunks, model):
    total = None
    for chunk in ref_value_chunks:
        part = chunk * chunk
        total = part if total is None else total + part
    return lax.rsqrt(jnp.sum(total, axis=1, keepdims=True) / model + EPS)


def when(possible, condition):
    return pl.when(condition) if possible else lambda body: None


def head_cols(head):
    return slice(head * HD, (head + 1) * HD)


def forward_kernel(
    tick, sections, micro, chips,
    incoming, w_score, wk, wv, cosine, sine, mask, ends, target,
    *rest,
):
    section = lax.axis_index("section")
    offset = tick - 2 * section
    slot = jnp.clip(offset, 0, micro - 1)
    rest = rest[6 + chips :]
    saved = rest[0]

    @pl.when((offset >= 0) & (offset < micro))
    def _():
        @pl.when(section != 0)
        def _():
            saved[slot] = incoming[...]

        forward_body(
            tick, slot, section, sections, chips, None,
            w_score, wk, wv, cosine, sine, mask, ends, target, *rest,
        )


def fill_block(block, columns, factors):
    chips = block.shape[0]
    share = columns.shape[1] // (2 * chips)
    wide = (block.shape[2] - factors.shape[1]) // 2
    for device in range(2 * chips):
        start = (device % 2) * wide
        block[device // 2, :, start : start + share] = columns[:, device * share : (device + 1) * share]
    for chip in range(chips):
        block[chip, :, 2 * wide :] = factors[...]


def block_copies(block, targets, sems):
    chips = len(targets)
    chip = lax.axis_index("dp") // 2
    return [
        pltpu.make_async_copy(block.at[partner(chip, mask, chips)], target, sems.at[mask])
        for mask, target in enumerate(targets)
    ]


def forward_body(
    tick, slot, section, sections, chips, wait_chunk,
    w_score, wk, wv, cosine, sine, mask, ends, target,
    saved, keys, values, probs, scales, grads, *rest,
):
    sent, outgoing = rest[:chips], rest[chips]
    acc_k, acc_v, normed, mixed, block, sems = rest[chips + 1 :]
    width, model = outgoing.shape
    features = KV_HEADS * HD
    step = CHUNK // 2

    def chunk_of(ref, start):
        return ref[slot, :, start : start + step].astype(F32)

    scale = row_scale([chunk_of(saved, c) for c in range(0, model, step)], model)
    scales[slot] = jnp.broadcast_to(scale, (width, HD))
    for c in range(0, model, step):
        normed[:, c : c + step] = (chunk_of(saved, c) * scale).astype(BF16)
    acc_k[...] = jnp.zeros_like(acc_k)
    acc_v[...] = jnp.zeros_like(acc_v)

    @pl.loop(0, model // CHUNK)
    def _(c):
        if wait_chunk is not None:
            wait_chunk(c)
        cols = pl.ds(pl.multiple_of(c * CHUNK, CHUNK), CHUNK)
        piece = normed[:, cols]
        acc_k[...] += dot(piece, wk[cols, :])
        acc_v[...] += dot(piece, wv[cols, :])

    cos_value = cosine[slot]
    sin_value = sine[slot]
    scores = []
    for head in range(KV_HEADS):
        vec = acc_k[:, head_cols(head)]
        turned = vec * cos_value + pltpu.roll(vec, HD // 2, 1) * sin_value
        key = turned.astype(BF16)
        keys[slot, :, head_cols(head)] = key
        scores.append(dot_tb(key, key))
    values[slot] = acc_v[...].astype(BF16)
    score = jnp.concatenate(scores, axis=0) / HD
    score = jnp.where(mask[slot] > 0.0, score, NEG)
    weight = jnp.exp(score - jnp.max(score, axis=1, keepdims=True))
    prob = weight / jnp.sum(weight, axis=1, keepdims=True)
    probs[slot] = prob
    prob_b = prob.astype(BF16)
    for head in range(KV_HEADS):
        out = dot(prob_b[head * width : (head + 1) * width, :], values[slot, :, head_cols(head)])
        mixed[:, head_cols(head)] = out.astype(BF16)

    fill_block(block, normed, mixed)
    copies = block_copies(block, [ref.at[slot] for ref in sent], sems)
    for copy in copies:
        copy.start()

    @pl.loop(0, model // CHUNK)
    def _(c):
        cols = pl.ds(pl.multiple_of(c * CHUNK, CHUNK), CHUNK)
        out = saved[slot, :, cols].astype(F32) + dot_tb(mixed[...], wv[cols, :])
        outgoing[:, cols] = out.astype(BF16)

    @when(tick >= 2 * (sections - 1), section == sections - 1)
    def _():
        def last_of(start):
            return outgoing[:, start : start + step].astype(F32)

        last_scale = row_scale([last_of(c) for c in range(0, model, step)], model)
        along = None
        for c in range(0, model, step):
            part = last_of(c) * w_score[:, c : c + step]
            along = part if along is None else along + part
        along = jnp.sum(along, axis=1, keepdims=True)
        is_end = ends[slot][:, :1] > 0.0
        logits = jnp.where(is_end, last_scale * along, NEG)
        part = jnp.exp(logits - jnp.max(logits, axis=0, keepdims=True))
        chosen = part / jnp.sum(part, axis=0, keepdims=True)
        g = jnp.where(is_end, chosen - target[slot][:, :1], 0.0)
        first = last_scale * g
        second = last_scale * last_scale * last_scale * (g * along / model)
        for c in range(0, model, step):
            value = first * w_score[:, c : c + step] - last_of(c) * second
            grads[slot, :, c : c + step] = value.astype(BF16)

    for copy in copies:
        copy.wait()


def backward_kernel(
    tick, sections, micro, chips, groups,
    incoming, wk, wv, cosine, sine, saved, keys, values, probs, scales, grads,
    *rest,
):
    count = len(groups) * chips
    sent = rest[count + 2 : 2 * count + 2]
    outgoing = rest[2 * count + 2]
    acc, full, current, flat, block, sems = rest[2 * count + 3 :]
    section = lax.axis_index("section")
    offset = tick - 2 * (sections - 1 - section)
    slot = jnp.clip(offset, 0, micro - 1)
    width, model = incoming.shape
    features = KV_HEADS * HD
    step = CHUNK // 2

    def for_group(act):
        for n, group in enumerate(groups):
            @pl.when((slot >= group[0]) & (slot <= group[-1]))
            def _():
                index = jnp.clip(slot - group[0], 0, len(group) - 1)
                targets = [ref.at[index] for ref in sent[n * chips : (n + 1) * chips]]
                for copy in block_copies(block, targets, sems):
                    act(copy)

    @pl.when((offset >= 0) & (offset < micro))
    def _():
        @when(tick < micro, section == sections - 1)
        def _():
            current[...] = grads[slot]

        @when(tick >= 2, section != sections - 1)
        def _():
            current[...] = incoming[...]

        acc[...] = jnp.zeros_like(acc)

        @pl.loop(0, model // CHUNK)
        def _(c):
            cols = pl.ds(pl.multiple_of(c * CHUNK, CHUNK), CHUNK)
            acc[...] += dot(current[:, cols], wv[cols, :])

        def factors(value_pass):
            cos_value = cosine[slot]
            sin_value = sine[slot]
            prob = probs[slot]
            prob_b = prob.astype(BF16)
            grad_probs = []
            for head in range(KV_HEADS):
                rows = slice(head * width, (head + 1) * width)
                mixed_grad = acc[:, head_cols(head)].astype(BF16)
                grad_probs.append(dot_tb(mixed_grad, values[slot, :, head_cols(head)]))
                flat[:, features + head * HD : features + (head + 1) * HD] = dot_ta(
                    prob_b[rows, :], mixed_grad
                ).astype(BF16)
            if value_pass:
                for c in range(0, model, CHUNK):
                    full[:, c : c + CHUNK] = dot_tb(flat[:, features:], wv[c : c + CHUNK, :])
            grad_prob = jnp.concatenate(grad_probs, axis=0)
            grad_score = prob * (grad_prob - jnp.sum(prob * grad_prob, axis=1, keepdims=True))
            grad_score = grad_score.astype(BF16)
            for head in range(KV_HEADS):
                piece = grad_score[head * width : (head + 1) * width, :]
                key = keys[slot, :, head_cols(head)]
                vec = (dot(piece, key) + dot_ta(piece, key)) / HD
                turned = vec * cos_value - pltpu.roll(vec, HD // 2, 1) * sin_value
                flat[:, head_cols(head)] = turned.astype(BF16)
            fill_block(block, current, flat)

        lowest = tick - 2 * (sections - 1)

        @when(lowest >= 0, section == 0)
        def _():
            factors(False)
            for_group(lambda copy: copy.start())

        @when(lowest + 2 < micro, section != 0)
        def _():
            factors(True)
            for_group(lambda copy: copy.start())
            acc[...] = jnp.zeros_like(acc)

            @pl.loop(0, model // CHUNK)
            def _(c):
                cols = pl.ds(pl.multiple_of(c * CHUNK, CHUNK), CHUNK)
                out = full[:, cols] + dot_tb(flat[:, :features], wk[cols, :])
                full[:, cols] = out
                along = out * saved[slot, :, cols].astype(F32)
                total = along[:, :HD]
                for start in range(HD, CHUNK, HD):
                    total = total + along[:, start : start + HD]
                acc[:, :HD] += total

            scale = scales[slot][:, :1]
            mean = jnp.sum(acc[:, :HD], axis=1, keepdims=True) / model
            second = scale * scale * scale * mean
            for c in range(0, model, step):
                cols = slice(c, c + step)
                value = (
                    current[:, cols].astype(F32)
                    + scale * full[:, cols]
                    - saved[slot, :, cols].astype(F32) * second
                )
                outgoing[:, cols] = value.astype(BF16)

        for_group(lambda copy: copy.wait())


def gather_kernel(groups, share, wide, features, final, *rest):
    count = 2 + 2 * len(groups)
    forward, backward = rest[:2], rest[2:count]
    before = rest[count : count + 2] if final else ()
    key_out, value_out = rest[count + len(before) : count + len(before) + 2]
    normed, mixed, grads, flat, totals, sems, out_sems = rest[count + len(before) + 2 :]
    mine = pl.multiple_of(lax.axis_index("dp") % 2 * wide, HD)
    first = groups[0][0]
    slots = normed.shape[2]
    pairs = []
    for half, ref in enumerate(forward):
        at = ref.at[:, pl.ds(first, slots)]
        pairs.append((at.at[:, :, :, pl.ds(mine, wide)], normed.at[half]))
        pairs.append((at.at[:, :, :, pl.ds(2 * wide, features)], mixed.at[half]))
    for n, ref in enumerate(backward):
        group = groups[n // 2]
        inside = pl.ds(group[0] - first, len(group))
        pairs.append((ref.at[:, :, :, pl.ds(mine, wide)], grads.at[n % 2, :, inside]))
        pairs.append((ref.at[:, :, :, pl.ds(2 * wide, 2 * features)], flat.at[n % 2, :, inside]))
    copies = [pltpu.make_async_copy(*pair, sems.at[n]) for n, pair in enumerate(pairs)]
    for copy in copies:
        copy.start()
    for copy in copies:
        copy.wait()
    tokens = normed.shape[0] * normed.shape[1] * normed.shape[3]

    def rows(ref, slot, start, size):
        return ref[:, :, slot, :, start : start + size].reshape(tokens, size)

    size = HD if share % HD == 0 else share
    outs = []
    for start in range(0, share, size):
        at = pl.ds(start, size)
        key_part, value_part = [ref[at, :] for ref in before] if final else (0.0, 0.0)
        for slot in range(slots):
            left = rows(normed, slot, start, size)
            key_part += dot_ta(left, rows(flat, slot, 0, features))
            value_part += dot_ta(left, rows(flat, slot, features, features))
            value_part += dot_ta(rows(grads, slot, start, size), rows(mixed, slot, 0, features))
        if final:
            totals[0, at, :] = key_part
            totals[1, at, :] = value_part
            for n, out in enumerate((key_out, value_out)):
                outs.append(
                    pltpu.make_async_copy(totals.at[n, at], out.at[at], out_sems.at[len(outs)])
                )
                outs[-1].start()
        else:
            key_out[at, :] = key_part
            value_out[at, :] = value_part
    for copy in outs:
        copy.wait()


def in_vmem(shape, dtype):
    return pltpu.VMEM(shape, dtype)


def shards(x0, w_key, w_value, w_score, segments, lengths, grades):
    sections = lax.axis_size("section")
    peers = lax.axis_size("dp")
    chips = peers // 2
    micro, width, model = x0.shape
    wk, wv = w_key[0], w_value[0]
    features = wk.shape[1]
    share = model // peers
    wide = -(-share // HD) * HD
    last = 2 * (sections - 1)
    ticks = micro + last
    rows = KV_HEADS * width

    tables = [
        in_vmem((1, model), F32),
        in_vmem(wk.shape, BF16),
        in_vmem(wv.shape, BF16),
        in_vmem((micro, width, HD), F32),
        in_vmem((micro, width, HD), F32),
        in_vmem((micro, rows, width), F32),
        in_vmem((micro, width, HD), F32),
        in_vmem((micro, width, HD), F32),
    ]
    state = [
        in_vmem((micro, width, model), BF16),
        in_vmem((micro, width, features), BF16),
        in_vmem((micro, width, features), BF16),
        in_vmem((micro, rows, width), F32),
        in_vmem((micro, width, HD), F32),
        in_vmem((micro, width, model), BF16),
    ]
    token = in_vmem((8, HD), F32)
    send_forward = pltpu.HBM((micro, width, 2 * wide + features), BF16)
    groups = [tuple(range(micro - 2)), (micro - 2,), (micro - 1,)]
    send_backward = [
        pltpu.HBM((len(group), width, 2 * wide + 2 * features), BF16) for group in groups
    ]
    row = jax.ShapeDtypeStruct((width, model), BF16)
    forward_scratch = [
        pltpu.VMEM((width, features), F32),
        pltpu.VMEM((width, features), F32),
        pltpu.VMEM((width, model), BF16),
        pltpu.VMEM((width, features), BF16),
        pltpu.VMEM((chips, width, 2 * wide + features), BF16),
        pltpu.SemaphoreType.DMA((chips,)),
    ]
    inputs = [wk, wv, x0, w_score.reshape(1, model), segments, lengths.reshape(1, micro), grades]
    chunks = model // CHUNK
    sends = [send_forward] * chips + [shape for shape in send_backward for _ in range(chips)]
    made = pl.pallas_call(
        functools.partial(first_kernel, sections, micro, chips),
        out_shape=tables + state + sends + [token, row],
        in_specs=[HBM] * len(inputs),
        out_specs=[VMEM] * (len(tables) + len(state)) + [HBM] * len(sends) + [VMEM, VMEM],
        scratch_shapes=[
            pltpu.VMEM(segments.shape, jnp.int32),
            pltpu.SMEM((1, micro), jnp.int32),
            pltpu.VMEM(grades.shape, jnp.int32),
            pltpu.SemaphoreType.DMA((6,)),
            pltpu.SemaphoreType.DMA((PIECES * chunks,)),
            pltpu.SemaphoreType.DMA((PIECES * chunks,)),
        ]
        + forward_scratch,
        compiler_params=params(),
        name="first",
    )(*[pltpu.with_memory_space_constraint(value, pltpu.HBM) for value in inputs])
    w_score, wk, wv, cosine, sine, mask, ends, target = made[: len(tables)]
    held = list(made[len(tables) : len(tables) + len(state) + chips])
    blocks = list(made[len(tables) + len(state) + chips : -2])
    blocks = [blocks[n : n + chips] for n in range(0, len(blocks), chips)]
    token_value, produced = made[-2:]

    def senders(tick, rank):
        return [s for s in range(sections) if rank(s) < sections - 1 and 0 <= tick - 2 * rank(s) < micro]

    def up(section):
        return section

    def down(section):
        return sections - 1 - section

    cost = pl.CostEstimate(flops=1000000, bytes_accessed=1000000, transcendentals=0)
    empty = jnp.zeros((width, model), BF16)
    incoming = [empty, empty, shifted(produced, 1, senders(0, up))]
    for tick in range(1, ticks):
        args = (incoming[tick], w_score, wk, wv, cosine, sine, mask, ends, target)
        count = len(held)
        *held, produced = pl.pallas_call(
            functools.partial(forward_kernel, tick, sections, micro, chips),
            out_shape=state + [send_forward] * chips + [row],
            in_specs=[VMEM] * (len(args) + len(state)) + [HBM] * chips,
            out_specs=[VMEM] * len(state) + [HBM] * chips + [VMEM],
            input_output_aliases={len(args) + n: n for n in range(count)},
            scratch_shapes=forward_scratch,
            compiler_params=params(),
            cost_estimate=cost,
            name="forward",
        )(*args, *held)
        if tick < ticks - 2:
            incoming.append(shifted(produced, 1, senders(tick, up)))

    saved, keys, values, probs, scales, grads, *sent = held
    incoming = [empty] * 2
    masks = sorted(range(1, chips), key=lambda m: (-bin(m).count("1"), m))
    per_tick = -(-len(masks) // 3)
    gathered = [None] * len(groups)
    for tick in range(ticks):
        for m in masks[(tick - 1) * per_tick : tick * per_tick] if tick else ():
            sent[m], token_value = lax.optimization_barrier((sent[m], token_value))
            sent[m] = between_chips(sent[m], m, chips)
        possible = [tick - 2 * hop for hop in range(sections)]
        filled = [n for n, group in enumerate(groups) if set(group) & set(possible)]
        args = (
            incoming[tick], wk, wv, cosine, sine, saved, keys, values, probs, scales, grads,
            token_value,
        )
        targets = [block for n in filled for block in blocks[n]]
        shapes = [send_backward[n] for n in filled for _ in range(chips)]
        token_value, *outs = pl.pallas_call(
            functools.partial(
                backward_kernel, tick, sections, micro, chips, [groups[n] for n in filled]
            ),
            out_shape=[token] + shapes + [row],
            in_specs=[VMEM] * len(args) + [HBM] * len(targets),
            out_specs=[VMEM] + [HBM] * len(targets) + [VMEM],
            input_output_aliases={len(args) - 1 + n: n for n in range(1 + len(targets))},
            scratch_shapes=[
                pltpu.VMEM((width, features), F32),
                pltpu.VMEM((width, model), F32),
                pltpu.VMEM((width, model), BF16),
                pltpu.VMEM((width, 2 * features), BF16),
                pltpu.VMEM((chips, width, 2 * wide + 2 * features), BF16),
                pltpu.SemaphoreType.DMA((chips,)),
            ],
            compiler_params=params(),
            cost_estimate=cost,
            name="backward",
        )(*args, *targets)
        for position, n in enumerate(filled):
            blocks[n] = outs[position * chips : (position + 1) * chips]
        if tick < ticks - 2:
            incoming.append(shifted(outs[-1], -1, senders(tick, down)))

        def both_cores(parts, token_value):
            parts, token_value = lax.optimization_barrier((parts, token_value))
            stacked = jnp.stack(parts)
            return [stacked, between_cores(stacked, chips)], token_value

        for n, group in enumerate(groups):
            if tick == last + group[-1]:
                for m in masks:
                    blocks[n][m] = between_chips(blocks[n][m], m, chips)
        if tick == last + groups[0][-1]:
            forward_blocks, token_value = both_cores(sent, token_value)
        for n, group in enumerate(groups[:-1]):
            if tick == last + group[-1] + 1:
                gathered[n], token_value = both_cores(blocks[n], token_value)
    gathered[-1], token_value = both_cores(blocks[-1], token_value)

    whole = jax.ShapeDtypeStruct((share, features), F32)
    total = ()
    for final, chosen in ((False, groups[:-1]), (True, groups[-1:])):
        args = [*forward_blocks, *[value for group in chosen for value in gathered[groups.index(group)]]]
        slots = sum(len(group) for group in chosen)
        at = (2, chips, slots, width)
        rows_out = share // HD if share % HD == 0 else 1
        total = pl.pallas_call(
            functools.partial(gather_kernel, chosen, share, wide, features, final),
            out_shape=[whole, whole],
            in_specs=[HBM] * len(args) + [VMEM] * len(total),
            out_specs=[HBM if final else VMEM] * 2,
            scratch_shapes=[
                pltpu.VMEM(at + (wide,), BF16),
                pltpu.VMEM(at + (features,), BF16),
                pltpu.VMEM(at + (wide,), BF16),
                pltpu.VMEM(at + (2 * features,), BF16),
                pltpu.VMEM((2, share if final else 8, features), F32),
                pltpu.SemaphoreType.DMA((2 * len(args),)),
                pltpu.SemaphoreType.DMA((2 * rows_out,)),
            ],
            compiler_params=params(24),
            cost_estimate=cost,
            name="gathered",
        )(*args, *total)
    return (total[0][None], total[1][None])


def solution(mesh):
    placed = (
        P(None, "dp", None),
        P("section", None, None),
        P("section", None, None),
        P(),
        P(None, "dp"),
        P(None, "dp"),
        P(None, "dp"),
    )
    return jax.shard_map(
        shards,
        mesh=mesh,
        in_specs=placed,
        out_specs=(P("section", "dp", None), P("section", "dp", None)),
        check_vma=False,
    )
```

```python
import functools

import jax
import jax.numpy as jnp
from jax import lax
from jax.experimental import pallas as pl
from jax.experimental.pallas import tpu as pltpu
from jax.sharding import PartitionSpec as P

HD = 128
KV_HEADS = 4
EPS = 1e-06
THETA = 1000000.0
NEG = -1e30
CHUNK = 1280
BF16 = jnp.bfloat16
F32 = jnp.float32

VMEM = pl.BlockSpec(memory_space=pltpu.VMEM)
HBM = pl.BlockSpec(memory_space=pl.ANY)


def params(mib=12):
    return pltpu.CompilerParams(vmem_limit_bytes=mib * 1024 * 1024)


def shifted(value, steps, senders):
    return lax.ppermute(value, "section", [(source, source + steps) for source in senders])


def between_chips(value, mask, chips):
    pairs = [(2 * c + k, 2 * partner(c, mask, chips) + k) for c in range(chips) for k in range(2)]
    return lax.ppermute(value, "dp", pairs)


def between_cores(value, chips):
    return lax.ppermute(value, "dp", [(d, d ^ 1) for d in range(2 * chips)])


def partner(chip, mask, chips):
    return chip ^ mask if chips & (chips - 1) == 0 else (mask - chip) % chips


def dot(left, right):
    return jnp.dot(left, right, preferred_element_type=F32)


def dot_tb(left, right):
    return lax.dot_general(left, right, (((1,), (1,)), ((), ())), preferred_element_type=F32)


def dot_ta(left, right):
    return lax.dot_general(left, right, (((0,), (0,)), ((), ())), preferred_element_type=F32)


def to_column(row, eye):
    return jnp.sum(jnp.where(eye, jnp.broadcast_to(row, eye.shape), 0.0), axis=1, keepdims=True)


def make_tables(
    micro, segments_ref, lengths_ref, grades_ref,
    cos_ref, sin_ref, mask_ref, ends_ref, target_ref,
):
    width = segments_ref.shape[1]
    square = (width, width)
    at_row = lax.broadcasted_iota(jnp.int32, square, 0)
    at_col = lax.broadcasted_iota(jnp.int32, square, 1)
    eye = at_row == at_col
    lane = lax.broadcasted_iota(jnp.int32, (width, HD), 1)
    half_lane = jnp.where(lane < HD // 2, lane, lane - HD // 2).astype(F32)
    freqs = jnp.exp(half_lane * F32(-2.0 / HD) * jnp.log(F32(THETA)))
    sign = jnp.where(lane < HD // 2, -1.0, 1.0)
    index = lax.broadcasted_iota(jnp.int32, (width, 1), 0)
    for slot in range(micro):
        seg_row = segments_ref[slot : slot + 1, :].astype(F32)
        seg_col = to_column(seg_row, eye)
        grade_col = to_column(grades_ref[slot : slot + 1, :].astype(F32), eye)
        length = lengths_ref[0, slot]
        same = seg_col == seg_row
        offset = jnp.sum(jnp.where(same & (at_col < at_row), 1.0, 0.0), axis=1, keepdims=True)
        angles = offset * freqs
        cos_ref[slot] = jnp.cos(angles)
        sin_ref[slot] = jnp.sin(angles) * sign
        allowed = same & (at_col <= at_row) & (at_row < length) & (at_col < length)
        mask = jnp.where(allowed | eye, 1.0, 0.0)
        for head in range(KV_HEADS):
            mask_ref[slot, head * width : (head + 1) * width, :] = mask
        changes = jnp.sum(
            jnp.where((at_col == at_row + 1) & jnp.logical_not(same), 1.0, 0.0),
            axis=1, keepdims=True,
        )
        following = (changes > 0.0) | (index == width - 1)
        ends = (index < length) & (following | (index == length - 1))
        logits = jnp.where(ends, grade_col, NEG)
        weight = jnp.exp(logits - jnp.max(logits, axis=0, keepdims=True))
        target = weight / jnp.sum(weight, axis=0, keepdims=True)
        ends_ref[slot] = jnp.broadcast_to(jnp.where(ends, 1.0, 0.0), (width, HD))
        target_ref[slot] = jnp.broadcast_to(target, (width, HD))


def first_kernel(
    sections, micro, chips,
    wk_hbm, wv_hbm, x0_hbm, score_hbm, segments_hbm, lengths_hbm, grades_hbm,
    w_score, wk, wv, cosine, sine, mask, ends, target,
    saved, keys, values, probs, scales, grads, *rest,
):
    sent = rest[:chips]
    outgoing = rest[-13]
    segments_ref, lengths_ref, grades_ref, small, key_sems, value_sems = rest[-12:-6]
    scratch = rest[-6:]
    model = wk.shape[0]
    copies = [
        pltpu.make_async_copy(segments_hbm, segments_ref, small.at[0]),
        pltpu.make_async_copy(lengths_hbm, lengths_ref, small.at[1]),
        pltpu.make_async_copy(grades_hbm, grades_ref, small.at[2]),
        pltpu.make_async_copy(x0_hbm, saved, small.at[3]),
        pltpu.make_async_copy(score_hbm, w_score, small.at[4]),
    ]
    for copy in copies:
        copy.start()

    def chunk_copies(c):
        cols = pl.ds(c * CHUNK, CHUNK)
        return (
            pltpu.make_async_copy(wk_hbm.at[cols], wk.at[cols], key_sems.at[c]),
            pltpu.make_async_copy(wv_hbm.at[cols], wv.at[cols], value_sems.at[c]),
        )

    for c in range(model // CHUNK):
        for copy in chunk_copies(c):
            copy.start()
    for copy in copies[:3]:
        copy.wait()
    make_tables(
        micro, segments_ref, lengths_ref, grades_ref, cosine, sine, mask, ends, target
    )
    for copy in copies[3:]:
        copy.wait()
    section = lax.axis_index("section")

    @pl.when(section == 0)
    def _():
        def wait_chunk(c):
            for copy in chunk_copies(c):
                copy.wait()

        forward_body(
            0, 0, section, sections, chips, wait_chunk,
            w_score, wk, wv, cosine, sine, mask, ends, target,
            saved, keys, values, probs, scales, grads, *sent, outgoing, *scratch,
        )

    @pl.when(section != 0)
    def _():
        for c in range(model // CHUNK):
            for copy in chunk_copies(c):
                copy.wait()


def row_scale(ref_value_chunks, model):
    total = None
    for chunk in ref_value_chunks:
        part = chunk * chunk
        total = part if total is None else total + part
    return lax.rsqrt(jnp.sum(total, axis=1, keepdims=True) / model + EPS)


def when(possible, condition):
    return pl.when(condition) if possible else lambda body: None


def head_cols(head):
    return slice(head * HD, (head + 1) * HD)


def forward_kernel(
    tick, sections, micro, chips,
    incoming, w_score, wk, wv, cosine, sine, mask, ends, target,
    *rest,
):
    section = lax.axis_index("section")
    offset = tick - 2 * section
    slot = jnp.clip(offset, 0, micro - 1)
    rest = rest[6 + chips :]
    saved = rest[0]

    @pl.when((offset >= 0) & (offset < micro))
    def _():
        @pl.when(section != 0)
        def _():
            saved[slot] = incoming[...]

        forward_body(
            tick, slot, section, sections, chips, None,
            w_score, wk, wv, cosine, sine, mask, ends, target, *rest,
        )


def fill_block(block, columns, factors):
    chips = block.shape[0]
    share = columns.shape[1] // (2 * chips)
    wide = (block.shape[2] - factors.shape[1]) // 2
    for device in range(2 * chips):
        start = (device % 2) * wide
        block[device // 2, :, start : start + share] = columns[:, device * share : (device + 1) * share]
    for chip in range(chips):
        block[chip, :, 2 * wide :] = factors[...]


def block_copies(block, targets, sems):
    chips = len(targets)
    chip = lax.axis_index("dp") // 2
    return [
        pltpu.make_async_copy(block.at[partner(chip, mask, chips)], target, sems.at[mask])
        for mask, target in enumerate(targets)
    ]


def forward_body(
    tick, slot, section, sections, chips, wait_chunk,
    w_score, wk, wv, cosine, sine, mask, ends, target,
    saved, keys, values, probs, scales, grads, *rest,
):
    sent, outgoing = rest[:chips], rest[chips]
    acc_k, acc_v, normed, mixed, block, sems = rest[chips + 1 :]
    width, model = outgoing.shape
    features = KV_HEADS * HD
    step = CHUNK // 2

    def chunk_of(ref, start):
        return ref[slot, :, start : start + step].astype(F32)

    scale = row_scale([chunk_of(saved, c) for c in range(0, model, step)], model)
    scales[slot] = jnp.broadcast_to(scale, (width, HD))
    for c in range(0, model, step):
        normed[:, c : c + step] = (chunk_of(saved, c) * scale).astype(BF16)
    acc_k[...] = jnp.zeros_like(acc_k)
    acc_v[...] = jnp.zeros_like(acc_v)

    @pl.loop(0, model // CHUNK)
    def _(c):
        if wait_chunk is not None:
            wait_chunk(c)
        cols = pl.ds(pl.multiple_of(c * CHUNK, CHUNK), CHUNK)
        piece = normed[:, cols]
        acc_k[...] += dot(piece, wk[cols, :])
        acc_v[...] += dot(piece, wv[cols, :])

    cos_value = cosine[slot]
    sin_value = sine[slot]
    scores = []
    for head in range(KV_HEADS):
        vec = acc_k[:, head_cols(head)]
        turned = vec * cos_value + pltpu.roll(vec, HD // 2, 1) * sin_value
        key = turned.astype(BF16)
        keys[slot, :, head_cols(head)] = key
        scores.append(dot_tb(key, key))
    values[slot] = acc_v[...].astype(BF16)
    score = jnp.concatenate(scores, axis=0) / HD
    score = jnp.where(mask[slot] > 0.0, score, NEG)
    weight = jnp.exp(score - jnp.max(score, axis=1, keepdims=True))
    prob = weight / jnp.sum(weight, axis=1, keepdims=True)
    probs[slot] = prob
    prob_b = prob.astype(BF16)
    for head in range(KV_HEADS):
        out = dot(prob_b[head * width : (head + 1) * width, :], values[slot, :, head_cols(head)])
        mixed[:, head_cols(head)] = out.astype(BF16)

    fill_block(block, normed, mixed)
    copies = block_copies(block, [ref.at[slot] for ref in sent], sems)
    for copy in copies:
        copy.start()

    @pl.loop(0, model // CHUNK)
    def _(c):
        cols = pl.ds(pl.multiple_of(c * CHUNK, CHUNK), CHUNK)
        out = saved[slot, :, cols].astype(F32) + dot_tb(mixed[...], wv[cols, :])
        outgoing[:, cols] = out.astype(BF16)

    @when(tick >= 2 * (sections - 1), section == sections - 1)
    def _():
        def last_of(start):
            return outgoing[:, start : start + step].astype(F32)

        last_scale = row_scale([last_of(c) for c in range(0, model, step)], model)
        along = None
        for c in range(0, model, step):
            part = last_of(c) * w_score[:, c : c + step]
            along = part if along is None else along + part
        along = jnp.sum(along, axis=1, keepdims=True)
        is_end = ends[slot][:, :1] > 0.0
        logits = jnp.where(is_end, last_scale * along, NEG)
        part = jnp.exp(logits - jnp.max(logits, axis=0, keepdims=True))
        chosen = part / jnp.sum(part, axis=0, keepdims=True)
        g = jnp.where(is_end, chosen - target[slot][:, :1], 0.0)
        first = last_scale * g
        second = last_scale * last_scale * last_scale * (g * along / model)
        for c in range(0, model, step):
            value = first * w_score[:, c : c + step] - last_of(c) * second
            grads[slot, :, c : c + step] = value.astype(BF16)

    for copy in copies:
        copy.wait()


def backward_kernel(
    tick, sections, micro, chips, groups,
    incoming, wk, wv, cosine, sine, saved, keys, values, probs, scales, grads,
    *rest,
):
    count = len(groups) * chips
    sent = rest[count + 2 : 2 * count + 2]
    outgoing = rest[2 * count + 2]
    acc, full, current, flat, block, sems = rest[2 * count + 3 :]
    section = lax.axis_index("section")
    offset = tick - 2 * (sections - 1 - section)
    slot = jnp.clip(offset, 0, micro - 1)
    width, model = incoming.shape
    features = KV_HEADS * HD
    step = CHUNK // 2

    def for_group(act):
        for n, group in enumerate(groups):
            @pl.when((slot >= group[0]) & (slot <= group[-1]))
            def _():
                index = jnp.clip(slot - group[0], 0, len(group) - 1)
                targets = [ref.at[index] for ref in sent[n * chips : (n + 1) * chips]]
                for copy in block_copies(block, targets, sems):
                    act(copy)

    @pl.when((offset >= 0) & (offset < micro))
    def _():
        @when(tick < micro, section == sections - 1)
        def _():
            current[...] = grads[slot]

        @when(tick >= 2, section != sections - 1)
        def _():
            current[...] = incoming[...]

        acc[...] = jnp.zeros_like(acc)

        @pl.loop(0, model // CHUNK)
        def _(c):
            cols = pl.ds(pl.multiple_of(c * CHUNK, CHUNK), CHUNK)
            acc[...] += dot(current[:, cols], wv[cols, :])

        def factors(value_pass):
            cos_value = cosine[slot]
            sin_value = sine[slot]
            prob = probs[slot]
            prob_b = prob.astype(BF16)
            grad_probs = []
            for head in range(KV_HEADS):
                rows = slice(head * width, (head + 1) * width)
                mixed_grad = acc[:, head_cols(head)].astype(BF16)
                grad_probs.append(dot_tb(mixed_grad, values[slot, :, head_cols(head)]))
                flat[:, features + head * HD : features + (head + 1) * HD] = dot_ta(
                    prob_b[rows, :], mixed_grad
                ).astype(BF16)
            if value_pass:
                for c in range(0, model, CHUNK):
                    full[:, c : c + CHUNK] = dot_tb(flat[:, features:], wv[c : c + CHUNK, :])
            grad_prob = jnp.concatenate(grad_probs, axis=0)
            grad_score = prob * (grad_prob - jnp.sum(prob * grad_prob, axis=1, keepdims=True))
            grad_score = grad_score.astype(BF16)
            for head in range(KV_HEADS):
                piece = grad_score[head * width : (head + 1) * width, :]
                key = keys[slot, :, head_cols(head)]
                vec = (dot(piece, key) + dot_ta(piece, key)) / HD
                turned = vec * cos_value - pltpu.roll(vec, HD // 2, 1) * sin_value
                flat[:, head_cols(head)] = turned.astype(BF16)
            fill_block(block, current, flat)

        lowest = tick - 2 * (sections - 1)

        @when(lowest >= 0, section == 0)
        def _():
            factors(False)
            for_group(lambda copy: copy.start())

        @when(lowest + 2 < micro, section != 0)
        def _():
            factors(True)
            for_group(lambda copy: copy.start())
            acc[...] = jnp.zeros_like(acc)

            @pl.loop(0, model // CHUNK)
            def _(c):
                cols = pl.ds(pl.multiple_of(c * CHUNK, CHUNK), CHUNK)
                out = full[:, cols] + dot_tb(flat[:, :features], wk[cols, :])
                full[:, cols] = out
                along = out * saved[slot, :, cols].astype(F32)
                total = along[:, :HD]
                for start in range(HD, CHUNK, HD):
                    total = total + along[:, start : start + HD]
                acc[:, :HD] += total

            scale = scales[slot][:, :1]
            mean = jnp.sum(acc[:, :HD], axis=1, keepdims=True) / model
            second = scale * scale * scale * mean
            for c in range(0, model, step):
                cols = slice(c, c + step)
                value = (
                    current[:, cols].astype(F32)
                    + scale * full[:, cols]
                    - saved[slot, :, cols].astype(F32) * second
                )
                outgoing[:, cols] = value.astype(BF16)

        for_group(lambda copy: copy.wait())


def gather_kernel(groups, share, wide, features, final, *rest):
    count = 2 + 2 * len(groups)
    forward, backward = rest[:2], rest[2:count]
    before = rest[count : count + 2] if final else ()
    key_out, value_out = rest[count + len(before) : count + len(before) + 2]
    normed, mixed, grads, flat, totals, sems, out_sems = rest[count + len(before) + 2 :]
    mine = pl.multiple_of(lax.axis_index("dp") % 2 * wide, HD)
    first = groups[0][0]
    slots = normed.shape[2]
    pairs = []
    for half, ref in enumerate(forward):
        at = ref.at[:, pl.ds(first, slots)]
        pairs.append((at.at[:, :, :, pl.ds(mine, wide)], normed.at[half]))
        pairs.append((at.at[:, :, :, pl.ds(2 * wide, features)], mixed.at[half]))
    for n, ref in enumerate(backward):
        group = groups[n // 2]
        inside = pl.ds(group[0] - first, len(group))
        pairs.append((ref.at[:, :, :, pl.ds(mine, wide)], grads.at[n % 2, :, inside]))
        pairs.append((ref.at[:, :, :, pl.ds(2 * wide, 2 * features)], flat.at[n % 2, :, inside]))
    copies = [pltpu.make_async_copy(*pair, sems.at[n]) for n, pair in enumerate(pairs)]
    for copy in copies:
        copy.start()
    for copy in copies:
        copy.wait()
    tokens = normed.shape[0] * normed.shape[1] * normed.shape[3]

    def rows(ref, slot, start, size):
        return ref[:, :, slot, :, start : start + size].reshape(tokens, size)

    size = HD if share % HD == 0 else share
    outs = []
    for start in range(0, share, size):
        at = pl.ds(start, size)
        key_part, value_part = [ref[at, :] for ref in before] if final else (0.0, 0.0)
        for slot in range(slots):
            left = rows(normed, slot, start, size)
            key_part += dot_ta(left, rows(flat, slot, 0, features))
            value_part += dot_ta(left, rows(flat, slot, features, features))
            value_part += dot_ta(rows(grads, slot, start, size), rows(mixed, slot, 0, features))
        if final:
            totals[0, at, :] = key_part
            totals[1, at, :] = value_part
            for n, out in enumerate((key_out, value_out)):
                outs.append(
                    pltpu.make_async_copy(totals.at[n, at], out.at[at], out_sems.at[len(outs)])
                )
                outs[-1].start()
        else:
            key_out[at, :] = key_part
            value_out[at, :] = value_part
    for copy in outs:
        copy.wait()


def in_vmem(shape, dtype):
    return pltpu.VMEM(shape, dtype)


def shards(x0, w_key, w_value, w_score, segments, lengths, grades):
    sections = lax.axis_size("section")
    peers = lax.axis_size("dp")
    chips = peers // 2
    micro, width, model = x0.shape
    wk, wv = w_key[0], w_value[0]
    features = wk.shape[1]
    share = model // peers
    wide = -(-share // HD) * HD
    last = 2 * (sections - 1)
    ticks = micro + last
    rows = KV_HEADS * width

    tables = [
        in_vmem((1, model), F32),
        in_vmem(wk.shape, BF16),
        in_vmem(wv.shape, BF16),
        in_vmem((micro, width, HD), F32),
        in_vmem((micro, width, HD), F32),
        in_vmem((micro, rows, width), F32),
        in_vmem((micro, width, HD), F32),
        in_vmem((micro, width, HD), F32),
    ]
    state = [
        in_vmem((micro, width, model), BF16),
        in_vmem((micro, width, features), BF16),
        in_vmem((micro, width, features), BF16),
        in_vmem((micro, rows, width), F32),
        in_vmem((micro, width, HD), F32),
        in_vmem((micro, width, model), BF16),
    ]
    token = in_vmem((8, HD), F32)
    send_forward = pltpu.HBM((micro, width, 2 * wide + features), BF16)
    groups = [tuple(range(micro - 2)), (micro - 2,), (micro - 1,)]
    send_backward = [
        pltpu.HBM((len(group), width, 2 * wide + 2 * features), BF16) for group in groups
    ]
    row = jax.ShapeDtypeStruct((width, model), BF16)
    forward_scratch = [
        pltpu.VMEM((width, features), F32),
        pltpu.VMEM((width, features), F32),
        pltpu.VMEM((width, model), BF16),
        pltpu.VMEM((width, features), BF16),
        pltpu.VMEM((chips, width, 2 * wide + features), BF16),
        pltpu.SemaphoreType.DMA((chips,)),
    ]
    inputs = [wk, wv, x0, w_score.reshape(1, model), segments, lengths.reshape(1, micro), grades]
    chunks = model // CHUNK
    sends = [send_forward] * chips + [shape for shape in send_backward for _ in range(chips)]
    made = pl.pallas_call(
        functools.partial(first_kernel, sections, micro, chips),
        out_shape=tables + state + sends + [token, row],
        in_specs=[HBM] * len(inputs),
        out_specs=[VMEM] * (len(tables) + len(state)) + [HBM] * len(sends) + [VMEM, VMEM],
        scratch_shapes=[
            pltpu.VMEM(segments.shape, jnp.int32),
            pltpu.SMEM((1, micro), jnp.int32),
            pltpu.VMEM(grades.shape, jnp.int32),
            pltpu.SemaphoreType.DMA((5,)),
            pltpu.SemaphoreType.DMA((chunks,)),
            pltpu.SemaphoreType.DMA((chunks,)),
        ]
        + forward_scratch,
        compiler_params=params(),
        name="first",
    )(*[pltpu.with_memory_space_constraint(value, pltpu.HBM) for value in inputs])
    w_score, wk, wv, cosine, sine, mask, ends, target = made[: len(tables)]
    held = list(made[len(tables) : len(tables) + len(state) + chips])
    blocks = list(made[len(tables) + len(state) + chips : -2])
    blocks = [blocks[n : n + chips] for n in range(0, len(blocks), chips)]
    token_value, produced = made[-2:]

    def senders(tick, rank):
        return [s for s in range(sections) if rank(s) < sections - 1 and 0 <= tick - 2 * rank(s) < micro]

    def up(section):
        return section

    def down(section):
        return sections - 1 - section

    cost = pl.CostEstimate(flops=1000000, bytes_accessed=1000000, transcendentals=0)
    empty = jnp.zeros((width, model), BF16)
    incoming = [empty, empty, shifted(produced, 1, senders(0, up))]
    for tick in range(1, ticks):
        args = (incoming[tick], w_score, wk, wv, cosine, sine, mask, ends, target)
        count = len(held)
        *held, produced = pl.pallas_call(
            functools.partial(forward_kernel, tick, sections, micro, chips),
            out_shape=state + [send_forward] * chips + [row],
            in_specs=[VMEM] * (len(args) + len(state)) + [HBM] * chips,
            out_specs=[VMEM] * len(state) + [HBM] * chips + [VMEM],
            input_output_aliases={len(args) + n: n for n in range(count)},
            scratch_shapes=forward_scratch,
            compiler_params=params(),
            cost_estimate=cost,
            name="forward",
        )(*args, *held)
        if tick < ticks - 2:
            incoming.append(shifted(produced, 1, senders(tick, up)))

    saved, keys, values, probs, scales, grads, *sent = held
    incoming = [empty] * 2
    masks = sorted(range(1, chips), key=lambda m: (-bin(m).count("1"), m))
    per_tick = -(-len(masks) // 3)
    gathered = [None] * len(groups)
    for tick in range(ticks):
        for m in masks[(tick - 1) * per_tick : tick * per_tick] if tick else ():
            sent[m], token_value = lax.optimization_barrier((sent[m], token_value))
            sent[m] = between_chips(sent[m], m, chips)
        possible = [tick - 2 * hop for hop in range(sections)]
        filled = [n for n, group in enumerate(groups) if set(group) & set(possible)]
        args = (
            incoming[tick], wk, wv, cosine, sine, saved, keys, values, probs, scales, grads,
            token_value,
        )
        targets = [block for n in filled for block in blocks[n]]
        shapes = [send_backward[n] for n in filled for _ in range(chips)]
        token_value, *outs = pl.pallas_call(
            functools.partial(
                backward_kernel, tick, sections, micro, chips, [groups[n] for n in filled]
            ),
            out_shape=[token] + shapes + [row],
            in_specs=[VMEM] * len(args) + [HBM] * len(targets),
            out_specs=[VMEM] + [HBM] * len(targets) + [VMEM],
            input_output_aliases={len(args) - 1 + n: n for n in range(1 + len(targets))},
            scratch_shapes=[
                pltpu.VMEM((width, features), F32),
                pltpu.VMEM((width, model), F32),
                pltpu.VMEM((width, model), BF16),
                pltpu.VMEM((width, 2 * features), BF16),
                pltpu.VMEM((chips, width, 2 * wide + 2 * features), BF16),
                pltpu.SemaphoreType.DMA((chips,)),
            ],
            compiler_params=params(),
            cost_estimate=cost,
            name="backward",
        )(*args, *targets)
        for position, n in enumerate(filled):
            blocks[n] = outs[position * chips : (position + 1) * chips]
        if tick < ticks - 2:
            incoming.append(shifted(outs[-1], -1, senders(tick, down)))

        def both_cores(parts, token_value):
            parts, token_value = lax.optimization_barrier((parts, token_value))
            stacked = jnp.stack(parts)
            return [stacked, between_cores(stacked, chips)], token_value

        for n, group in enumerate(groups):
            if tick == last + group[-1]:
                for m in masks:
                    blocks[n][m] = between_chips(blocks[n][m], m, chips)
        if tick == last + groups[0][-1]:
            forward_blocks, token_value = both_cores(sent, token_value)
        for n, group in enumerate(groups[:-1]):
            if tick == last + group[-1] + 1:
                gathered[n], token_value = both_cores(blocks[n], token_value)
    gathered[-1], token_value = both_cores(blocks[-1], token_value)

    whole = jax.ShapeDtypeStruct((share, features), F32)
    total = ()
    for final, chosen in ((False, groups[:1]), (True, groups[1:])):
        args = [*forward_blocks, *[value for group in chosen for value in gathered[groups.index(group)]]]
        slots = sum(len(group) for group in chosen)
        at = (2, chips, slots, width)
        rows_out = share // HD if share % HD == 0 else 1
        total = pl.pallas_call(
            functools.partial(gather_kernel, chosen, share, wide, features, final),
            out_shape=[whole, whole],
            in_specs=[HBM] * len(args) + [VMEM] * len(total),
            out_specs=[HBM if final else VMEM] * 2,
            scratch_shapes=[
                pltpu.VMEM(at + (wide,), BF16),
                pltpu.VMEM(at + (features,), BF16),
                pltpu.VMEM(at + (wide,), BF16),
                pltpu.VMEM(at + (2 * features,), BF16),
                pltpu.VMEM((2, share if final else 8, features), F32),
                pltpu.SemaphoreType.DMA((2 * len(args),)),
                pltpu.SemaphoreType.DMA((2 * rows_out,)),
            ],
            compiler_params=params(24),
            cost_estimate=cost,
            name="gathered",
        )(*args, *total)
    return (total[0][None], total[1][None])


def solution(mesh):
    placed = (
        P(None, "dp", None),
        P("section", None, None),
        P("section", None, None),
        P(),
        P(None, "dp"),
        P(None, "dp"),
        P(None, "dp"),
    )
    return jax.shard_map(
        shards,
        mesh=mesh,
        in_specs=placed,
        out_specs=(P("section", "dp", None), P("section", "dp", None)),
        check_vma=False,
    )
```

```python
import functools

import jax
import jax.numpy as jnp
from jax import lax
from jax.experimental import pallas as pl
from jax.experimental.pallas import tpu as pltpu
from jax.sharding import PartitionSpec as P

HD = 128
KV_HEADS = 4
EPS = 1e-06
THETA = 1000000.0
NEG = -1e30
CHUNK = 1280
BF16 = jnp.bfloat16
F32 = jnp.float32

VMEM = pl.BlockSpec(memory_space=pltpu.VMEM)
HBM = pl.BlockSpec(memory_space=pl.ANY)


def params(mib=12):
    return pltpu.CompilerParams(vmem_limit_bytes=mib * 1024 * 1024)


def shifted(value, steps, senders):
    return lax.ppermute(value, "section", [(source, source + steps) for source in senders])


def between_chips(value, mask, chips):
    pairs = [(2 * c + k, 2 * partner(c, mask, chips) + k) for c in range(chips) for k in range(2)]
    return lax.ppermute(value, "dp", pairs)


def between_cores(value, chips):
    return lax.ppermute(value, "dp", [(d, d ^ 1) for d in range(2 * chips)])


def partner(chip, mask, chips):
    return chip ^ mask if chips & (chips - 1) == 0 else (mask - chip) % chips


def dot(left, right):
    return jnp.dot(left, right, preferred_element_type=F32)


def dot_tb(left, right):
    return lax.dot_general(left, right, (((1,), (1,)), ((), ())), preferred_element_type=F32)


def dot_ta(left, right):
    return lax.dot_general(left, right, (((0,), (0,)), ((), ())), preferred_element_type=F32)


def to_column(row, eye):
    return jnp.sum(jnp.where(eye, jnp.broadcast_to(row, eye.shape), 0.0), axis=1, keepdims=True)


def make_tables(
    micro, segments_ref, lengths_ref, grades_ref,
    cos_ref, sin_ref, mask_ref, ends_ref, target_ref,
):
    width = segments_ref.shape[1]
    square = (width, width)
    at_row = lax.broadcasted_iota(jnp.int32, square, 0)
    at_col = lax.broadcasted_iota(jnp.int32, square, 1)
    eye = at_row == at_col
    lane = lax.broadcasted_iota(jnp.int32, (width, HD), 1)
    half_lane = jnp.where(lane < HD // 2, lane, lane - HD // 2).astype(F32)
    freqs = jnp.exp(half_lane * F32(-2.0 / HD) * jnp.log(F32(THETA)))
    sign = jnp.where(lane < HD // 2, -1.0, 1.0)
    index = lax.broadcasted_iota(jnp.int32, (width, 1), 0)
    for slot in range(micro):
        seg_row = segments_ref[slot : slot + 1, :].astype(F32)
        seg_col = to_column(seg_row, eye)
        grade_col = to_column(grades_ref[slot : slot + 1, :].astype(F32), eye)
        length = lengths_ref[0, slot]
        same = seg_col == seg_row
        offset = jnp.sum(jnp.where(same & (at_col < at_row), 1.0, 0.0), axis=1, keepdims=True)
        angles = offset * freqs
        cos_ref[slot] = jnp.cos(angles)
        sin_ref[slot] = jnp.sin(angles) * sign
        allowed = same & (at_col <= at_row) & (at_row < length) & (at_col < length)
        mask = jnp.where(allowed | eye, 1.0, 0.0)
        for head in range(KV_HEADS):
            mask_ref[slot, head * width : (head + 1) * width, :] = mask
        changes = jnp.sum(
            jnp.where((at_col == at_row + 1) & jnp.logical_not(same), 1.0, 0.0),
            axis=1, keepdims=True,
        )
        following = (changes > 0.0) | (index == width - 1)
        ends = (index < length) & (following | (index == length - 1))
        logits = jnp.where(ends, grade_col, NEG)
        weight = jnp.exp(logits - jnp.max(logits, axis=0, keepdims=True))
        target = weight / jnp.sum(weight, axis=0, keepdims=True)
        ends_ref[slot] = jnp.broadcast_to(jnp.where(ends, 1.0, 0.0), (width, HD))
        target_ref[slot] = jnp.broadcast_to(target, (width, HD))


def first_kernel(
    sections, micro, chips,
    wk_hbm, wv_hbm, x0_hbm, score_hbm, segments_hbm, lengths_hbm, grades_hbm,
    w_score, wk, wv, cosine, sine, mask, ends, target,
    saved, keys, values, probs, scales, grads, *rest,
):
    sent = rest[:chips]
    outgoing = rest[-13]
    segments_ref, lengths_ref, grades_ref, small, key_sems, value_sems = rest[-12:-6]
    scratch = rest[-6:]
    model = wk.shape[0]
    copies = [
        pltpu.make_async_copy(segments_hbm, segments_ref, small.at[0]),
        pltpu.make_async_copy(lengths_hbm, lengths_ref, small.at[1]),
        pltpu.make_async_copy(grades_hbm, grades_ref, small.at[2]),
        pltpu.make_async_copy(x0_hbm, saved, small.at[3]),
        pltpu.make_async_copy(score_hbm, w_score, small.at[4]),
    ]
    for copy in copies:
        copy.start()

    def chunk_copies(c):
        cols = pl.ds(c * CHUNK, CHUNK)
        return (
            pltpu.make_async_copy(wk_hbm.at[cols], wk.at[cols], key_sems.at[c]),
            pltpu.make_async_copy(wv_hbm.at[cols], wv.at[cols], value_sems.at[c]),
        )

    for c in range(model // CHUNK):
        for copy in chunk_copies(c):
            copy.start()
    for copy in copies[:3]:
        copy.wait()
    make_tables(
        micro, segments_ref, lengths_ref, grades_ref, cosine, sine, mask, ends, target
    )
    for copy in copies[3:]:
        copy.wait()
    section = lax.axis_index("section")

    @pl.when(section == 0)
    def _():
        def wait_chunk(c):
            for copy in chunk_copies(c):
                copy.wait()

        forward_body(
            0, 0, section, sections, chips, wait_chunk,
            w_score, wk, wv, cosine, sine, mask, ends, target,
            saved, keys, values, probs, scales, grads, *sent, outgoing, *scratch,
        )

    @pl.when(section != 0)
    def _():
        for c in range(model // CHUNK):
            for copy in chunk_copies(c):
                copy.wait()


def row_scale(ref_value_chunks, model):
    total = None
    for chunk in ref_value_chunks:
        part = chunk * chunk
        total = part if total is None else total + part
    return lax.rsqrt(jnp.sum(total, axis=1, keepdims=True) / model + EPS)


def when(possible, condition):
    return pl.when(condition) if possible else lambda body: None


def head_cols(head):
    return slice(head * HD, (head + 1) * HD)


def forward_kernel(
    tick, sections, micro, chips,
    incoming, w_score, wk, wv, cosine, sine, mask, ends, target,
    *rest,
):
    section = lax.axis_index("section")
    offset = tick - 2 * section
    slot = jnp.clip(offset, 0, micro - 1)
    rest = rest[6 + chips :]
    saved = rest[0]

    @pl.when((offset >= 0) & (offset < micro))
    def _():
        @pl.when(section != 0)
        def _():
            saved[slot] = incoming[...]

        forward_body(
            tick, slot, section, sections, chips, None,
            w_score, wk, wv, cosine, sine, mask, ends, target, *rest,
        )


def fill_block(block, columns, factors):
    chips = block.shape[0]
    share = columns.shape[1] // (2 * chips)
    wide = (block.shape[2] - factors.shape[1]) // 2
    for device in range(2 * chips):
        start = (device % 2) * wide
        block[device // 2, :, start : start + share] = columns[:, device * share : (device + 1) * share]
    for chip in range(chips):
        block[chip, :, 2 * wide :] = factors[...]


def block_copies(block, targets, sems):
    chips = len(targets)
    chip = lax.axis_index("dp") // 2
    return [
        pltpu.make_async_copy(block.at[partner(chip, mask, chips)], target, sems.at[mask])
        for mask, target in enumerate(targets)
    ]


def forward_body(
    tick, slot, section, sections, chips, wait_chunk,
    w_score, wk, wv, cosine, sine, mask, ends, target,
    saved, keys, values, probs, scales, grads, *rest,
):
    sent, outgoing = rest[:chips], rest[chips]
    acc_k, acc_v, normed, mixed, block, sems = rest[chips + 1 :]
    width, model = outgoing.shape
    features = KV_HEADS * HD
    step = CHUNK // 2

    def chunk_of(ref, start):
        return ref[slot, :, start : start + step].astype(F32)

    scale = row_scale([chunk_of(saved, c) for c in range(0, model, step)], model)
    scales[slot] = jnp.broadcast_to(scale, (width, HD))
    for c in range(0, model, step):
        normed[:, c : c + step] = (chunk_of(saved, c) * scale).astype(BF16)
    acc_k[...] = jnp.zeros_like(acc_k)
    acc_v[...] = jnp.zeros_like(acc_v)

    @pl.loop(0, model // CHUNK)
    def _(c):
        if wait_chunk is not None:
            wait_chunk(c)
        cols = pl.ds(pl.multiple_of(c * CHUNK, CHUNK), CHUNK)
        piece = normed[:, cols]
        acc_k[...] += dot(piece, wk[cols, :])
        acc_v[...] += dot(piece, wv[cols, :])

    cos_value = cosine[slot]
    sin_value = sine[slot]
    scores = []
    for head in range(KV_HEADS):
        vec = acc_k[:, head_cols(head)]
        turned = vec * cos_value + pltpu.roll(vec, HD // 2, 1) * sin_value
        key = turned.astype(BF16)
        keys[slot, :, head_cols(head)] = key
        scores.append(dot_tb(key, key))
    values[slot] = acc_v[...].astype(BF16)
    score = jnp.concatenate(scores, axis=0) / HD
    score = jnp.where(mask[slot] > 0.0, score, NEG)
    weight = jnp.exp(score - jnp.max(score, axis=1, keepdims=True))
    prob = weight / jnp.sum(weight, axis=1, keepdims=True)
    probs[slot] = prob
    prob_b = prob.astype(BF16)
    for head in range(KV_HEADS):
        out = dot(prob_b[head * width : (head + 1) * width, :], values[slot, :, head_cols(head)])
        mixed[:, head_cols(head)] = out.astype(BF16)

    fill_block(block, normed, mixed)
    copies = block_copies(block, [ref.at[slot] for ref in sent], sems)
    for copy in copies:
        copy.start()

    @pl.loop(0, model // CHUNK)
    def _(c):
        cols = pl.ds(pl.multiple_of(c * CHUNK, CHUNK), CHUNK)
        out = saved[slot, :, cols].astype(F32) + dot_tb(mixed[...], wv[cols, :])
        outgoing[:, cols] = out.astype(BF16)

    @when(tick >= 2 * (sections - 1), section == sections - 1)
    def _():
        def last_of(start):
            return outgoing[:, start : start + step].astype(F32)

        last_scale = row_scale([last_of(c) for c in range(0, model, step)], model)
        along = None
        for c in range(0, model, step):
            part = last_of(c) * w_score[:, c : c + step]
            along = part if along is None else along + part
        along = jnp.sum(along, axis=1, keepdims=True)
        is_end = ends[slot][:, :1] > 0.0
        logits = jnp.where(is_end, last_scale * along, NEG)
        part = jnp.exp(logits - jnp.max(logits, axis=0, keepdims=True))
        chosen = part / jnp.sum(part, axis=0, keepdims=True)
        g = jnp.where(is_end, chosen - target[slot][:, :1], 0.0)
        first = last_scale * g
        second = last_scale * last_scale * last_scale * (g * along / model)
        for c in range(0, model, step):
            value = first * w_score[:, c : c + step] - last_of(c) * second
            grads[slot, :, c : c + step] = value.astype(BF16)

    for copy in copies:
        copy.wait()


def backward_kernel(
    tick, sections, micro, chips, groups,
    incoming, wk, wv, cosine, sine, saved, keys, values, probs, scales, grads,
    *rest,
):
    count = len(groups) * chips
    sent = rest[count + 2 : 2 * count + 2]
    outgoing = rest[2 * count + 2]
    acc, full, current, flat, block, sems = rest[2 * count + 3 :]
    section = lax.axis_index("section")
    offset = tick - 2 * (sections - 1 - section)
    slot = jnp.clip(offset, 0, micro - 1)
    width, model = incoming.shape
    features = KV_HEADS * HD
    step = CHUNK // 2

    def for_group(act):
        for n, group in enumerate(groups):
            @pl.when((slot >= group[0]) & (slot <= group[-1]))
            def _():
                index = jnp.clip(slot - group[0], 0, len(group) - 1)
                targets = [ref.at[index] for ref in sent[n * chips : (n + 1) * chips]]
                for copy in block_copies(block, targets, sems):
                    act(copy)

    @pl.when((offset >= 0) & (offset < micro))
    def _():
        @when(tick < micro, section == sections - 1)
        def _():
            current[...] = grads[slot]

        @when(tick >= 2, section != sections - 1)
        def _():
            current[...] = incoming[...]

        acc[...] = jnp.zeros_like(acc)

        @pl.loop(0, model // CHUNK)
        def _(c):
            cols = pl.ds(pl.multiple_of(c * CHUNK, CHUNK), CHUNK)
            acc[...] += dot(current[:, cols], wv[cols, :])

        def factors(value_pass):
            cos_value = cosine[slot]
            sin_value = sine[slot]
            prob = probs[slot]
            prob_b = prob.astype(BF16)
            grad_probs = []
            for head in range(KV_HEADS):
                rows = slice(head * width, (head + 1) * width)
                mixed_grad = acc[:, head_cols(head)].astype(BF16)
                grad_probs.append(dot_tb(mixed_grad, values[slot, :, head_cols(head)]))
                flat[:, features + head * HD : features + (head + 1) * HD] = dot_ta(
                    prob_b[rows, :], mixed_grad
                ).astype(BF16)
            if value_pass:
                for c in range(0, model, CHUNK):
                    full[:, c : c + CHUNK] = dot_tb(flat[:, features:], wv[c : c + CHUNK, :])
            grad_prob = jnp.concatenate(grad_probs, axis=0)
            grad_score = prob * (grad_prob - jnp.sum(prob * grad_prob, axis=1, keepdims=True))
            grad_score = grad_score.astype(BF16)
            for head in range(KV_HEADS):
                piece = grad_score[head * width : (head + 1) * width, :]
                key = keys[slot, :, head_cols(head)]
                vec = (dot(piece, key) + dot_ta(piece, key)) / HD
                turned = vec * cos_value - pltpu.roll(vec, HD // 2, 1) * sin_value
                flat[:, head_cols(head)] = turned.astype(BF16)
            fill_block(block, current, flat)

        lowest = tick - 2 * (sections - 1)

        @when(lowest >= 0, section == 0)
        def _():
            factors(False)
            for_group(lambda copy: copy.start())

        @when(lowest + 2 < micro, section != 0)
        def _():
            factors(True)
            for_group(lambda copy: copy.start())
            acc[...] = jnp.zeros_like(acc)

            @pl.loop(0, model // CHUNK)
            def _(c):
                cols = pl.ds(pl.multiple_of(c * CHUNK, CHUNK), CHUNK)
                out = full[:, cols] + dot_tb(flat[:, :features], wk[cols, :])
                full[:, cols] = out
                along = out * saved[slot, :, cols].astype(F32)
                total = along[:, :HD]
                for start in range(HD, CHUNK, HD):
                    total = total + along[:, start : start + HD]
                acc[:, :HD] += total

            scale = scales[slot][:, :1]
            mean = jnp.sum(acc[:, :HD], axis=1, keepdims=True) / model
            second = scale * scale * scale * mean
            for c in range(0, model, step):
                cols = slice(c, c + step)
                value = (
                    current[:, cols].astype(F32)
                    + scale * full[:, cols]
                    - saved[slot, :, cols].astype(F32) * second
                )
                outgoing[:, cols] = value.astype(BF16)

        for_group(lambda copy: copy.wait())


def gather_kernel(groups, share, wide, features, final, *rest):
    count = 2 + 2 * len(groups)
    forward, backward = rest[:2], rest[2:count]
    before = rest[count : count + 2] if final else ()
    key_out, value_out = rest[count + len(before) : count + len(before) + 2]
    normed, mixed, grads, flat, totals, sems, out_sems = rest[count + len(before) + 2 :]
    mine = pl.multiple_of(lax.axis_index("dp") % 2 * wide, HD)
    first = groups[0][0]
    slots = normed.shape[2]
    pairs = []
    for half, ref in enumerate(forward):
        at = ref.at[:, pl.ds(first, slots)]
        pairs.append((at.at[:, :, :, pl.ds(mine, wide)], normed.at[half]))
        pairs.append((at.at[:, :, :, pl.ds(2 * wide, features)], mixed.at[half]))
    for n, ref in enumerate(backward):
        group = groups[n // 2]
        inside = pl.ds(group[0] - first, len(group))
        pairs.append((ref.at[:, :, :, pl.ds(mine, wide)], grads.at[n % 2, :, inside]))
        pairs.append((ref.at[:, :, :, pl.ds(2 * wide, 2 * features)], flat.at[n % 2, :, inside]))
    copies = [pltpu.make_async_copy(*pair, sems.at[n]) for n, pair in enumerate(pairs)]
    for copy in copies:
        copy.start()
    for copy in copies:
        copy.wait()
    tokens = normed.shape[0] * normed.shape[1] * normed.shape[3]

    def rows(ref, slot, start, size):
        return ref[:, :, slot, :, start : start + size].reshape(tokens, size)

    size = HD if share % HD == 0 else share
    outs = []
    for start in range(0, share, size):
        at = pl.ds(start, size)
        key_part, value_part = [ref[at, :] for ref in before] if final else (0.0, 0.0)
        for slot in range(slots):
            left = rows(normed, slot, start, size)
            key_part += dot_ta(left, rows(flat, slot, 0, features))
            value_part += dot_ta(left, rows(flat, slot, features, features))
            value_part += dot_ta(rows(grads, slot, start, size), rows(mixed, slot, 0, features))
        if final:
            totals[0, at, :] = key_part
            totals[1, at, :] = value_part
            for n, out in enumerate((key_out, value_out)):
                outs.append(
                    pltpu.make_async_copy(totals.at[n, at], out.at[at], out_sems.at[len(outs)])
                )
                outs[-1].start()
        else:
            key_out[at, :] = key_part
            value_out[at, :] = value_part
    for copy in outs:
        copy.wait()


def in_vmem(shape, dtype):
    return pltpu.VMEM(shape, dtype)


def shards(x0, w_key, w_value, w_score, segments, lengths, grades):
    sections = lax.axis_size("section")
    peers = lax.axis_size("dp")
    chips = peers // 2
    micro, width, model = x0.shape
    wk, wv = w_key[0], w_value[0]
    features = wk.shape[1]
    share = model // peers
    wide = -(-share // HD) * HD
    last = 2 * (sections - 1)
    ticks = micro + last
    rows = KV_HEADS * width

    tables = [
        in_vmem((1, model), F32),
        in_vmem(wk.shape, BF16),
        in_vmem(wv.shape, BF16),
        in_vmem((micro, width, HD), F32),
        in_vmem((micro, width, HD), F32),
        in_vmem((micro, rows, width), F32),
        in_vmem((micro, width, HD), F32),
        in_vmem((micro, width, HD), F32),
    ]
    state = [
        in_vmem((micro, width, model), BF16),
        in_vmem((micro, width, features), BF16),
        in_vmem((micro, width, features), BF16),
        in_vmem((micro, rows, width), F32),
        in_vmem((micro, width, HD), F32),
        in_vmem((micro, width, model), BF16),
    ]
    token = in_vmem((8, HD), F32)
    send_forward = pltpu.HBM((micro, width, 2 * wide + features), BF16)
    groups = [tuple(range(micro - 2)), (micro - 2,), (micro - 1,)]
    send_backward = [
        pltpu.HBM((len(group), width, 2 * wide + 2 * features), BF16) for group in groups
    ]
    row = jax.ShapeDtypeStruct((width, model), BF16)
    forward_scratch = [
        pltpu.VMEM((width, features), F32),
        pltpu.VMEM((width, features), F32),
        pltpu.VMEM((width, model), BF16),
        pltpu.VMEM((width, features), BF16),
        pltpu.VMEM((chips, width, 2 * wide + features), BF16),
        pltpu.SemaphoreType.DMA((chips,)),
    ]
    inputs = [wk, wv, x0, w_score.reshape(1, model), segments, lengths.reshape(1, micro), grades]
    chunks = model // CHUNK
    sends = [send_forward] * chips + [shape for shape in send_backward for _ in range(chips)]
    made = pl.pallas_call(
        functools.partial(first_kernel, sections, micro, chips),
        out_shape=tables + state + sends + [token, row],
        in_specs=[HBM] * len(inputs),
        out_specs=[VMEM] * (len(tables) + len(state)) + [HBM] * len(sends) + [VMEM, VMEM],
        scratch_shapes=[
            pltpu.VMEM(segments.shape, jnp.int32),
            pltpu.SMEM((1, micro), jnp.int32),
            pltpu.VMEM(grades.shape, jnp.int32),
            pltpu.SemaphoreType.DMA((5,)),
            pltpu.SemaphoreType.DMA((chunks,)),
            pltpu.SemaphoreType.DMA((chunks,)),
        ]
        + forward_scratch,
        compiler_params=params(),
        name="first",
    )(*[pltpu.with_memory_space_constraint(value, pltpu.HBM) for value in inputs])
    w_score, wk, wv, cosine, sine, mask, ends, target = made[: len(tables)]
    held = list(made[len(tables) : len(tables) + len(state) + chips])
    blocks = list(made[len(tables) + len(state) + chips : -2])
    blocks = [blocks[n : n + chips] for n in range(0, len(blocks), chips)]
    token_value, produced = made[-2:]

    def senders(tick, rank):
        return [s for s in range(sections) if rank(s) < sections - 1 and 0 <= tick - 2 * rank(s) < micro]

    def up(section):
        return section

    def down(section):
        return sections - 1 - section

    cost = pl.CostEstimate(flops=1000000, bytes_accessed=1000000, transcendentals=0)
    empty = jnp.zeros((width, model), BF16)
    incoming = [empty, empty, shifted(produced, 1, senders(0, up))]
    for tick in range(1, ticks):
        args = (incoming[tick], w_score, wk, wv, cosine, sine, mask, ends, target)
        count = len(held)
        sends = tick < ticks - 2
        outs = pl.pallas_call(
            functools.partial(forward_kernel, tick, sections, micro, chips),
            out_shape=state + [send_forward] * chips + [row] * sends,
            in_specs=[VMEM] * (len(args) + len(state)) + [HBM] * chips,
            out_specs=[VMEM] * len(state) + [HBM] * chips + [VMEM] * sends,
            input_output_aliases={len(args) + n: n for n in range(count)},
            scratch_shapes=[pltpu.VMEM(row.shape, row.dtype)] * (not sends) + forward_scratch,
            compiler_params=params(),
            cost_estimate=cost,
            name="forward",
        )(*args, *held)
        held = list(outs[:count])
        if sends:
            incoming.append(shifted(outs[-1], 1, senders(tick, up)))

    saved, keys, values, probs, scales, grads, *sent = held
    incoming = [empty] * 2
    masks = sorted(range(1, chips), key=lambda m: (-bin(m).count("1"), m))
    per_tick = -(-len(masks) // 3)
    gathered = [None] * len(groups)
    for tick in range(ticks):
        for m in masks[(tick - 1) * per_tick : tick * per_tick] if tick else ():
            sent[m], token_value = lax.optimization_barrier((sent[m], token_value))
            sent[m] = between_chips(sent[m], m, chips)
        possible = [tick - 2 * hop for hop in range(sections)]
        filled = [n for n, group in enumerate(groups) if set(group) & set(possible)]
        args = (
            incoming[tick], wk, wv, cosine, sine, saved, keys, values, probs, scales, grads,
            token_value,
        )
        targets = [block for n in filled for block in blocks[n]]
        shapes = [send_backward[n] for n in filled for _ in range(chips)]
        sends = tick < ticks - 2
        token_value, *outs = pl.pallas_call(
            functools.partial(
                backward_kernel, tick, sections, micro, chips, [groups[n] for n in filled]
            ),
            out_shape=[token] + shapes + [row] * sends,
            in_specs=[VMEM] * len(args) + [HBM] * len(targets),
            out_specs=[VMEM] + [HBM] * len(targets) + [VMEM] * sends,
            input_output_aliases={len(args) - 1 + n: n for n in range(1 + len(targets))},
            scratch_shapes=[pltpu.VMEM(row.shape, row.dtype)] * (not sends)
            + [
                pltpu.VMEM((width, features), F32),
                pltpu.VMEM((width, model), F32),
                pltpu.VMEM((width, model), BF16),
                pltpu.VMEM((width, 2 * features), BF16),
                pltpu.VMEM((chips, width, 2 * wide + 2 * features), BF16),
                pltpu.SemaphoreType.DMA((chips,)),
            ],
            compiler_params=params(),
            cost_estimate=cost,
            name="backward",
        )(*args, *targets)
        for position, n in enumerate(filled):
            blocks[n] = outs[position * chips : (position + 1) * chips]
        if sends:
            incoming.append(shifted(outs[-1], -1, senders(tick, down)))

        def both_cores(parts, token_value):
            parts, token_value = lax.optimization_barrier((parts, token_value))
            stacked = jnp.stack(parts)
            return [stacked, between_cores(stacked, chips)], token_value

        for n, group in enumerate(groups):
            if tick == last + group[-1]:
                for m in masks:
                    blocks[n][m] = between_chips(blocks[n][m], m, chips)
        if tick == last + groups[0][-1]:
            forward_blocks, token_value = both_cores(sent, token_value)
        for n, group in enumerate(groups[:-1]):
            if tick == last + group[-1] + 1:
                gathered[n], token_value = both_cores(blocks[n], token_value)
    gathered[-1], token_value = both_cores(blocks[-1], token_value)

    whole = jax.ShapeDtypeStruct((share, features), F32)
    total = ()
    for final, chosen in ((False, groups[:1]), (True, groups[1:])):
        args = [*forward_blocks, *[value for group in chosen for value in gathered[groups.index(group)]]]
        slots = sum(len(group) for group in chosen)
        at = (2, chips, slots, width)
        rows_out = share // HD if share % HD == 0 else 1
        total = pl.pallas_call(
            functools.partial(gather_kernel, chosen, share, wide, features, final),
            out_shape=[whole, whole],
            in_specs=[HBM] * len(args) + [VMEM] * len(total),
            out_specs=[HBM if final else VMEM] * 2,
            scratch_shapes=[
                pltpu.VMEM(at + (wide,), BF16),
                pltpu.VMEM(at + (features,), BF16),
                pltpu.VMEM(at + (wide,), BF16),
                pltpu.VMEM(at + (2 * features,), BF16),
                pltpu.VMEM((2, share if final else 8, features), F32),
                pltpu.SemaphoreType.DMA((2 * len(args),)),
                pltpu.SemaphoreType.DMA((2 * rows_out,)),
            ],
            compiler_params=params(24),
            cost_estimate=cost,
            name="gathered",
        )(*args, *total)
    return (total[0][None], total[1][None])


def solution(mesh):
    placed = (
        P(None, "dp", None),
        P("section", None, None),
        P("section", None, None),
        P(),
        P(None, "dp"),
        P(None, "dp"),
        P(None, "dp"),
    )
    return jax.shard_map(
        shards,
        mesh=mesh,
        in_specs=placed,
        out_specs=(P("section", "dp", None), P("section", "dp", None)),
        check_vma=False,
    )
```

```python
import functools

import jax
import jax.numpy as jnp
from jax import lax
from jax.experimental import pallas as pl
from jax.experimental.pallas import tpu as pltpu
from jax.sharding import PartitionSpec as P

HD = 128
KV_HEADS = 4
EPS = 1e-06
THETA = 1000000.0
NEG = -1e30
CHUNK = 1280
BF16 = jnp.bfloat16
F32 = jnp.float32

VMEM = pl.BlockSpec(memory_space=pltpu.VMEM)
HBM = pl.BlockSpec(memory_space=pl.ANY)


def params(mib=12):
    return pltpu.CompilerParams(vmem_limit_bytes=mib * 1024 * 1024)


def shifted(value, steps, senders):
    return lax.ppermute(value, "section", [(source, source + steps) for source in senders])


def between_chips(value, mask, chips):
    pairs = [(2 * c + k, 2 * partner(c, mask, chips) + k) for c in range(chips) for k in range(2)]
    return lax.ppermute(value, "dp", pairs)


def between_cores(value, chips):
    return lax.ppermute(value, "dp", [(d, d ^ 1) for d in range(2 * chips)])


def partner(chip, mask, chips):
    return chip ^ mask if chips & (chips - 1) == 0 else (mask - chip) % chips


def dot(left, right):
    return jnp.dot(left, right, preferred_element_type=F32)


def dot_tb(left, right):
    return lax.dot_general(left, right, (((1,), (1,)), ((), ())), preferred_element_type=F32)


def dot_ta(left, right):
    return lax.dot_general(left, right, (((0,), (0,)), ((), ())), preferred_element_type=F32)


def to_column(row, eye):
    return jnp.sum(jnp.where(eye, jnp.broadcast_to(row, eye.shape), 0.0), axis=1, keepdims=True)


def make_tables(
    micro, segments_ref, lengths_ref, grades_ref,
    cos_ref, sin_ref, mask_ref, ends_ref, target_ref,
):
    width = segments_ref.shape[1]
    square = (width, width)
    at_row = lax.broadcasted_iota(jnp.int32, square, 0)
    at_col = lax.broadcasted_iota(jnp.int32, square, 1)
    eye = at_row == at_col
    lane = lax.broadcasted_iota(jnp.int32, (width, HD), 1)
    half_lane = jnp.where(lane < HD // 2, lane, lane - HD // 2).astype(F32)
    freqs = jnp.exp(half_lane * F32(-2.0 / HD) * jnp.log(F32(THETA)))
    sign = jnp.where(lane < HD // 2, -1.0, 1.0)
    index = lax.broadcasted_iota(jnp.int32, (width, 1), 0)
    for slot in range(micro):
        seg_row = segments_ref[slot : slot + 1, :].astype(F32)
        seg_col = to_column(seg_row, eye)
        grade_col = to_column(grades_ref[slot : slot + 1, :].astype(F32), eye)
        length = lengths_ref[0, slot]
        same = seg_col == seg_row
        offset = jnp.sum(jnp.where(same & (at_col < at_row), 1.0, 0.0), axis=1, keepdims=True)
        angles = offset * freqs
        cos_ref[slot] = jnp.cos(angles)
        sin_ref[slot] = jnp.sin(angles) * sign
        allowed = same & (at_col <= at_row) & (at_row < length) & (at_col < length)
        mask = jnp.where(allowed | eye, 1.0, 0.0)
        for head in range(KV_HEADS):
            mask_ref[slot, head * width : (head + 1) * width, :] = mask
        changes = jnp.sum(
            jnp.where((at_col == at_row + 1) & jnp.logical_not(same), 1.0, 0.0),
            axis=1, keepdims=True,
        )
        following = (changes > 0.0) | (index == width - 1)
        ends = (index < length) & (following | (index == length - 1))
        logits = jnp.where(ends, grade_col, NEG)
        weight = jnp.exp(logits - jnp.max(logits, axis=0, keepdims=True))
        target = weight / jnp.sum(weight, axis=0, keepdims=True)
        ends_ref[slot] = jnp.broadcast_to(jnp.where(ends, 1.0, 0.0), (width, HD))
        target_ref[slot] = jnp.broadcast_to(target, (width, HD))


def first_kernel(
    sections, micro, chips,
    wk_hbm, wv_hbm, x0_hbm, score_hbm, segments_hbm, lengths_hbm, grades_hbm,
    w_score, wk, wv, cosine, sine, mask, ends, target,
    saved, keys, values, probs, scales, grads, *rest,
):
    sent = rest[:chips]
    outgoing = rest[-13]
    segments_ref, lengths_ref, grades_ref, small, key_sems, value_sems = rest[-12:-6]
    scratch = rest[-6:]
    model = wk.shape[0]
    copies = [
        pltpu.make_async_copy(segments_hbm, segments_ref, small.at[0]),
        pltpu.make_async_copy(lengths_hbm, lengths_ref, small.at[1]),
        pltpu.make_async_copy(grades_hbm, grades_ref, small.at[2]),
        pltpu.make_async_copy(x0_hbm, saved, small.at[3]),
        pltpu.make_async_copy(score_hbm, w_score, small.at[4]),
    ]
    for copy in copies:
        copy.start()

    def chunk_copies(c):
        cols = pl.ds(c * CHUNK, CHUNK)
        return (
            pltpu.make_async_copy(wk_hbm.at[cols], wk.at[cols], key_sems.at[c]),
            pltpu.make_async_copy(wv_hbm.at[cols], wv.at[cols], value_sems.at[c]),
        )

    for c in range(model // CHUNK):
        for copy in chunk_copies(c):
            copy.start()
    for copy in copies[:3]:
        copy.wait()
    make_tables(
        micro, segments_ref, lengths_ref, grades_ref, cosine, sine, mask, ends, target
    )
    for copy in copies[3:]:
        copy.wait()
    section = lax.axis_index("section")

    @pl.when(section == 0)
    def _():
        def wait_chunk(c):
            for copy in chunk_copies(c):
                copy.wait()

        forward_body(
            0, 0, section, sections, chips, wait_chunk,
            w_score, wk, wv, cosine, sine, mask, ends, target,
            saved, keys, values, probs, scales, grads, *sent, outgoing, *scratch,
        )

    @pl.when(section != 0)
    def _():
        for c in range(model // CHUNK):
            for copy in chunk_copies(c):
                copy.wait()


def row_scale(ref_value_chunks, model):
    total = None
    for chunk in ref_value_chunks:
        part = chunk * chunk
        total = part if total is None else total + part
    return lax.rsqrt(jnp.sum(total, axis=1, keepdims=True) / model + EPS)


def when(possible, condition):
    return pl.when(condition) if possible else lambda body: None


def head_cols(head):
    return slice(head * HD, (head + 1) * HD)


def forward_kernel(
    tick, sections, micro, chips,
    incoming, w_score, wk, wv, cosine, sine, mask, ends, target,
    *rest,
):
    section = lax.axis_index("section")
    offset = tick - 2 * section
    slot = jnp.clip(offset, 0, micro - 1)
    rest = rest[6 + chips :]
    saved = rest[0]

    @pl.when((offset >= 0) & (offset < micro))
    def _():
        @pl.when(section != 0)
        def _():
            saved[slot] = incoming[...]

        forward_body(
            tick, slot, section, sections, chips, None,
            w_score, wk, wv, cosine, sine, mask, ends, target, *rest,
        )


def fill_block(block, columns, factors):
    fill_columns(block, columns)
    for chip in range(block.shape[0]):
        block[chip, :, block.shape[2] - factors.shape[1] :] = factors[...]


def fill_columns(block, columns):
    chips = block.shape[0]
    share = columns.shape[1] // (2 * chips)
    wide = -(-share // HD) * HD
    for device in range(2 * chips):
        start = (device % 2) * wide
        block[device // 2, :, start : start + share] = columns[:, device * share : (device + 1) * share]


def block_copies(block, targets, sems):
    chips = len(targets)
    chip = lax.axis_index("dp") // 2
    return [
        pltpu.make_async_copy(block.at[partner(chip, mask, chips)], target, sems.at[mask])
        for mask, target in enumerate(targets)
    ]


def forward_body(
    tick, slot, section, sections, chips, wait_chunk,
    w_score, wk, wv, cosine, sine, mask, ends, target,
    saved, keys, values, probs, scales, grads, *rest,
):
    sent, outgoing = rest[:chips], rest[chips]
    acc_k, acc_v, normed, mixed, block, sems = rest[chips + 1 :]
    width, model = outgoing.shape
    features = KV_HEADS * HD
    step = CHUNK // 2

    def chunk_of(ref, start):
        return ref[slot, :, start : start + step].astype(F32)

    scale = row_scale([chunk_of(saved, c) for c in range(0, model, step)], model)
    scales[slot] = jnp.broadcast_to(scale, (width, HD))
    for c in range(0, model, step):
        normed[:, c : c + step] = (chunk_of(saved, c) * scale).astype(BF16)
    acc_k[...] = jnp.zeros_like(acc_k)
    acc_v[...] = jnp.zeros_like(acc_v)

    @pl.loop(0, model // CHUNK)
    def _(c):
        if wait_chunk is not None:
            wait_chunk(c)
        cols = pl.ds(pl.multiple_of(c * CHUNK, CHUNK), CHUNK)
        piece = normed[:, cols]
        acc_k[...] += dot(piece, wk[cols, :])
        acc_v[...] += dot(piece, wv[cols, :])

    cos_value = cosine[slot]
    sin_value = sine[slot]
    scores = []
    for head in range(KV_HEADS):
        vec = acc_k[:, head_cols(head)]
        turned = vec * cos_value + pltpu.roll(vec, HD // 2, 1) * sin_value
        key = turned.astype(BF16)
        keys[slot, :, head_cols(head)] = key
        scores.append(dot_tb(key, key))
    values[slot] = acc_v[...].astype(BF16)
    score = jnp.concatenate(scores, axis=0) / HD
    score = jnp.where(mask[slot] > 0.0, score, NEG)
    weight = jnp.exp(score - jnp.max(score, axis=1, keepdims=True))
    prob = weight / jnp.sum(weight, axis=1, keepdims=True)
    probs[slot] = prob
    prob_b = prob.astype(BF16)
    for head in range(KV_HEADS):
        out = dot(prob_b[head * width : (head + 1) * width, :], values[slot, :, head_cols(head)])
        mixed[:, head_cols(head)] = out.astype(BF16)

    fill_block(block, normed, mixed)
    copies = block_copies(block, [ref.at[slot] for ref in sent], sems)
    for copy in copies:
        copy.start()

    @pl.loop(0, model // CHUNK)
    def _(c):
        cols = pl.ds(pl.multiple_of(c * CHUNK, CHUNK), CHUNK)
        out = saved[slot, :, cols].astype(F32) + dot_tb(mixed[...], wv[cols, :])
        outgoing[:, cols] = out.astype(BF16)

    @when(tick >= 2 * (sections - 1), section == sections - 1)
    def _():
        def last_of(start):
            return outgoing[:, start : start + step].astype(F32)

        last_scale = row_scale([last_of(c) for c in range(0, model, step)], model)
        along = None
        for c in range(0, model, step):
            part = last_of(c) * w_score[:, c : c + step]
            along = part if along is None else along + part
        along = jnp.sum(along, axis=1, keepdims=True)
        is_end = ends[slot][:, :1] > 0.0
        logits = jnp.where(is_end, last_scale * along, NEG)
        part = jnp.exp(logits - jnp.max(logits, axis=0, keepdims=True))
        chosen = part / jnp.sum(part, axis=0, keepdims=True)
        g = jnp.where(is_end, chosen - target[slot][:, :1], 0.0)
        first = last_scale * g
        second = last_scale * last_scale * last_scale * (g * along / model)
        for c in range(0, model, step):
            value = first * w_score[:, c : c + step] - last_of(c) * second
            grads[slot, :, c : c + step] = value.astype(BF16)

    for copy in copies:
        copy.wait()


def backward_kernel(
    tick, sections, micro, chips, groups,
    incoming, wk, wv, cosine, sine, saved, keys, values, probs, scales, grads,
    *rest,
):
    count = len(groups) * chips
    sent = rest[count + 2 : 2 * count + 2]
    outgoing = rest[2 * count + 2]
    acc, full, current, flat, block, sems = rest[2 * count + 3 :]
    section = lax.axis_index("section")
    offset = tick - 2 * (sections - 1 - section)
    slot = jnp.clip(offset, 0, micro - 1)
    width, model = incoming.shape
    features = KV_HEADS * HD
    step = CHUNK // 2

    split = block.shape[2]
    chip = lax.axis_index("dp") // 2

    def for_group(act, columns):
        for n, group in enumerate(groups):
            @pl.when((slot >= group[0]) & (slot <= group[-1]))
            def _():
                index = jnp.clip(slot - group[0], 0, len(group) - 1)
                for mask, ref in enumerate(sent[n * chips : (n + 1) * chips]):
                    if columns:
                        source, part = block.at[partner(chip, mask, chips)], pl.ds(0, split)
                    else:
                        source, part = flat, pl.ds(split, 2 * features)
                    target = ref.at[index, :, part]
                    at = mask if columns else chips + mask
                    act(pltpu.make_async_copy(source, target, sems.at[at]))

    @pl.when((offset >= 0) & (offset < micro))
    def _():
        @when(tick < micro, section == sections - 1)
        def _():
            current[...] = grads[slot]

        @when(tick >= 2, section != sections - 1)
        def _():
            current[...] = incoming[...]

        fill_columns(block, current)
        for_group(lambda copy: copy.start(), True)
        acc[...] = jnp.zeros_like(acc)

        @pl.loop(0, model // CHUNK)
        def _(c):
            cols = pl.ds(pl.multiple_of(c * CHUNK, CHUNK), CHUNK)
            acc[...] += dot(current[:, cols], wv[cols, :])

        def factors(value_pass):
            cos_value = cosine[slot]
            sin_value = sine[slot]
            prob = probs[slot]
            prob_b = prob.astype(BF16)
            grad_probs = []
            for head in range(KV_HEADS):
                rows = slice(head * width, (head + 1) * width)
                mixed_grad = acc[:, head_cols(head)].astype(BF16)
                grad_probs.append(dot_tb(mixed_grad, values[slot, :, head_cols(head)]))
                flat[:, features + head * HD : features + (head + 1) * HD] = dot_ta(
                    prob_b[rows, :], mixed_grad
                ).astype(BF16)
            if value_pass:
                for c in range(0, model, CHUNK):
                    full[:, c : c + CHUNK] = dot_tb(flat[:, features:], wv[c : c + CHUNK, :])
            grad_prob = jnp.concatenate(grad_probs, axis=0)
            grad_score = prob * (grad_prob - jnp.sum(prob * grad_prob, axis=1, keepdims=True))
            grad_score = grad_score.astype(BF16)
            for head in range(KV_HEADS):
                piece = grad_score[head * width : (head + 1) * width, :]
                key = keys[slot, :, head_cols(head)]
                vec = (dot(piece, key) + dot_ta(piece, key)) / HD
                turned = vec * cos_value - pltpu.roll(vec, HD // 2, 1) * sin_value
                flat[:, head_cols(head)] = turned.astype(BF16)

        lowest = tick - 2 * (sections - 1)

        @when(lowest >= 0, section == 0)
        def _():
            factors(False)
            for_group(lambda copy: copy.start(), False)

        @when(lowest + 2 < micro, section != 0)
        def _():
            factors(True)
            for_group(lambda copy: copy.start(), False)
            acc[...] = jnp.zeros_like(acc)

            @pl.loop(0, model // CHUNK)
            def _(c):
                cols = pl.ds(pl.multiple_of(c * CHUNK, CHUNK), CHUNK)
                out = full[:, cols] + dot_tb(flat[:, :features], wk[cols, :])
                full[:, cols] = out
                along = out * saved[slot, :, cols].astype(F32)
                total = along[:, :HD]
                for start in range(HD, CHUNK, HD):
                    total = total + along[:, start : start + HD]
                acc[:, :HD] += total

            scale = scales[slot][:, :1]
            mean = jnp.sum(acc[:, :HD], axis=1, keepdims=True) / model
            second = scale * scale * scale * mean
            for c in range(0, model, step):
                cols = slice(c, c + step)
                value = (
                    current[:, cols].astype(F32)
                    + scale * full[:, cols]
                    - saved[slot, :, cols].astype(F32) * second
                )
                outgoing[:, cols] = value.astype(BF16)

        for_group(lambda copy: copy.wait(), True)
        for_group(lambda copy: copy.wait(), False)


def gather_kernel(groups, share, wide, features, final, *rest):
    count = 2 + 2 * len(groups)
    forward, backward = rest[:2], rest[2:count]
    before = rest[count : count + 2] if final else ()
    key_out, value_out = rest[count + len(before) : count + len(before) + 2]
    normed, mixed, grads, flat, totals, sems, out_sems = rest[count + len(before) + 2 :]
    mine = pl.multiple_of(lax.axis_index("dp") % 2 * wide, HD)
    first = groups[0][0]
    slots = normed.shape[2]
    pairs = []
    for half, ref in enumerate(forward):
        at = ref.at[:, pl.ds(first, slots)]
        pairs.append((at.at[:, :, :, pl.ds(mine, wide)], normed.at[half]))
        pairs.append((at.at[:, :, :, pl.ds(2 * wide, features)], mixed.at[half]))
    for n, ref in enumerate(backward):
        group = groups[n // 2]
        inside = pl.ds(group[0] - first, len(group))
        pairs.append((ref.at[:, :, :, pl.ds(mine, wide)], grads.at[n % 2, :, inside]))
        pairs.append((ref.at[:, :, :, pl.ds(2 * wide, 2 * features)], flat.at[n % 2, :, inside]))
    copies = [pltpu.make_async_copy(*pair, sems.at[n]) for n, pair in enumerate(pairs)]
    for copy in copies:
        copy.start()
    for copy in copies:
        copy.wait()
    tokens = normed.shape[0] * normed.shape[1] * normed.shape[3]

    def rows(ref, slot, start, size):
        return ref[:, :, slot, :, start : start + size].reshape(tokens, size)

    size = HD if share % HD == 0 else share
    outs = []
    for start in range(0, share, size):
        at = pl.ds(start, size)
        key_part, value_part = [ref[at, :] for ref in before] if final else (0.0, 0.0)
        for slot in range(slots):
            left = rows(normed, slot, start, size)
            key_part += dot_ta(left, rows(flat, slot, 0, features))
            value_part += dot_ta(left, rows(flat, slot, features, features))
            value_part += dot_ta(rows(grads, slot, start, size), rows(mixed, slot, 0, features))
        if final:
            totals[0, at, :] = key_part
            totals[1, at, :] = value_part
            for n, out in enumerate((key_out, value_out)):
                outs.append(
                    pltpu.make_async_copy(totals.at[n, at], out.at[at], out_sems.at[len(outs)])
                )
                outs[-1].start()
        else:
            key_out[at, :] = key_part
            value_out[at, :] = value_part
    for copy in outs:
        copy.wait()


def in_vmem(shape, dtype):
    return pltpu.VMEM(shape, dtype)


def shards(x0, w_key, w_value, w_score, segments, lengths, grades):
    sections = lax.axis_size("section")
    peers = lax.axis_size("dp")
    chips = peers // 2
    micro, width, model = x0.shape
    wk, wv = w_key[0], w_value[0]
    features = wk.shape[1]
    share = model // peers
    wide = -(-share // HD) * HD
    last = 2 * (sections - 1)
    ticks = micro + last
    rows = KV_HEADS * width

    tables = [
        in_vmem((1, model), F32),
        in_vmem(wk.shape, BF16),
        in_vmem(wv.shape, BF16),
        in_vmem((micro, width, HD), F32),
        in_vmem((micro, width, HD), F32),
        in_vmem((micro, rows, width), F32),
        in_vmem((micro, width, HD), F32),
        in_vmem((micro, width, HD), F32),
    ]
    state = [
        in_vmem((micro, width, model), BF16),
        in_vmem((micro, width, features), BF16),
        in_vmem((micro, width, features), BF16),
        in_vmem((micro, rows, width), F32),
        in_vmem((micro, width, HD), F32),
        in_vmem((micro, width, model), BF16),
    ]
    token = in_vmem((8, HD), F32)
    send_forward = pltpu.HBM((micro, width, 2 * wide + features), BF16)
    groups = [tuple(range(micro - 2)), (micro - 2,), (micro - 1,)]
    send_backward = [
        pltpu.HBM((len(group), width, 2 * wide + 2 * features), BF16) for group in groups
    ]
    row = jax.ShapeDtypeStruct((width, model), BF16)
    forward_scratch = [
        pltpu.VMEM((width, features), F32),
        pltpu.VMEM((width, features), F32),
        pltpu.VMEM((width, model), BF16),
        pltpu.VMEM((width, features), BF16),
        pltpu.VMEM((chips, width, 2 * wide + features), BF16),
        pltpu.SemaphoreType.DMA((chips,)),
    ]
    inputs = [wk, wv, x0, w_score.reshape(1, model), segments, lengths.reshape(1, micro), grades]
    chunks = model // CHUNK
    sends = [send_forward] * chips + [shape for shape in send_backward for _ in range(chips)]
    made = pl.pallas_call(
        functools.partial(first_kernel, sections, micro, chips),
        out_shape=tables + state + sends + [token, row],
        in_specs=[HBM] * len(inputs),
        out_specs=[VMEM] * (len(tables) + len(state)) + [HBM] * len(sends) + [VMEM, VMEM],
        scratch_shapes=[
            pltpu.VMEM(segments.shape, jnp.int32),
            pltpu.SMEM((1, micro), jnp.int32),
            pltpu.VMEM(grades.shape, jnp.int32),
            pltpu.SemaphoreType.DMA((5,)),
            pltpu.SemaphoreType.DMA((chunks,)),
            pltpu.SemaphoreType.DMA((chunks,)),
        ]
        + forward_scratch,
        compiler_params=params(),
        name="first",
    )(*[pltpu.with_memory_space_constraint(value, pltpu.HBM) for value in inputs])
    w_score, wk, wv, cosine, sine, mask, ends, target = made[: len(tables)]
    held = list(made[len(tables) : len(tables) + len(state) + chips])
    blocks = list(made[len(tables) + len(state) + chips : -2])
    blocks = [blocks[n : n + chips] for n in range(0, len(blocks), chips)]
    token_value, produced = made[-2:]

    def senders(tick, rank):
        return [s for s in range(sections) if rank(s) < sections - 1 and 0 <= tick - 2 * rank(s) < micro]

    def up(section):
        return section

    def down(section):
        return sections - 1 - section

    cost = pl.CostEstimate(flops=1000000, bytes_accessed=1000000, transcendentals=0)
    empty = jnp.zeros((width, model), BF16)
    incoming = [empty, empty, shifted(produced, 1, senders(0, up))]
    for tick in range(1, ticks):
        args = (incoming[tick], w_score, wk, wv, cosine, sine, mask, ends, target)
        count = len(held)
        sends = tick < ticks - 2
        outs = pl.pallas_call(
            functools.partial(forward_kernel, tick, sections, micro, chips),
            out_shape=state + [send_forward] * chips + [row] * sends,
            in_specs=[VMEM] * (len(args) + len(state)) + [HBM] * chips,
            out_specs=[VMEM] * len(state) + [HBM] * chips + [VMEM] * sends,
            input_output_aliases={len(args) + n: n for n in range(count)},
            scratch_shapes=[pltpu.VMEM(row.shape, row.dtype)] * (not sends) + forward_scratch,
            compiler_params=params(),
            cost_estimate=cost,
            name="forward",
        )(*args, *held)
        held = list(outs[:count])
        if sends:
            incoming.append(shifted(outs[-1], 1, senders(tick, up)))

    saved, keys, values, probs, scales, grads, *sent = held
    incoming = [empty] * 2
    masks = sorted(range(1, chips), key=lambda m: (-bin(m).count("1"), m))
    per_tick = -(-len(masks) // 3)
    gathered = [None] * len(groups)
    for tick in range(ticks):
        for m in masks[(tick - 1) * per_tick : tick * per_tick] if tick else ():
            sent[m], token_value = lax.optimization_barrier((sent[m], token_value))
            sent[m] = between_chips(sent[m], m, chips)
        possible = [tick - 2 * hop for hop in range(sections)]
        filled = [n for n, group in enumerate(groups) if set(group) & set(possible)]
        args = (
            incoming[tick], wk, wv, cosine, sine, saved, keys, values, probs, scales, grads,
            token_value,
        )
        targets = [block for n in filled for block in blocks[n]]
        shapes = [send_backward[n] for n in filled for _ in range(chips)]
        sends = tick < ticks - 2
        token_value, *outs = pl.pallas_call(
            functools.partial(
                backward_kernel, tick, sections, micro, chips, [groups[n] for n in filled]
            ),
            out_shape=[token] + shapes + [row] * sends,
            in_specs=[VMEM] * len(args) + [HBM] * len(targets),
            out_specs=[VMEM] + [HBM] * len(targets) + [VMEM] * sends,
            input_output_aliases={len(args) - 1 + n: n for n in range(1 + len(targets))},
            scratch_shapes=[pltpu.VMEM(row.shape, row.dtype)] * (not sends)
            + [
                pltpu.VMEM((width, features), F32),
                pltpu.VMEM((width, model), F32),
                pltpu.VMEM((width, model), BF16),
                pltpu.VMEM((width, 2 * features), BF16),
                pltpu.VMEM((chips, width, 2 * wide), BF16),
                pltpu.SemaphoreType.DMA((2 * chips,)),
            ],
            compiler_params=params(),
            cost_estimate=cost,
            name="backward",
        )(*args, *targets)
        for position, n in enumerate(filled):
            blocks[n] = outs[position * chips : (position + 1) * chips]
        if sends:
            incoming.append(shifted(outs[-1], -1, senders(tick, down)))

        def both_cores(parts, token_value):
            parts, token_value = lax.optimization_barrier((parts, token_value))
            stacked = jnp.stack(parts)
            return [stacked, between_cores(stacked, chips)], token_value

        for n, group in enumerate(groups):
            if tick == last + group[-1]:
                for m in masks:
                    blocks[n][m] = between_chips(blocks[n][m], m, chips)
        if tick == last + groups[0][-1]:
            forward_blocks, token_value = both_cores(sent, token_value)
        for n, group in enumerate(groups[:-1]):
            if tick == last + group[-1] + 1:
                gathered[n], token_value = both_cores(blocks[n], token_value)
    gathered[-1], token_value = both_cores(blocks[-1], token_value)

    whole = jax.ShapeDtypeStruct((share, features), F32)
    total = ()
    for final, chosen in ((False, groups[:1]), (True, groups[1:])):
        args = [*forward_blocks, *[value for group in chosen for value in gathered[groups.index(group)]]]
        slots = sum(len(group) for group in chosen)
        at = (2, chips, slots, width)
        rows_out = share // HD if share % HD == 0 else 1
        total = pl.pallas_call(
            functools.partial(gather_kernel, chosen, share, wide, features, final),
            out_shape=[whole, whole],
            in_specs=[HBM] * len(args) + [VMEM] * len(total),
            out_specs=[HBM if final else VMEM] * 2,
            scratch_shapes=[
                pltpu.VMEM(at + (wide,), BF16),
                pltpu.VMEM(at + (features,), BF16),
                pltpu.VMEM(at + (wide,), BF16),
                pltpu.VMEM(at + (2 * features,), BF16),
                pltpu.VMEM((2, share if final else 8, features), F32),
                pltpu.SemaphoreType.DMA((2 * len(args),)),
                pltpu.SemaphoreType.DMA((2 * rows_out,)),
            ],
            compiler_params=params(24),
            cost_estimate=cost,
            name="gathered",
        )(*args, *total)
    return (total[0][None], total[1][None])


def solution(mesh):
    placed = (
        P(None, "dp", None),
        P("section", None, None),
        P("section", None, None),
        P(),
        P(None, "dp"),
        P(None, "dp"),
        P(None, "dp"),
    )
    return jax.shard_map(
        shards,
        mesh=mesh,
        in_specs=placed,
        out_specs=(P("section", "dp", None), P("section", "dp", None)),
        check_vma=False,
    )
```
